32 devices in a mesh: cells: 8 (over z, y), tm: 4 (over x, core).
Axes of the slice: x: 2, y: 2, z: 4, core: 2. Of those that a mesh axis runs over, the one named last changes fastest.
Arguments:
- attitude: float32 [4, 8192], P(None, ('cells', 'tm')), may hold values from -6 to 6
- star_partials: float32 [5, 64, 16384], P(None, None, ('cells', 'tm')), may hold values from -6 to 6
- attitude_partials: float32 [4, 64, 16384], P(None, None, ('cells', 'tm')), may hold values from -6 to 6
- observed: float32 [64, 16384], P(None, ('cells', 'tm')), may hold values from -6 to 6
- phase: float32 [64, 16384], P(None, ('cells', 'tm')), may hold values from 0 to 1
- knot_offset: int32 [64, 16384], P(None, ('cells', 'tm')), may hold values from 0 to 12
- cell_counts: int32 [128], P(('cells', 'tm')), may hold values from 40 to 64, as said below
- interval_owner: int32 [128, 64, 1], P(('cells', 'tm')), may hold values from 0 to 31; in each aligned block of 256 rows (0 to 255, 256 to 511, ..., all dimensions but the last counted through in order) at most 12 rows name the same one
- block_slot: int32 [128, 64], P(('cells', 'tm')), may hold values from 0 to 15
Outputs:
- star_step: float32 [5, 16384], P(None, ('cells', 'tm'))
- attitude_step: float32 [4, 8192], P(None, ('cells', 'tm'))
The draws below stay inside these ranges and needn't reach their ends.
Inputs may be any that keep to these rules, and one draw needn't show every extreme that they name: `interval_owner`: among the 256 transits of the cells of one device no owner is named more than 12 times, and in every draw some owner is named exactly 12 times by the transits of some device. Transits that are not live are listed too. `cell_counts`: some cell has all 64 transits live in every draw.
All inputs are finite; a program needn't handle non-finite values.
Results may differ from the reference program's by a relative error of at most 0.0003.
Values sent between devices are 32-bit elements; how exact they have to be, the bound alone decides.
No kernel may reach another device: no remote copies, remote signals or barrier semaphores. Data moves between devices by JAX's collectives and lax.ppermute only.
A program may use at most 128 MiB of HBM per device.

```python
import math
import jax
import jax.numpy as jnp
import numpy as np
from jax import lax

NT = 64
CS = 128
KB = 16
ITERS = 6
BPD = 16
CELLS = 128
STARS = 16384
TR_DEV = 256
BLOCKS = 512
KNOTS = 8192
CAP = 12
N_CELLS = 8
N_TM = 4


def draw_cell_counts(key, part):
    first = jax.random.fold_in(key, 11)
    second = jax.random.fold_in(key, 12)
    counts = jax.random.randint(first, (CELLS,), NT * 5 // 8, NT + 1)
    chosen = jax.random.randint(second, (), 0, CELLS)
    return counts.at[chosen].set(NT).astype(jnp.int32)


def with_ends(array, own_key, low, top_value):
    extent = array.shape
    place = [jax.random.randint(jax.random.fold_in(own_key, axis), (), 0, extent[axis]) for axis in range(len(extent))]
    array = array.at[tuple(place)].set(low)
    longest = extent.index(max(extent))
    place[longest] = (place[longest] + 1) % extent[longest]
    return array.at[tuple(place)].set(top_value)


def block_levels(key, dims, cuts, smallest, high):
    loudness, own = 1.0, jax.random.fold_in(key, 6)
    for dim, parts in cuts:
        draws = jnp.exp(jax.random.uniform(jax.random.fold_in(own, dim), (parts,), jnp.float32, smallest / len(cuts), high / len(cuts)))
        loudness = loudness * jnp.repeat(draws, dims[dim] // parts).reshape([-1 if axis == dim else 1 for axis in range(len(dims))])
    return loudness


def routed_block(key, own, number, rows, number_of, top, most, lean):
    sequence = jax.random.permutation(key, number_of)
    crowded, ordinary = portions_of(number_of, rows * top, most, lean, True), portions_of(number_of, rows * top, most, lean, False)
    places = jnp.arange(number_of)

    def named(lengths, offset_by):
        used = int((lengths > 0).sum())
        fixed = max(1, used // 4)
        passed = fixed + (places - fixed + offset_by * (used - fixed)) % max(1, number_of - fixed)
        return jnp.zeros((number_of,), jnp.int32).at[sequence[jnp.where(places < fixed, places, passed)]].set(jnp.asarray(lengths, jnp.int32))

    lengths = jnp.where(number % 4 == 0, named(crowded, number // 4), named(ordinary, number - number // 4 - 1))
    mixed = jax.random.permutation(jax.random.fold_in(own, 3), number_of)
    donor, sink = mixed[0:number_of // 2 * 2:2], mixed[1:number_of // 2 * 2:2]
    room = jnp.minimum(lengths[donor] - 1, most - lengths[sink]) // 2
    room = jnp.where((donor == sequence[0]) | (sink == sequence[0]) | (lengths[sink] == 0), 0, jnp.maximum(room, 0))
    passed = jax.random.randint(jax.random.fold_in(own, 4), (number_of // 2,), 0, 1 << 20) % (room + 1)
    lengths = lengths.at[donor].add(-passed).at[sink].add(passed)
    labels = jnp.searchsorted(jnp.cumsum(lengths), jnp.arange(rows * top), side="right").astype(jnp.int32)
    table = labels.reshape(top, rows).T
    table = table[jax.random.permutation(jax.random.fold_in(own, 1), rows)]
    offset_by = jax.random.randint(jax.random.fold_in(own, 2), (rows, 1), 0, top)
    return jnp.take_along_axis(table, (jnp.arange(top)[None, :] + offset_by) % top, axis=1)


def portions_of(amount, total, bound, lean, full):
    weights = [(1 << 20) // math.isqrt(rank ** lean) + 1 for rank in range(1, amount + 1)]
    largest = bound if full else min(bound, max(-(-total // amount), total * weights[0] // sum(weights)))
    least = 1 if total - largest >= amount - 1 else 0
    given, spare = [largest] + [least] * (amount - 1), total - largest - least * (amount - 1)
    while spare > 0:
        free = [i for i in range(1, amount) if given[i] < largest] or [i for i in range(1, amount) if given[i] < bound]
        mass, budget = sum([weights[i] for i in free]), spare
        for i in free:
            addition = min(bound - given[i], max(1, budget * weights[i] // mass), spare)
            given[i] = given[i] + addition
            spare = spare - addition
    return np.array(given)


def bell_draw(own_key, dims, width, bound, cuts=(), held_as=jnp.bfloat16):
    values = width * jax.random.normal(own_key, dims, jnp.float32)
    if cuts:
        values = values * block_levels(own_key, dims, cuts, -0.22, 0.18)
    return jnp.clip(values, -bound, bound).astype(held_as)


def setup_inputs(seed: int = 0) -> dict:
    streams_of = jax.random.split(jax.random.key(seed), 10)
    attitude = bell_draw(streams_of[0], (4, KNOTS), 1.0, 6.0, ((1, 32),), jnp.float32)
    star_partials = bell_draw(streams_of[1], (5, NT, STARS), 1.0, 6.0, ((2, 32),), jnp.float32)
    attitude_partials = bell_draw(streams_of[2], (4, NT, STARS), 1.0, 6.0, ((2, 32),), jnp.float32)
    observed = bell_draw(streams_of[3], (NT, STARS), 1.0, 6.0, ((1, 32),), jnp.float32)
    phase = jnp.clip(1.0 * jax.random.uniform(streams_of[4], (NT, STARS), jnp.float32) ** block_levels(streams_of[4], (NT, STARS), ((1, 32),), -0.2, 0.2), 0.0, 1.0)
    knot_offset = with_ends(jax.random.randint(streams_of[5], (NT, STARS), 0, KB - 3), jax.random.fold_in(streams_of[5], 1), 0, (KB - 3) - 1).astype(jnp.int32)
    cell_counts = draw_cell_counts(jax.random.fold_in(streams_of[9], 71), 0)
    interval_owner_keys = jax.random.split(jax.random.fold_in(streams_of[7], 1), CELLS * NT // TR_DEV)
    interval_owner_turns = jax.random.permutation(jax.random.fold_in(streams_of[7], 3), CELLS * NT // TR_DEV)
    interval_owner = jax.vmap(lambda own, number: routed_block(jax.random.fold_in(streams_of[7], 2), own, number, TR_DEV, N_CELLS * N_TM, 1, CAP, 2))(interval_owner_keys, interval_owner_turns).reshape((CELLS, NT, 1))
    block_slot = with_ends(jax.random.randint(streams_of[8], (CELLS, NT), 0, BPD), jax.random.fold_in(streams_of[8], 1), 0, BPD - 1).astype(jnp.int32)
    return {"attitude": attitude, "star_partials": star_partials, "attitude_partials": attitude_partials, "observed": observed, "phase": phase, "knot_offset": knot_offset, "cell_counts": cell_counts, "interval_owner": interval_owner, "block_slot": block_slot}


smoothing = 16.0
damping = 2.0
relaxation = 0.5
star_prior = 1.0
highest = lax.Precision.HIGHEST

def spline_basis(phase):
    square = phase * phase
    cube = square * phase
    rest = 1.0 - phase
    return (rest * rest * rest / 6.0, (3.0 * cube - 6.0 * square + 4.0) / 6.0, (-3.0 * cube + 3.0 * square + 3.0 * phase + 1.0) / 6.0, cube / 6.0)

def design_rows(phase, knot_offset, partials, live):
    knots = lax.broadcasted_iota(jnp.int32, (KB, 1), 0)
    basis = spline_basis(phase)
    spread = jnp.zeros(phase.shape[:-1] + (KB, phase.shape[-1]), jnp.float32)
    for order in range(4):
        hit = knots == knot_offset[..., None, :] + order
        spread = spread + jnp.where(hit, basis[order][..., None, :], 0.0)
    spread = spread * live[..., None, None]
    return jnp.moveaxis(partials, 0, -2)[..., :, None, :] * spread[..., None, :, :]

def cholesky_factor(matrix, size):
    lower = [[None for column in range(size)] for row in range(size)]
    for column in range(size):
        total = matrix[column][column]
        for inner in range(column):
            total = total - lower[column][inner] * lower[column][inner]
        pivot = jnp.sqrt(total)
        lower[column][column] = pivot
        for row in range(column + 1, size):
            accum = matrix[row][column]
            for inner in range(column):
                accum = accum - lower[row][inner] * lower[column][inner]
            lower[row][column] = accum / pivot
    return lower

def cholesky_solve(lower, rhs, size):
    forward = []
    for row in range(size):
        accum = rhs[row]
        for inner in range(row):
            accum = accum - lower[row][inner] * forward[inner]
        forward.append(accum / lower[row][row])
    answer = [None for row in range(size)]
    for row in reversed(range(size)):
        accum = forward[row]
        for inner in range(row + 1, size):
            accum = accum - lower[inner][row] * answer[inner]
        answer[row] = accum / lower[row][row]
    return answer

def star_update(partials, first, live):
    normal = [[lax.optimization_barrier(jnp.sum(live * partials[row] * partials[column], axis=0)) + (star_prior if row == column else 0.0) for column in range(5)] for row in range(5)]
    rhs = [lax.optimization_barrier(jnp.sum(partials[row] * first, axis=0)) for row in range(5)]
    lower = cholesky_factor(normal, 5)
    step = cholesky_solve(lower, rhs, 5)
    fitted = partials[0] * step[0]
    for row in range(1, 5):
        fitted = fitted + partials[row] * step[row]
    return (jnp.stack(step), first - live * fitted)

def cell_terms(cell_phase, cell_offset, cell_axis, cell_star, cell_observed, cell_live, cell_values):
    rows = design_rows(cell_phase, cell_offset, cell_axis, cell_live)
    predicted = jnp.einsum('tmas,tma->ts', rows, cell_values, precision=highest)
    first = cell_live[:, None] * cell_observed - predicted
    step, second = star_update(cell_star, first, cell_live[:, None])
    gradient = jnp.einsum('tmas,ts->tma', rows, second, precision=highest)
    return (rows, step, gradient)

def band_products(rows):
    pieces = []
    for shift in range(4):
        left = rows[..., :KB - shift, :]
        right = rows[..., shift:, :]
        product = jnp.einsum('...mas,...nas->...mna', left, right, precision=highest)
        filler = jnp.zeros(product.shape[:-1] + (shift,), jnp.float32)
        pieces.append(jnp.concatenate([product, filler], axis=-1))
    return jnp.stack(pieces, axis=-2)

def band_apply(band, vector):
    result = jnp.einsum('bmna,nba->mba', band[:, :, :, 0, :], vector, precision=highest)
    for shift in range(1, 4):
        filler = jnp.zeros(vector.shape[:-1] + (shift,), jnp.float32)
        ahead = jnp.concatenate([vector[..., shift:], filler], axis=-1)
        result = result + jnp.einsum('bmna,nba->mba', band[:, :, :, shift, :], ahead, precision=highest)
        lagged = jnp.einsum('bnma,nba->mba', band[:, :, :, shift, :], vector, precision=highest)
        result = result + jnp.concatenate([filler, lagged[..., :KB - shift]], axis=-1)
    return result

def diagonal_factor(band):
    shifted = 2.0 * smoothing + damping
    entries = [[band[:, row, column, 0, :] + (shifted if row == column else 0.0) for column in range(4)] for row in range(4)]
    return cholesky_factor(entries, 4)

def sweep(band, lower, gradient, solution, padded):
    count = band.shape[0]
    applied = band_apply(band, solution.reshape(4, count, KB))
    regular = smoothing * (2.0 * solution - padded[:, :-2] - padded[:, 2:]) + damping * solution
    misfit = gradient - applied - regular.reshape(4, count, KB)
    correction = cholesky_solve(lower, [misfit[row] for row in range(4)], 4)
    return solution + relaxation * jnp.stack(correction).reshape(4, count * KB)

def reference(attitude, star_partials, attitude_partials, observed, phase, knot_offset, cell_counts, interval_owner, block_slot):
    block_ids = (interval_owner[:, :, 0] * BPD + block_slot).astype(jnp.int32)
    blocks = attitude.reshape(4, BLOCKS, KB).transpose(1, 0, 2)
    transit = lax.broadcasted_iota(jnp.int32, (CELLS, NT), 1)
    live = jnp.where(transit < cell_counts[:, None], 1.0, 0.0).astype(jnp.float32)
    items = (phase.reshape(NT, CELLS, CS).transpose(1, 0, 2), knot_offset.reshape(NT, CELLS, CS).transpose(1, 0, 2), attitude_partials.reshape(4, NT, CELLS, CS).transpose(2, 0, 1, 3), star_partials.reshape(5, NT, CELLS, CS).transpose(2, 0, 1, 3), observed.reshape(NT, CELLS, CS).transpose(1, 0, 2), live, block_ids)

    def per_cell(carry, pieces):
        band_sum, grad_sum = carry
        cell_phase, cell_offset, cell_axis, cell_star, cell_observed, cell_live, ids = pieces
        rows, step, gradient = cell_terms(cell_phase, cell_offset, cell_axis, cell_star, cell_observed, cell_live, blocks[ids])
        band_sum = band_sum.at[ids].add(band_products(rows))
        grad_sum = grad_sum.at[ids].add(gradient)
        return ((band_sum, grad_sum), step)
    start = (jnp.zeros((BLOCKS, 4, 4, 4, KB), jnp.float32), jnp.zeros((BLOCKS, 4, KB), jnp.float32))
    (band_sum, grad_sum), steps = lax.scan(per_cell, start, items)
    star_step = steps.transpose(1, 0, 2).reshape(5, STARS)
    gradient = grad_sum.transpose(1, 0, 2)
    lower = diagonal_factor(band_sum)
    solution = jnp.zeros((4, KNOTS), jnp.float32)
    for index in range(ITERS):
        padded = jnp.pad(solution, ((0, 0), (1, 1)))
        solution = sweep(band_sum, lower, gradient, solution, padded)
    return (star_step, solution)
```

```python
import functools

import jax
import jax.numpy as jnp
from jax import lax
from jax.experimental import pallas as pl
from jax.experimental.pallas import tpu as pltpu
from jax.sharding import PartitionSpec as P

CS = 128
KB = 16
ITERS = 6
LANES = 128
PAIRS = tuple((m, n) for m in range(4) for n in range(m, 4))
ROWS = 5
VMEM_LIMIT = 48 * 1024 * 1024

smoothing = 16.0
damping = 2.0
relaxation = 0.5
star_prior = 1.0


def spline_basis(phase):
    square = phase * phase
    cube = square * phase
    rest = 1.0 - phase
    return (
        rest * rest * rest * (1.0 / 6.0),
        (3.0 * cube - 6.0 * square + 4.0) * (1.0 / 6.0),
        (-3.0 * cube + 3.0 * square + 3.0 * phase + 1.0) * (1.0 / 6.0),
        cube * (1.0 / 6.0),
    )


def cholesky_factor(matrix, size):
    lower = [[None for column in range(size)] for row in range(size)]
    inverse = [None for column in range(size)]
    for column in range(size):
        total = matrix[column][column]
        for inner in range(column):
            total = total - lower[column][inner] * lower[column][inner]
        inverse[column] = 1.0 / jnp.sqrt(total)
        for row in range(column + 1, size):
            accum = matrix[row][column]
            for inner in range(column):
                accum = accum - lower[row][inner] * lower[column][inner]
            lower[row][column] = accum * inverse[column]
    return lower, inverse


def cholesky_solve(lower, inverse, rhs, size):
    forward = []
    for row in range(size):
        accum = rhs[row]
        for inner in range(row):
            accum = accum - lower[row][inner] * forward[inner]
        forward.append(accum * inverse[row])
    answer = [None for row in range(size)]
    for row in reversed(range(size)):
        accum = forward[row]
        for inner in range(row + 1, size):
            accum = accum - lower[inner][row] * answer[inner]
        answer[row] = accum * inverse[row]
    return answer


def split(value):
    high = value.astype(jnp.bfloat16)
    low = (value - high.astype(jnp.float32)).astype(jnp.bfloat16)
    return high, low


def pair_rows(value):
    return jnp.broadcast_to(value, (KB, LANES))


def product(weights, matrix_high, matrix_low):
    return lax.dot_general(
        weights,
        jnp.concatenate([matrix_high, matrix_low], axis=1),
        (((1,), (1,)), ((), ())),
        preferred_element_type=jnp.float32,
    )


def normal_kernel(
    spread, counts, home, halo, phase_ref, offset_ref, axis_ref, out_ref, total, weights, basis, offsets
):
    transits, stars = phase_ref.shape
    cells = stars // LANES
    knots = lax.broadcasted_iota(jnp.int32, (KB, LANES), 0)
    left_half = lax.broadcasted_iota(jnp.int32, (8, LANES), 1) < 64
    total[...] = jnp.zeros_like(total)
    weights[...] = jnp.zeros_like(weights)
    groups = transits // 8

    def group(index, carry):
        cell = index // groups
        first = pl.multiple_of((index % groups) * 8, 8)
        rows = pl.ds(first, 8)
        columns = pl.ds(pl.multiple_of(cell * LANES, LANES), LANES)
        number = first + lax.broadcasted_iota(jnp.int32, (8, LANES), 0)
        live = jnp.where(number < counts[cell], 1.0, 0.0)
        values = spline_basis(phase_ref[rows, columns])
        for shift in range(4):
            for order in range(4 - shift):
                basis[shift * 4 + order] = values[order] * values[order + shift]
        offsets[...] = offset_ref[rows, columns]
        parts = [axis_ref[m, rows, columns] for m in range(4)]
        lively = [part * live for part in parts]
        for place, (m, n) in enumerate(PAIRS):
            row = place if place < ROWS else place + 3
            weights[pl.ds(row, 8, stride=16), :] = lively[m] * parts[n]
        for j in range(8):
            relative = knots - pair_rows(offsets[pl.ds(j, 1), :])
            hits = [relative == order for order in range(4)]
            highs, lows = [], []
            for shift in range(4):
                piece = jnp.zeros((KB, LANES), jnp.float32)
                for order in range(4 - shift):
                    value = pair_rows(basis[shift * 4 + order, pl.ds(j, 1), :])
                    piece = jnp.where(hits[order], value, piece)
                high, low = split(piece)
                highs.append(high)
                lows.append(low)
            weight_high, weight_low = split(weights[pl.ds(j * 16, 16), :])
            left = jnp.concatenate([weight_high, weight_low], axis=0)
            right = jnp.concatenate([weight_high, jnp.zeros_like(weight_low)], axis=0)
            result = product(
                jnp.concatenate([left, right], axis=1),
                jnp.concatenate(highs + highs, axis=0),
                jnp.concatenate(lows + lows, axis=0),
            )
            band = jnp.where(
                left_half, result[0:8] + result[16:24], result[8:16] + result[24:32]
            )
            transit = cell * transits + first + j
            for place in (home[transit], halo[transit]):
                block = pl.ds(pl.multiple_of(place * 8, 8), 8)
                total[block, :] = total[block, :] + band
        return carry

    lax.fori_loop(0, cells * groups, group, 0)

    def pack(index, carry):
        source = pl.multiple_of(index * 64, 64)
        target = pl.multiple_of(index * 8 * ROWS, 8)
        for j in range(8):
            out_ref[pl.ds(target + j * ROWS, ROWS), :] = total[pl.ds(source + j * 8, ROWS), :]
        return carry

    lax.fori_loop(0, out_ref.shape[0] // (8 * ROWS), pack, 0)


def star_kernel(
    spread,
    counts,
    home,
    halo,
    ids,
    attitude_ref,
    phase_ref,
    offset_ref,
    axis_ref,
    star_ref,
    observed_ref,
    step_ref,
    out_ref,
    total,
    table,
    first_order,
    sums,
    steps,
    weights,
    basis,
    offsets,
):
    transits, stars = phase_ref.shape
    cells = stars // LANES
    groups = transits // 8
    knots = lax.broadcasted_iota(jnp.int32, (KB, LANES), 0)
    lanes_block = lax.broadcasted_iota(jnp.int32, (8, LANES), 1) // KB
    total[...] = jnp.zeros_like(total)
    weights[...] = jnp.zeros_like(weights)
    sums[...] = jnp.zeros_like(sums)
    entries = [(row, column) for row in range(5) for column in range(row + 1)]

    def predict_cell(cell, carry):
        columns = pl.ds(pl.multiple_of(cell * LANES, LANES), LANES)

        def predict(index, accumulated):
            first = pl.multiple_of(index * 8, 8)
            rows = pl.ds(first, 8)
            for j in range(8):
                block = ids[cell * transits + first + j]
                row = attitude_ref[pl.ds(block // 2, 1), :]
                table[pl.ds(j, 1), :] = pltpu.roll(row, (block % 2) * 64, axis=1)
            looked = table[...]
            number = first + lax.broadcasted_iota(jnp.int32, (8, LANES), 0)
            live = jnp.where(number < counts[cell], 1.0, 0.0)
            values = spline_basis(phase_ref[rows, columns])
            offset = offset_ref[rows, columns]
            predicted = jnp.zeros((8, LANES), jnp.float32)
            for m in range(4):
                spline = jnp.zeros((8, LANES), jnp.float32)
                for order in range(4):
                    found = jnp.take_along_axis(looked, offset + (m * KB + order), axis=1)
                    spline = spline + found * values[order]
                predicted = predicted + spline * axis_ref[m, rows, columns]
            first_value = live * (observed_ref[rows, columns] - predicted)
            first_order[rows, columns] = first_value
            parts = [star_ref[row, rows, columns] for row in range(5)]
            lively = [part * live for part in parts]
            added = [lively[row] * parts[column] for row, column in entries]
            added += [part * first_value for part in parts]
            return tuple(old + new for old, new in zip(accumulated, added))

        start = tuple(jnp.zeros((8, LANES), jnp.float32) for entry in range(20))
        accumulated = lax.fori_loop(0, groups, predict, start)
        for entry in range(20):
            sums[entry, pl.ds(cell, 1), :] = jnp.sum(accumulated[entry], axis=0, keepdims=True)
        return carry

    lax.fori_loop(0, cells, predict_cell, 0)

    normal = [[None for column in range(5)] for row in range(5)]
    for entry, (row, column) in enumerate(entries):
        normal[row][column] = sums[entry] + (star_prior if row == column else 0.0)
    lower, inverse = cholesky_factor(normal, 5)
    answer = cholesky_solve(lower, inverse, [sums[15 + row] for row in range(5)], 5)
    for row in range(5):
        steps[row] = answer[row]
        for cell in range(cells):
            step_ref[row : row + 1, cell * LANES : (cell + 1) * LANES] = answer[row][
                cell : cell + 1
            ]

    def group(index, carry):
        cell = index // groups
        first = pl.multiple_of((index % groups) * 8, 8)
        rows = pl.ds(first, 8)
        columns = pl.ds(pl.multiple_of(cell * LANES, LANES), LANES)
        number = first + lax.broadcasted_iota(jnp.int32, (8, LANES), 0)
        live = jnp.where(number < counts[cell], 1.0, 0.0)
        fitted = jnp.zeros((8, LANES), jnp.float32)
        for row in range(5):
            step = jnp.broadcast_to(steps[row, pl.ds(cell, 1), :], (8, LANES))
            fitted = fitted + star_ref[row, rows, columns] * step
        second = first_order[rows, columns] - live * fitted
        for m in range(4):
            value = axis_ref[m, rows, columns] * second
            high = value.astype(jnp.bfloat16).astype(jnp.float32)
            weights[pl.ds(m, 8, stride=16), :] = high
            weights[pl.ds(4 + m, 8, stride=16), :] = value - high
        values = spline_basis(phase_ref[rows, columns])
        for order in range(4):
            basis[order] = values[order]
        offsets[...] = offset_ref[rows, columns]
        for j in range(8):
            relative = knots - pair_rows(offsets[pl.ds(j, 1), :])
            piece = jnp.zeros((KB, LANES), jnp.float32)
            for order in range(4):
                value = pair_rows(basis[order, pl.ds(j, 1), :])
                piece = jnp.where(relative == order, value, piece)
            high, low = split(piece)
            weight = weights[pl.ds(j * 16, 16), :]
            right = jnp.where(knots < 4, weight, 0.0)
            result = product(
                jnp.concatenate([weight, right], axis=1).astype(jnp.bfloat16),
                jnp.concatenate([high] * 8, axis=0),
                jnp.concatenate([low] * 8, axis=0),
            )[0:8]
            transit = cell * transits + first + j
            for place in (home[transit], halo[transit]):
                owner = place // spread
                slot = place % spread
                chosen = jnp.where(lanes_block == slot % 8, result, 0.0)
                tile = owner * ((spread + 7) // 8) + slot // 8
                block = pl.ds(pl.multiple_of(tile * 8, 8), 8)
                total[block, :] = total[block, :] + chosen
        return carry

    lax.fori_loop(0, cells * groups, group, 0)

    def pack(index, carry):
        source = pl.multiple_of(index * 16, 16)
        first_tile = total[pl.ds(source, 8), :]
        second_tile = total[pl.ds(source + 8, 8), :]
        target = pl.multiple_of(index * 8, 8)
        out_ref[pl.ds(target, 4), :] = first_tile[0:4] + first_tile[4:8]
        out_ref[pl.ds(target + 4, 4), :] = second_tile[0:4] + second_tile[4:8]
        return carry

    lax.fori_loop(0, out_ref.shape[0] // 8, pack, 0)


def sweep_kernel(spread, ends, band_ref, gradient_ref, out_ref, band):
    width = band.shape[2]
    tiles = width // LANES
    lane_block = lax.broadcasted_iota(jnp.int32, (8, LANES), 1) // KB
    filler = jnp.zeros((8 - ROWS, LANES), jnp.float32)
    for half in range(2):
        for shift in range(4):
            start = half * 64 + shift * KB
            for tile in range(tiles):
                merged = jnp.zeros((8, LANES), jnp.float32)
                for place in range(min(8, spread - tile * 8)):
                    block = tile * 8 + place
                    piece = jnp.concatenate(
                        [band_ref[block * ROWS : (block + 1) * ROWS, :], filler], axis=0
                    )
                    moved = (place * KB - start) % LANES
                    if moved:
                        piece = pltpu.roll(piece, moved, axis=1)
                    merged = jnp.where(lane_block == place, piece, merged)
                band[shift, half * 8 : half * 8 + 8, tile * LANES : (tile + 1) * LANES] = merged
    index = {}
    for place, (m, n) in enumerate(PAIRS):
        row = place if place < ROWS else place + 3
        index[(m, n)] = row
        index[(n, m)] = row

    def row_of(shift, m, n):
        return band[shift, index[(m, n)] : index[(m, n)] + 1, :]

    ahead = [
        [jnp.concatenate([row_of(shift, m, n) for n in range(4)], axis=0) for m in range(4)]
        for shift in range(4)
    ]
    behind = [
        [pltpu.roll(ahead[shift][m], shift, axis=1) if shift else None for m in range(4)]
        for shift in range(4)
    ]
    shifted = 2.0 * smoothing + damping
    diagonal = [
        [row_of(0, row, column) + (shifted if row == column else 0.0) for column in range(4)]
        for row in range(4)
    ]
    lower, inverse = cholesky_factor(diagonal, 4)
    gradient = jnp.concatenate(
        [gradient_ref[tile * 4 : (tile + 1) * 4, :] for tile in range(tiles)], axis=1
    )
    lane = lax.broadcasted_iota(jnp.int32, (4, width), 1)
    keep = jnp.where((lane >= ends[0]) & (lane < ends[1]), relaxation, 0.0)
    answer = jnp.zeros((4, width), jnp.float32)
    for sweep in range(ITERS):
        misfit = gradient
        if sweep:
            moved = {}
            for shift in range(1, 4):
                moved[shift] = pltpu.roll(answer, width - shift, axis=1)
                moved[-shift] = pltpu.roll(answer, shift, axis=1)
            applied = []
            for m in range(4):
                terms = ahead[0][m] * answer
                for shift in range(1, 4):
                    terms = terms + ahead[shift][m] * moved[shift]
                    terms = terms + behind[shift][m] * moved[-shift]
                applied.append(jnp.sum(terms, axis=0, keepdims=True))
            regular = smoothing * (2.0 * answer - moved[-1] - moved[1]) + damping * answer
            misfit = gradient - regular - jnp.concatenate(applied, axis=0)
        correction = cholesky_solve(lower, inverse, [misfit[m : m + 1] for m in range(4)], 4)
        answer = answer + keep * jnp.concatenate(correction, axis=0)
    out_ref[...] = answer[:, KB : KB + out_ref.shape[1]]


def in_vmem(count):
    return [pl.BlockSpec(memory_space=pltpu.VMEM) for operand in range(count)]


def in_smem(count):
    return [pl.BlockSpec(memory_space=pltpu.SMEM) for operand in range(count)]


def params():
    return pltpu.CompilerParams(vmem_limit_bytes=VMEM_LIMIT)


def halving_sum(parts, axes, devices):
    me = lax.axis_index(axes)
    for bit in range(devices.bit_length() - 1):
        half = parts.shape[0] // 2
        upper = (me >> bit) & 1
        kept = lax.dynamic_slice_in_dim(parts, upper * half, half, 0)
        sent = lax.dynamic_slice_in_dim(parts, (1 - upper) * half, half, 0)
        pairs = [(i, i ^ (1 << bit)) for i in range(devices)]
        parts = kept + lax.ppermute(sent, axes, pairs)
    return parts


def per_device(
    attitude,
    star_partials,
    attitude_partials,
    observed,
    phase,
    knot_offset,
    cell_counts,
    interval_owner,
    block_slot,
):
    axes = ("cells", "tm")
    devices = lax.axis_size("cells") * lax.axis_size("tm")
    levels = devices.bit_length() - 1
    cells = cell_counts.shape[0]
    transits = observed.shape[0]
    total = cells * transits
    stars = cells * CS
    blocks = attitude.shape[1] // KB
    spread = blocks + 2
    tiles = (spread + 7) // 8
    width = tiles * LANES
    me = lax.axis_index(axes)

    owners = interval_owner.reshape(total)
    slots = block_slot.reshape(total)

    def position(owner):
        reversed_bits = jnp.zeros_like(owner)
        for bit in range(levels):
            reversed_bits = reversed_bits | (((owner >> bit) & 1) << (levels - 1 - bit))
        return reversed_bits * spread

    nowhere = devices * spread
    home = position(owners) + slots + 1
    before = jnp.where(owners > 0, position(jnp.maximum(owners - 1, 0)) + spread - 1, nowhere)
    after = jnp.where(owners < devices - 1, position(jnp.minimum(owners + 1, devices - 1)), nowhere)
    halo = jnp.where(slots == 0, before, jnp.where(slots == blocks - 1, after, nowhere))
    ids = owners * blocks + slots

    table = attitude.reshape(4, blocks, KB).transpose(1, 0, 2).reshape(blocks // 2, 8 * KB)
    whole = lax.all_to_all(
        jnp.broadcast_to(table[None], (devices,) + table.shape),
        axes,
        split_axis=0,
        concat_axis=0,
        tiled=True,
    ).reshape(devices * blocks // 2, 8 * KB)

    f32 = jnp.float32
    normals = pl.pallas_call(
        functools.partial(normal_kernel, spread),
        out_shape=jax.ShapeDtypeStruct((devices * spread * ROWS, LANES), f32),
        in_specs=in_smem(3) + in_vmem(3),
        out_specs=in_vmem(1)[0],
        scratch_shapes=[
            pltpu.VMEM(((devices * spread + 1) * 8, LANES), f32),
            pltpu.VMEM((8 * 16, LANES), f32),
            pltpu.VMEM((16, 8, LANES), f32),
            pltpu.VMEM((8, LANES), jnp.int32),
        ],
        compiler_params=params(),
        name="normals",
    )(cell_counts, home, halo, phase, knot_offset, attitude_partials)

    star_step, gradients = pl.pallas_call(
        functools.partial(star_kernel, spread),
        out_shape=[
            jax.ShapeDtypeStruct((5, stars), f32),
            jax.ShapeDtypeStruct((devices * tiles * 4, LANES), f32),
        ],
        in_specs=in_smem(4) + in_vmem(6),
        out_specs=in_vmem(2),
        scratch_shapes=[
            pltpu.VMEM(((devices + 1) * tiles * 8, LANES), f32),
            pltpu.VMEM((8, LANES), f32),
            pltpu.VMEM((transits, stars), f32),
            pltpu.VMEM((20, 8, LANES), f32),
            pltpu.VMEM((5, 8, LANES), f32),
            pltpu.VMEM((8 * 16, LANES), f32),
            pltpu.VMEM((4, 8, LANES), f32),
            pltpu.VMEM((8, LANES), jnp.int32),
        ],
        compiler_params=params(),
        name="stars",
    )(
        cell_counts,
        home,
        halo,
        ids,
        whole,
        phase,
        knot_offset,
        attitude_partials,
        star_partials,
        observed,
    )

    band = halving_sum(normals, axes, devices)
    gradient = halving_sum(gradients, axes, devices)
    ends = jnp.stack(
        [
            jnp.where(me == 0, KB, 0),
            jnp.where(me == devices - 1, (spread - 1) * KB, spread * KB),
        ]
    ).astype(jnp.int32)
    attitude_step = pl.pallas_call(
        functools.partial(sweep_kernel, spread),
        out_shape=jax.ShapeDtypeStruct((4, blocks * KB), f32),
        in_specs=in_smem(1) + in_vmem(2),
        out_specs=in_vmem(1)[0],
        scratch_shapes=[pltpu.VMEM((4, 16, width), f32)],
        compiler_params=params(),
        name="sweeps",
    )(ends, band, gradient)
    return (star_step, attitude_step)


def solution(mesh):
    split_axes = ("cells", "tm")
    placed = (
        P(None, split_axes),
        P(None, None, split_axes),
        P(None, None, split_axes),
        P(None, split_axes),
        P(None, split_axes),
        P(None, split_axes),
        P(split_axes),
        P(split_axes, None, None),
        P(split_axes, None),
    )
    return jax.shard_map(
        per_device,
        mesh=mesh,
        in_specs=placed,
        out_specs=(P(None, split_axes), P(None, split_axes)),
        check_vma=False,
    )
```

```python
import functools

import jax
import jax.numpy as jnp
from jax import lax
from jax.experimental import pallas as pl
from jax.experimental.pallas import tpu as pltpu
from jax.sharding import PartitionSpec as P

CS = 128
KB = 16
ITERS = 6
LANES = 128
PAIRS = tuple((m, n) for m in range(4) for n in range(m, 4))
ROWS = 5
UNROLL = 4
VMEM_LIMIT = 48 * 1024 * 1024

smoothing = 16.0
damping = 2.0
relaxation = 0.5
star_prior = 1.0


def spline_basis(phase):
    square = phase * phase
    cube = square * phase
    rest = 1.0 - phase
    return (
        rest * rest * rest * (1.0 / 6.0),
        (3.0 * cube - 6.0 * square + 4.0) * (1.0 / 6.0),
        (-3.0 * cube + 3.0 * square + 3.0 * phase + 1.0) * (1.0 / 6.0),
        cube * (1.0 / 6.0),
    )


def cholesky_factor(matrix, size):
    lower = [[None for column in range(size)] for row in range(size)]
    inverse = [None for column in range(size)]
    for column in range(size):
        total = matrix[column][column]
        for inner in range(column):
            total = total - lower[column][inner] * lower[column][inner]
        inverse[column] = 1.0 / jnp.sqrt(total)
        for row in range(column + 1, size):
            accum = matrix[row][column]
            for inner in range(column):
                accum = accum - lower[row][inner] * lower[column][inner]
            lower[row][column] = accum * inverse[column]
    return lower, inverse


def cholesky_solve(lower, inverse, rhs, size):
    forward = []
    for row in range(size):
        accum = rhs[row]
        for inner in range(row):
            accum = accum - lower[row][inner] * forward[inner]
        forward.append(accum * inverse[row])
    answer = [None for row in range(size)]
    for row in reversed(range(size)):
        accum = forward[row]
        for inner in range(row + 1, size):
            accum = accum - lower[inner][row] * answer[inner]
        answer[row] = accum * inverse[row]
    return answer


def split(value):
    high = value.astype(jnp.bfloat16)
    low = (value - high.astype(jnp.float32)).astype(jnp.bfloat16)
    return high, low


def over_groups(cells, groups, body, unroll):
    def cell_body(cell, carry):
        def group_body(index, inner):
            body(cell, index)
            return inner

        return lax.fori_loop(0, groups, group_body, carry, unroll=unroll)

    lax.fori_loop(0, cells, cell_body, 0)


def pair_rows(value):
    return jnp.broadcast_to(value, (KB, LANES))


def product(weights, matrix_high, matrix_low):
    return lax.dot_general(
        weights,
        jnp.concatenate([matrix_high, matrix_low], axis=1),
        (((1,), (1,)), ((), ())),
        preferred_element_type=jnp.float32,
    )


def normal_kernel(
    spread, counts, home, halo, phase_ref, offset_ref, axis_ref, out_ref, total, weights, basis, offsets
):
    transits, stars = phase_ref.shape
    cells = stars // LANES
    knots = lax.broadcasted_iota(jnp.int32, (KB, LANES), 0)
    total[...] = jnp.zeros_like(total)
    weights[...] = jnp.zeros_like(weights)
    groups = transits // 8

    def group(cell, index):
        first = pl.multiple_of(index * 8, 8)
        rows = pl.ds(first, 8)
        columns = pl.ds(pl.multiple_of(cell * LANES, LANES), LANES)
        number = first + lax.broadcasted_iota(jnp.int32, (8, LANES), 0)
        live = jnp.where(number < counts[cell], 1.0, 0.0)
        values = spline_basis(phase_ref[rows, columns])
        for shift in range(4):
            for order in range(4 - shift):
                basis[shift * 4 + order] = values[order] * values[order + shift]
        offsets[...] = offset_ref[rows, columns]
        parts = [axis_ref[m, rows, columns] for m in range(4)]
        lively = [part * live for part in parts]
        for place, (m, n) in enumerate(PAIRS):
            row = place if place < ROWS else place + 3
            weights[pl.ds(row, 8, stride=16), :] = lively[m] * parts[n]
        for j in range(8):
            relative = knots - pair_rows(offsets[pl.ds(j, 1), :])
            hits = [relative == order for order in range(4)]
            highs, lows = [], []
            for shift in range(4):
                piece = jnp.zeros((KB, LANES), jnp.float32)
                for order in range(4 - shift):
                    value = pair_rows(basis[shift * 4 + order, pl.ds(j, 1), :])
                    piece = jnp.where(hits[order], value, piece)
                high, low = split(piece)
                highs.append(high)
                lows.append(low)
            weight_high, weight_low = split(weights[pl.ds(j * 16, 16), :])
            left = jnp.concatenate([weight_high, weight_low], axis=0)
            right = jnp.concatenate([weight_high, jnp.zeros_like(weight_low)], axis=0)
            result = product(
                jnp.concatenate([left, right], axis=1),
                jnp.concatenate(highs, axis=0),
                jnp.concatenate(lows, axis=0),
            )
            band = jnp.concatenate(
                [result[0:8] + result[16:24], result[8:16] + result[24:32]], axis=1
            )
            for place in (home[cell, first + j], halo[cell, first + j]):
                block = pl.ds(pl.multiple_of(place * 8, 8), 8)
                total[block, :] = total[block, :] + band

    over_groups(cells, groups, group, UNROLL)

    def pack(index, carry):
        source = pl.multiple_of(index * 64, 64)
        target = pl.multiple_of(index * 8 * ROWS, 8)
        for j in range(8):
            out_ref[pl.ds(target + j * ROWS, ROWS), :] = total[pl.ds(source + j * 8, ROWS), :]
        return carry

    lax.fori_loop(0, out_ref.shape[0] // (8 * ROWS), pack, 0)


def star_kernel(
    spread,
    counts,
    home,
    halo,
    owners,
    slots,
    attitude_ref,
    phase_ref,
    offset_ref,
    axis_ref,
    star_ref,
    observed_ref,
    step_ref,
    out_ref,
    total,
    table,
    first_order,
    sums,
    steps,
    weights,
    basis,
    offsets,
):
    transits, stars = phase_ref.shape
    cells = stars // LANES
    groups = transits // 8
    knots = lax.broadcasted_iota(jnp.int32, (KB, LANES), 0)
    lanes_block = lax.broadcasted_iota(jnp.int32, (8, LANES), 1) // KB
    total[...] = jnp.zeros_like(total)
    weights[...] = jnp.zeros_like(weights)
    sums[...] = jnp.zeros_like(sums)
    sublane = lax.broadcasted_iota(jnp.int32, (8, LANES), 0)
    entries = [(row, column) for row in range(5) for column in range(row + 1)]

    def predict_cell(cell, carry):
        columns = pl.ds(pl.multiple_of(cell * LANES, LANES), LANES)

        def predict(index, accumulated):
            first = pl.multiple_of(index * 8, 8)
            rows = pl.ds(first, 8)
            shift = jnp.zeros((8, LANES), jnp.int32)
            for j in range(8):
                owner = owners[cell, first + j]
                slot = slots[cell, first + j]
                column = pl.multiple_of((slot >> 3) * LANES, LANES)
                table[index, pl.ds(j, 4, stride=8), :] = attitude_ref[owner, :, pl.ds(column, LANES)]
                shift = jnp.where(sublane == j, (slot & 7) * KB, shift)
            number = first + lax.broadcasted_iota(jnp.int32, (8, LANES), 0)
            live = jnp.where(number < counts[cell], 1.0, 0.0)
            values = spline_basis(phase_ref[rows, columns])
            offset = offset_ref[rows, columns] + shift
            places = [offset + order for order in range(4)]
            predicted = jnp.zeros((8, LANES), jnp.float32)
            for m in range(4):
                spline = jnp.zeros((8, LANES), jnp.float32)
                looked = table[index, m * 8 : m * 8 + 8, :]
                for order in range(4):
                    found = jnp.take_along_axis(looked, places[order], axis=1)
                    spline = spline + found * values[order]
                predicted = predicted + spline * axis_ref[m, rows, columns]
            first_value = live * (observed_ref[rows, columns] - predicted)
            first_order[rows, columns] = first_value
            parts = [star_ref[row, rows, columns] for row in range(5)]
            lively = [part * live for part in parts]
            added = [lively[row] * parts[column] for row, column in entries]
            added += [part * first_value for part in parts]
            return tuple(old + new for old, new in zip(accumulated, added))

        start = tuple(jnp.zeros((8, LANES), jnp.float32) for entry in range(20))
        accumulated = lax.fori_loop(0, groups, predict, start, unroll=8)
        for entry in range(20):
            sums[entry, pl.ds(cell, 1), :] = jnp.sum(accumulated[entry], axis=0, keepdims=True)
        return carry

    lax.fori_loop(0, cells, predict_cell, 0)

    normal = [[None for column in range(5)] for row in range(5)]
    for entry, (row, column) in enumerate(entries):
        normal[row][column] = sums[entry] + (star_prior if row == column else 0.0)
    lower, inverse = cholesky_factor(normal, 5)
    answer = cholesky_solve(lower, inverse, [sums[15 + row] for row in range(5)], 5)
    for row in range(5):
        steps[row] = answer[row]
        for cell in range(cells):
            step_ref[row : row + 1, cell * LANES : (cell + 1) * LANES] = answer[row][
                cell : cell + 1
            ]

    def group(cell, index):
        first = pl.multiple_of(index * 8, 8)
        rows = pl.ds(first, 8)
        columns = pl.ds(pl.multiple_of(cell * LANES, LANES), LANES)
        number = first + lax.broadcasted_iota(jnp.int32, (8, LANES), 0)
        live = jnp.where(number < counts[cell], 1.0, 0.0)
        fitted = jnp.zeros((8, LANES), jnp.float32)
        for row in range(5):
            step = jnp.broadcast_to(steps[row, pl.ds(cell, 1), :], (8, LANES))
            fitted = fitted + star_ref[row, rows, columns] * step
        second = first_order[rows, columns] - live * fitted
        for m in range(4):
            value = axis_ref[m, rows, columns] * second
            high = value.astype(jnp.bfloat16).astype(jnp.float32)
            weights[pl.ds(m, 8, stride=16), :] = high
            weights[pl.ds(4 + m, 8, stride=16), :] = value - high
        values = spline_basis(phase_ref[rows, columns])
        for order in range(4):
            basis[order] = values[order]
        offsets[...] = offset_ref[rows, columns]
        for j in range(8):
            relative = knots - pair_rows(offsets[pl.ds(j, 1), :])
            piece = jnp.zeros((KB, LANES), jnp.float32)
            for order in range(4):
                value = pair_rows(basis[order, pl.ds(j, 1), :])
                piece = jnp.where(relative == order, value, piece)
            high, low = split(piece)
            weight = weights[pl.ds(j * 16, 16), :]
            right = jnp.where(knots < 4, weight, 0.0)
            result = product(
                jnp.concatenate([weight, right], axis=1).astype(jnp.bfloat16),
                jnp.concatenate([high] * 4, axis=0),
                jnp.concatenate([low] * 4, axis=0),
            )[0:8]
            result = jnp.concatenate([result, result], axis=1)
            for place in (home[cell, first + j], halo[cell, first + j]):
                chosen = jnp.where(lanes_block == (place & 7), result, 0.0)
                block = pl.ds(pl.multiple_of((place >> 3) * 8, 8), 8)
                total[block, :] = total[block, :] + chosen

    over_groups(cells, groups, group, UNROLL)

    def pack(index, carry):
        source = pl.multiple_of(index * 16, 16)
        first_tile = total[pl.ds(source, 8), :]
        second_tile = total[pl.ds(source + 8, 8), :]
        target = pl.multiple_of(index * 8, 8)
        out_ref[pl.ds(target, 4), :] = first_tile[0:4] + first_tile[4:8]
        out_ref[pl.ds(target + 4, 4), :] = second_tile[0:4] + second_tile[4:8]
        return carry

    lax.fori_loop(0, out_ref.shape[0] // 8, pack, 0)


def sweep_kernel(spread, axes, band_ref, gradient_ref, out_ref, band):
    width = band.shape[2]
    tiles = width // LANES
    lane_block = lax.broadcasted_iota(jnp.int32, (8, LANES), 1) // KB
    filler = jnp.zeros((8 - ROWS, LANES), jnp.float32)
    for half in range(2):
        for shift in range(4):
            start = half * 64 + shift * KB
            for tile in range(tiles):
                merged = jnp.zeros((8, LANES), jnp.float32)
                for place in range(min(8, spread - tile * 8)):
                    block = tile * 8 + place
                    piece = jnp.concatenate(
                        [band_ref[block * ROWS : (block + 1) * ROWS, :], filler], axis=0
                    )
                    moved = (place * KB - start) % LANES
                    if moved:
                        piece = pltpu.roll(piece, moved, axis=1)
                    merged = jnp.where(lane_block == place, piece, merged)
                band[shift, half * 8 : half * 8 + 8, tile * LANES : (tile + 1) * LANES] = merged
    index = {}
    for place, (m, n) in enumerate(PAIRS):
        row = place if place < ROWS else place + 3
        index[(m, n)] = row
        index[(n, m)] = row

    def row_of(shift, m, n):
        return band[shift, index[(m, n)] : index[(m, n)] + 1, :]

    ahead = [
        [jnp.concatenate([row_of(shift, m, n) for n in range(4)], axis=0) for m in range(4)]
        for shift in range(4)
    ]
    behind = [
        [pltpu.roll(ahead[shift][m], shift, axis=1) if shift else None for m in range(4)]
        for shift in range(4)
    ]
    shifted = 2.0 * smoothing + damping
    diagonal = [
        [row_of(0, row, column) + (shifted if row == column else 0.0) for column in range(4)]
        for row in range(4)
    ]
    lower, inverse = cholesky_factor(diagonal, 4)
    gradient = jnp.concatenate(
        [gradient_ref[tile * 4 : (tile + 1) * 4, :] for tile in range(tiles)], axis=1
    )
    lane = lax.broadcasted_iota(jnp.int32, (4, width), 1)
    me = lax.axis_index(axes)
    start = jnp.where(me == 0, KB, 0)
    stop = jnp.where(me == lax.axis_size(axes) - 1, (spread - 1) * KB, spread * KB)
    keep = jnp.where((lane >= start) & (lane < stop), relaxation, 0.0)
    answer = jnp.zeros((4, width), jnp.float32)
    for sweep in range(ITERS):
        misfit = gradient
        if sweep:
            moved = {}
            for shift in range(1, 4):
                moved[shift] = pltpu.roll(answer, width - shift, axis=1)
                moved[-shift] = pltpu.roll(answer, shift, axis=1)
            applied = []
            for m in range(4):
                terms = ahead[0][m] * answer
                for shift in range(1, 4):
                    terms = terms + ahead[shift][m] * moved[shift]
                    terms = terms + behind[shift][m] * moved[-shift]
                applied.append(jnp.sum(terms, axis=0, keepdims=True))
            regular = smoothing * (2.0 * answer - moved[-1] - moved[1]) + damping * answer
            misfit = gradient - regular - jnp.concatenate(applied, axis=0)
        correction = cholesky_solve(lower, inverse, [misfit[m : m + 1] for m in range(4)], 4)
        answer = answer + keep * jnp.concatenate(correction, axis=0)
    out_ref[...] = answer[:, KB : KB + out_ref.shape[1]]


def in_vmem(count):
    return [pl.BlockSpec(memory_space=pltpu.VMEM) for operand in range(count)]


def in_smem(count):
    return [pl.BlockSpec(memory_space=pltpu.SMEM) for operand in range(count)]


def work(microseconds):
    return pl.CostEstimate(flops=0, bytes_accessed=microseconds * 3_600_000, transcendentals=0)


def params():
    return pltpu.CompilerParams(vmem_limit_bytes=VMEM_LIMIT)


def call_normals(counts, home, halo, phase, knot_offset, partials, devices, spread):
    f32 = jnp.float32
    return pl.pallas_call(
        functools.partial(normal_kernel, spread),
        out_shape=jax.ShapeDtypeStruct((devices * spread * ROWS, LANES), f32),
        in_specs=in_smem(3) + in_vmem(3),
        out_specs=in_vmem(1)[0],
        scratch_shapes=[
            pltpu.VMEM(((devices * spread + 1) * 8, LANES), f32),
            pltpu.VMEM((8 * 16, LANES), f32),
            pltpu.VMEM((16, 8, LANES), f32),
            pltpu.VMEM((8, LANES), jnp.int32),
        ],
        compiler_params=params(),
        cost_estimate=work(8),
        name="normals",
    )(counts, home, halo, phase, knot_offset, partials)


def call_stars(
    counts,
    home,
    halo,
    owners,
    slots,
    attitude,
    phase,
    knot_offset,
    partials,
    star_partials,
    observed,
    devices,
    spread,
):
    f32 = jnp.float32
    tiles = (spread + 7) // 8
    transits, stars = phase.shape
    return pl.pallas_call(
        functools.partial(star_kernel, spread),
        out_shape=[
            jax.ShapeDtypeStruct((5, stars), f32),
            jax.ShapeDtypeStruct((devices * tiles * 4, LANES), f32),
        ],
        in_specs=in_smem(5) + in_vmem(6),
        out_specs=in_vmem(2),
        scratch_shapes=[
            pltpu.VMEM(((devices + 1) * tiles * 8, LANES), f32),
            pltpu.VMEM((transits // 8, 32, LANES), f32),
            pltpu.VMEM((transits, stars), f32),
            pltpu.VMEM((20, 8, LANES), f32),
            pltpu.VMEM((5, 8, LANES), f32),
            pltpu.VMEM((8 * 16, LANES), f32),
            pltpu.VMEM((4, 8, LANES), f32),
            pltpu.VMEM((8, LANES), jnp.int32),
        ],
        compiler_params=params(),
        cost_estimate=work(10),
        name="stars",
    )(
        counts,
        home,
        halo,
        owners,
        slots,
        attitude,
        phase,
        knot_offset,
        partials,
        star_partials,
        observed,
    )


def exchange_sum(parts, axes, devices):
    me = lax.axis_index(axes)
    bits = list(range(devices.bit_length() - 1))
    groups = [bits[:1]] + [bits[start : start + 2] for start in range(1, len(bits), 2)]
    for group in groups:
        members = 1 << len(group)
        rows = parts.shape[0] // members
        mine = 0
        for bit in group:
            mine = mine * 2 + ((me >> bit) & 1)
        added = lax.dynamic_slice_in_dim(parts, mine * rows, rows, 0)
        arrived = []
        for other in range(1, members):
            mask = sum(1 << bit for place, bit in enumerate(reversed(group)) if (other >> place) & 1)
            sent = lax.dynamic_slice_in_dim(parts, (mine ^ other) * rows, rows, 0)
            arrived.append(lax.ppermute(sent, axes, [(i, i ^ mask) for i in range(devices)]))
        for part in arrived:
            added = added + part
        parts = added
    return parts


def per_device(
    attitude,
    star_partials,
    attitude_partials,
    observed,
    phase,
    knot_offset,
    cell_counts,
    interval_owner,
    block_slot,
):
    axes = ("cells", "tm")
    devices = lax.axis_size("cells") * lax.axis_size("tm")
    levels = devices.bit_length() - 1
    cells = cell_counts.shape[0]
    transits = observed.shape[0]
    blocks = attitude.shape[1] // KB
    spread = blocks + 2
    tiles = (spread + 7) // 8
    width = tiles * LANES

    owners = interval_owner.reshape(cells, transits)
    slots = block_slot

    def position(owner):
        reversed_bits = jnp.zeros_like(owner)
        for bit in range(levels):
            reversed_bits = reversed_bits | (((owner >> bit) & 1) << (levels - 1 - bit))
        return reversed_bits * spread

    nowhere = devices * spread
    home = position(owners) + slots + 1
    before = jnp.where(owners > 0, position(jnp.maximum(owners - 1, 0)) + spread - 1, nowhere)
    after = jnp.where(owners < devices - 1, position(jnp.minimum(owners + 1, devices - 1)), nowhere)
    halo = jnp.where(slots == 0, before, jnp.where(slots == blocks - 1, after, nowhere))

    def lane_place(place):
        return place // spread * (8 * tiles) + place % spread

    whole = lax.all_to_all(
        jnp.broadcast_to(attitude[None], (devices,) + attitude.shape),
        axes,
        split_axis=0,
        concat_axis=0,
        tiled=True,
    )
    normals = call_normals(
        cell_counts, home, halo, phase, knot_offset, attitude_partials, devices, spread
    )
    star_step, gradients = call_stars(
        cell_counts,
        lane_place(home),
        lane_place(halo),
        owners,
        slots,
        whole,
        phase,
        knot_offset,
        attitude_partials,
        star_partials,
        observed,
        devices,
        spread,
    )

    band = exchange_sum(normals, axes, devices)
    gradient = exchange_sum(gradients, axes, devices)
    attitude_step = pl.pallas_call(
        functools.partial(sweep_kernel, spread, axes),
        out_shape=jax.ShapeDtypeStruct((4, blocks * KB), jnp.float32),
        in_specs=in_vmem(2),
        out_specs=in_vmem(1)[0],
        scratch_shapes=[pltpu.VMEM((4, 16, width), jnp.float32)],
        compiler_params=params(),
        name="sweeps",
    )(band, gradient)
    return (star_step, attitude_step)


def solution(mesh):
    split_axes = ("cells", "tm")
    placed = (
        P(None, split_axes),
        P(None, None, split_axes),
        P(None, None, split_axes),
        P(None, split_axes),
        P(None, split_axes),
        P(None, split_axes),
        P(split_axes),
        P(split_axes, None, None),
        P(split_axes, None),
    )
    return jax.shard_map(
        per_device,
        mesh=mesh,
        in_specs=placed,
        out_specs=(P(None, split_axes), P(None, split_axes)),
        check_vma=False,
    )
```

```python
import functools

import jax
import jax.numpy as jnp
from jax import lax
from jax.experimental import pallas as pl
from jax.experimental.pallas import tpu as pltpu
from jax.sharding import PartitionSpec as P

CS = 128
KB = 16
ITERS = 6
LANES = 128
PAIRS = tuple((m, n) for m in range(4) for n in range(m, 4))
HOME, HALO, HOME_LANES, HALO_LANES, OWNER, SLOT, COUNT = range(7)
ROWS = 5
UNROLL = 4

smoothing = 16.0
damping = 2.0
relaxation = 0.5
star_prior = 1.0


def spline_basis(phase):
    square = phase * phase
    cube = square * phase
    rest = 1.0 - phase
    return (
        rest * rest * rest * (1.0 / 6.0),
        (3.0 * cube - 6.0 * square + 4.0) * (1.0 / 6.0),
        (-3.0 * cube + 3.0 * square + 3.0 * phase + 1.0) * (1.0 / 6.0),
        cube * (1.0 / 6.0),
    )


def cholesky_factor(matrix, size):
    lower = [[None for column in range(size)] for row in range(size)]
    inverse = [None for column in range(size)]
    for column in range(size):
        total = matrix[column][column]
        for inner in range(column):
            total = total - lower[column][inner] * lower[column][inner]
        inverse[column] = 1.0 / jnp.sqrt(total)
        for row in range(column + 1, size):
            accum = matrix[row][column]
            for inner in range(column):
                accum = accum - lower[row][inner] * lower[column][inner]
            lower[row][column] = accum * inverse[column]
    return lower, inverse


def cholesky_solve(lower, inverse, rhs, size):
    forward = []
    for row in range(size):
        accum = rhs[row]
        for inner in range(row):
            accum = accum - lower[row][inner] * forward[inner]
        forward.append(accum * inverse[row])
    answer = [None for row in range(size)]
    for row in reversed(range(size)):
        accum = forward[row]
        for inner in range(row + 1, size):
            accum = accum - lower[inner][row] * answer[inner]
        answer[row] = accum * inverse[row]
    return answer


def split(value):
    high = value.astype(jnp.bfloat16)
    low = (value - high.astype(jnp.float32)).astype(jnp.bfloat16)
    return high, low


def over_groups(cells, groups, body, unroll):
    def cell_body(cell, carry):
        def group_body(index, inner):
            body(cell, index)
            return inner

        return lax.fori_loop(0, groups, group_body, carry, unroll=unroll)

    lax.fori_loop(0, cells, cell_body, 0)


def pair_rows(value):
    return jnp.broadcast_to(value, (KB, LANES))


def product(weights, matrix_high, matrix_low):
    return lax.dot_general(
        weights,
        jnp.concatenate([matrix_high, matrix_low], axis=1),
        (((1,), (1,)), ((), ())),
        preferred_element_type=jnp.float32,
    )


def facts_kernel(blocks, counts, attitude_ref, owners_ref, slots_ref, facts_ref, wide_ref):
    devices = wide_ref.shape[0]
    levels = devices.bit_length() - 1
    spread = blocks + 2
    lanes = (spread + 7) // 8 * 8
    owners = owners_ref[...]
    slots = slots_ref[...]
    cells = owners.shape[0]

    def reverse(owner):
        reversed_bits = jnp.zeros_like(owner)
        for bit in range(levels):
            reversed_bits = reversed_bits | (((owner >> bit) & 1) << (levels - 1 - bit))
        return reversed_bits

    first = slots == 0
    final = slots == blocks - 1
    neighbour = owners + jnp.where(first, -1, jnp.where(final, 1, 0))
    nowhere = (neighbour == owners) | (neighbour < 0) | (neighbour >= devices)
    home_owner = reverse(owners)
    halo_owner = jnp.where(nowhere, devices, reverse(neighbour))
    home_place = slots + 1
    halo_place = jnp.where(first & ~nowhere, spread - 1, 0)
    facts_ref[HOME] = home_owner * spread + home_place
    facts_ref[HALO] = halo_owner * spread + halo_place
    facts_ref[HOME_LANES] = home_owner * lanes + home_place
    facts_ref[HALO_LANES] = halo_owner * lanes + halo_place
    facts_ref[OWNER] = owners
    facts_ref[SLOT] = slots
    for cell in range(cells):
        facts_ref[COUNT, cell : cell + 1, :] = jnp.full((1, owners.shape[1]), counts[cell], jnp.int32)
    attitude = attitude_ref[...]

    def copy(index, carry):
        wide_ref[index] = attitude
        return carry

    lax.fori_loop(0, devices, copy, 0, unroll=8)


def normal_kernel(
    axes,
    facts,
    phase_ref,
    offset_ref,
    axis_ref,
    kept_ref,
    sent_ref,
    total,
    weights,
    basis,
    offsets,
):
    transits, stars = phase_ref.shape
    cells = stars // LANES
    knots = lax.broadcasted_iota(jnp.int32, (KB, LANES), 0)
    total[...] = jnp.zeros_like(total)
    weights[...] = jnp.zeros_like(weights)
    groups = transits // 8

    def group(cell, index):
        first = pl.multiple_of(index * 8, 8)
        rows = pl.ds(first, 8)
        columns = pl.ds(pl.multiple_of(cell * LANES, LANES), LANES)
        number = first + lax.broadcasted_iota(jnp.int32, (8, LANES), 0)
        live = jnp.where(number < facts[COUNT, cell, 0], 1.0, 0.0)
        values = spline_basis(phase_ref[rows, columns])
        for shift in range(4):
            for order in range(4 - shift):
                basis[shift * 4 + order] = values[order] * values[order + shift]
        offsets[...] = offset_ref[rows, columns]
        parts = [axis_ref[m, rows, columns] for m in range(4)]
        lively = [part * live for part in parts]
        for place, (m, n) in enumerate(PAIRS):
            row = place if place < ROWS else place + 3
            weights[pl.ds(row, 8, stride=16), :] = lively[m] * parts[n]
        for j in range(8):
            relative = knots - pair_rows(offsets[pl.ds(j, 1), :])
            hits = [relative == order for order in range(4)]
            highs, lows = [], []
            for shift in range(4):
                piece = jnp.zeros((KB, LANES), jnp.float32)
                for order in range(4 - shift):
                    value = pair_rows(basis[shift * 4 + order, pl.ds(j, 1), :])
                    piece = jnp.where(hits[order], value, piece)
                high, low = split(piece)
                highs.append(high)
                lows.append(low)
            weight_high, weight_low = split(weights[pl.ds(j * 16, 16), :])
            left = jnp.concatenate([weight_high, weight_low], axis=0)
            right = jnp.concatenate([weight_high, jnp.zeros_like(weight_low)], axis=0)
            result = product(
                jnp.concatenate([left, right], axis=1),
                jnp.concatenate(highs, axis=0),
                jnp.concatenate(lows, axis=0),
            )
            band = jnp.concatenate(
                [result[0:8] + result[16:24], result[8:16] + result[24:32]], axis=1
            )
            for place in (facts[HOME, cell, first + j], facts[HALO, cell, first + j]):
                block = pl.ds(pl.multiple_of(place * 8, 8), 8)
                total[block, :] = total[block, :] + band

    over_groups(cells, groups, group, UNROLL)

    mine = lax.axis_index(axes) & 1
    half = kept_ref.shape[0] // ROWS * 8

    def pack(index, carry):
        target = pl.multiple_of(index * 8 * ROWS, 8)
        for out_ref, part in ((kept_ref, mine), (sent_ref, 1 - mine)):
            source = pl.multiple_of(part * half + index * 64, 64)
            for j in range(8):
                out_ref[pl.ds(target + j * ROWS, ROWS), :] = total[pl.ds(source + j * 8, ROWS), :]
        return carry

    lax.fori_loop(0, half // 64, pack, 0)


ENTRIES = tuple((row, column) for row in range(5) for column in range(row + 1))


def factor_kernel(facts, star_ref, factors_ref, sums):
    transits, stars = star_ref.shape[1:]
    sums[...] = jnp.zeros_like(sums)

    def cell_body(cell, carry):
        columns = pl.ds(pl.multiple_of(cell * LANES, LANES), LANES)

        def add(index, accumulated):
            first = pl.multiple_of(index * 8, 8)
            number = first + lax.broadcasted_iota(jnp.int32, (8, LANES), 0)
            live = jnp.where(number < facts[COUNT, cell, 0], 1.0, 0.0)
            parts = [star_ref[row, pl.ds(first, 8), columns] for row in range(5)]
            lively = [part * live for part in parts]
            return tuple(
                old + lively[row] * parts[column] for old, (row, column) in zip(accumulated, ENTRIES)
            )

        start = tuple(jnp.zeros((8, LANES), jnp.float32) for entry in ENTRIES)
        accumulated = lax.fori_loop(0, transits // 8, add, start, unroll=4)
        for entry in range(len(ENTRIES)):
            sums[entry, pl.ds(cell, 1), :] = jnp.sum(accumulated[entry], axis=0, keepdims=True)
        return carry

    lax.fori_loop(0, stars // LANES, cell_body, 0)
    normal = [[None for column in range(5)] for row in range(5)]
    for entry, (row, column) in enumerate(ENTRIES):
        normal[row][column] = sums[entry] + (star_prior if row == column else 0.0)
    lower, inverse = cholesky_factor(normal, 5)
    for entry, (row, column) in enumerate(ENTRIES):
        factors_ref[entry] = inverse[row] if row == column else lower[row][column]


def star_kernel(
    axes,
    facts,
    attitude_ref,
    factors_ref,
    phase_ref,
    offset_ref,
    axis_ref,
    star_ref,
    observed_ref,
    step_ref,
    kept_ref,
    sent_ref,
    total,
    table,
    first_order,
    sums,
    steps,
    weights,
    basis,
    offsets,
):
    transits, stars = phase_ref.shape
    cells = stars // LANES
    groups = transits // 8
    knots = lax.broadcasted_iota(jnp.int32, (KB, LANES), 0)
    lanes_block = lax.broadcasted_iota(jnp.int32, (8, LANES), 1) // KB
    total[...] = jnp.zeros_like(total)
    weights[...] = jnp.zeros_like(weights)
    sums[...] = jnp.zeros_like(sums)
    sublane = lax.broadcasted_iota(jnp.int32, (8, LANES), 0)

    def predict_cell(cell, carry):
        columns = pl.ds(pl.multiple_of(cell * LANES, LANES), LANES)

        def predict(index, accumulated):
            first = pl.multiple_of(index * 8, 8)
            rows = pl.ds(first, 8)
            shift = jnp.zeros((8, LANES), jnp.int32)
            for j in range(8):
                owner = facts[OWNER, cell, first + j]
                slot = facts[SLOT, cell, first + j]
                column = pl.multiple_of((slot >> 3) * LANES, LANES)
                table[index, pl.ds(j, 4, stride=8), :] = attitude_ref[owner, :, pl.ds(column, LANES)]
                shift = jnp.where(sublane == j, (slot & 7) * KB, shift)
            number = first + lax.broadcasted_iota(jnp.int32, (8, LANES), 0)
            live = jnp.where(number < facts[COUNT, cell, 0], 1.0, 0.0)
            values = spline_basis(phase_ref[rows, columns])
            offset = offset_ref[rows, columns] + shift
            places = [offset + order for order in range(4)]
            predicted = jnp.zeros((8, LANES), jnp.float32)
            for m in range(4):
                spline = jnp.zeros((8, LANES), jnp.float32)
                looked = table[index, m * 8 : m * 8 + 8, :]
                for order in range(4):
                    found = jnp.take_along_axis(looked, places[order], axis=1)
                    spline = spline + found * values[order]
                predicted = predicted + spline * axis_ref[m, rows, columns]
            first_value = live * (observed_ref[rows, columns] - predicted)
            first_order[rows, columns] = first_value
            parts = [star_ref[row, rows, columns] for row in range(5)]
            return tuple(old + part * first_value for old, part in zip(accumulated, parts))

        start = tuple(jnp.zeros((8, LANES), jnp.float32) for row in range(5))
        accumulated = lax.fori_loop(0, groups, predict, start, unroll=8)
        for entry in range(5):
            sums[entry, pl.ds(cell, 1), :] = jnp.sum(accumulated[entry], axis=0, keepdims=True)
        return carry

    lax.fori_loop(0, cells, predict_cell, 0)

    lower = [[None for column in range(5)] for row in range(5)]
    for entry, (row, column) in enumerate(ENTRIES):
        lower[row][column] = factors_ref[entry]
    inverse = [lower[row][row] for row in range(5)]
    answer = cholesky_solve(lower, inverse, [sums[row] for row in range(5)], 5)
    for row in range(5):
        steps[row] = answer[row]
        for cell in range(cells):
            step_ref[row : row + 1, cell * LANES : (cell + 1) * LANES] = answer[row][
                cell : cell + 1
            ]

    def group(cell, index):
        first = pl.multiple_of(index * 8, 8)
        rows = pl.ds(first, 8)
        columns = pl.ds(pl.multiple_of(cell * LANES, LANES), LANES)
        number = first + lax.broadcasted_iota(jnp.int32, (8, LANES), 0)
        live = jnp.where(number < facts[COUNT, cell, 0], 1.0, 0.0)
        fitted = jnp.zeros((8, LANES), jnp.float32)
        for row in range(5):
            step = jnp.broadcast_to(steps[row, pl.ds(cell, 1), :], (8, LANES))
            fitted = fitted + star_ref[row, rows, columns] * step
        second = first_order[rows, columns] - live * fitted
        for m in range(4):
            value = axis_ref[m, rows, columns] * second
            high = value.astype(jnp.bfloat16).astype(jnp.float32)
            weights[pl.ds(m, 8, stride=16), :] = high
            weights[pl.ds(4 + m, 8, stride=16), :] = value - high
        values = spline_basis(phase_ref[rows, columns])
        for order in range(4):
            basis[order] = values[order]
        offsets[...] = offset_ref[rows, columns]
        for j in range(8):
            relative = knots - pair_rows(offsets[pl.ds(j, 1), :])
            piece = jnp.zeros((KB, LANES), jnp.float32)
            for order in range(4):
                value = pair_rows(basis[order, pl.ds(j, 1), :])
                piece = jnp.where(relative == order, value, piece)
            high, low = split(piece)
            weight = weights[pl.ds(j * 16, 16), :]
            right = jnp.where(knots < 4, weight, 0.0)
            result = product(
                jnp.concatenate([weight, right], axis=1).astype(jnp.bfloat16),
                jnp.concatenate([high] * 4, axis=0),
                jnp.concatenate([low] * 4, axis=0),
            )[0:8]
            result = jnp.concatenate([result, result], axis=1)
            for place in (facts[HOME_LANES, cell, first + j], facts[HALO_LANES, cell, first + j]):
                chosen = jnp.where(lanes_block == (place & 7), result, 0.0)
                block = pl.ds(pl.multiple_of((place >> 3) * 8, 8), 8)
                total[block, :] = total[block, :] + chosen

    over_groups(cells, groups, group, UNROLL)

    mine = lax.axis_index(axes) & 1
    half = kept_ref.shape[0] * 2

    def pack(index, carry):
        target = pl.multiple_of(index * 8, 8)
        for out_ref, part in ((kept_ref, mine), (sent_ref, 1 - mine)):
            source = pl.multiple_of(part * half + index * 16, 16)
            for j in range(2):
                tile = total[pl.ds(source + j * 8, 8), :]
                out_ref[pl.ds(target + j * 4, 4), :] = tile[0:4] + tile[4:8]
        return carry

    lax.fori_loop(0, half // 16, pack, 0)


def share_of(axes, group):
    me = lax.axis_index(axes)
    mine = 0
    for bit in group:
        mine = mine * 2 + ((me >> bit) & 1)
    return mine


def add_kernel(axes, group, families, *refs):
    mine = share_of(axes, group)
    members = 1 << len(group)
    outputs = refs[-members:]
    first = 0
    base = 0
    for count, rows in families:
        inputs = refs[first : first + count]
        first += count
        step = 40 if rows % 40 == 0 else rows
        for other, out_ref in enumerate(outputs):
            start = (mine ^ other) * rows

            def add(index, carry, out_ref=out_ref, inputs=inputs, start=start, step=step, base=base):
                source = pl.ds(start + index * step, step)
                added = inputs[0][source, :]
                for ref in inputs[1:]:
                    added = added + ref[source, :]
                out_ref[pl.ds(base + index * step, step), :] = added
                return carry

            if step == rows:
                add(0, 0)
            else:
                lax.fori_loop(0, rows // step, add, 0)
        base += rows


def sweep_kernel(spread, axes, *refs):
    *parts, out_ref, band_ref, band = refs
    added = parts[0][...]
    for part in parts[1:]:
        added = added + part[...]
    band_ref[...] = added
    width = band.shape[2]
    tiles = width // LANES
    lane_block = lax.broadcasted_iota(jnp.int32, (8, LANES), 1) // KB
    filler = jnp.zeros((8 - ROWS, LANES), jnp.float32)
    for half in range(2):
        for shift in range(4):
            start = half * 64 + shift * KB
            for tile in range(tiles):
                merged = jnp.zeros((8, LANES), jnp.float32)
                for place in range(min(8, spread - tile * 8)):
                    block = tile * 8 + place
                    piece = jnp.concatenate(
                        [band_ref[block * ROWS : (block + 1) * ROWS, :], filler], axis=0
                    )
                    moved = (place * KB - start) % LANES
                    if moved:
                        piece = pltpu.roll(piece, moved, axis=1)
                    merged = jnp.where(lane_block == place, piece, merged)
                band[shift, half * 8 : half * 8 + 8, tile * LANES : (tile + 1) * LANES] = merged
    index = {}
    for place, (m, n) in enumerate(PAIRS):
        row = place if place < ROWS else place + 3
        index[(m, n)] = row
        index[(n, m)] = row

    def row_of(shift, m, n):
        return band[shift, index[(m, n)] : index[(m, n)] + 1, :]

    ahead = [
        [jnp.concatenate([row_of(shift, m, n) for n in range(4)], axis=0) for m in range(4)]
        for shift in range(4)
    ]
    behind = [
        [pltpu.roll(ahead[shift][m], shift, axis=1) if shift else None for m in range(4)]
        for shift in range(4)
    ]
    shifted = 2.0 * smoothing + damping
    diagonal = [
        [row_of(0, row, column) + (shifted if row == column else 0.0) for column in range(4)]
        for row in range(4)
    ]
    lower, inverse = cholesky_factor(diagonal, 4)
    gradient = jnp.concatenate(
        [
            band_ref[spread * ROWS + tile * 4 : spread * ROWS + (tile + 1) * 4, :]
            for tile in range(tiles)
        ],
        axis=1,
    )
    lane = lax.broadcasted_iota(jnp.int32, (4, width), 1)
    me = lax.axis_index(axes)
    start = jnp.where(me == 0, KB, 0)
    stop = jnp.where(me == lax.axis_size(axes) - 1, (spread - 1) * KB, spread * KB)
    keep = jnp.where((lane >= start) & (lane < stop), relaxation, 0.0)
    answer = jnp.zeros((4, width), jnp.float32)
    for sweep in range(ITERS):
        misfit = gradient
        if sweep:
            moved = {}
            for shift in range(1, 4):
                moved[shift] = pltpu.roll(answer, width - shift, axis=1)
                moved[-shift] = pltpu.roll(answer, shift, axis=1)
            applied = []
            for m in range(4):
                terms = ahead[0][m] * answer
                for shift in range(1, 4):
                    terms = terms + ahead[shift][m] * moved[shift]
                    terms = terms + behind[shift][m] * moved[-shift]
                applied.append(jnp.sum(terms, axis=0, keepdims=True))
            regular = smoothing * (2.0 * answer - moved[-1] - moved[1]) + damping * answer
            misfit = gradient - regular - jnp.concatenate(applied, axis=0)
        correction = cholesky_solve(lower, inverse, [misfit[m : m + 1] for m in range(4)], 4)
        answer = answer + keep * jnp.concatenate(correction, axis=0)
    out_ref[...] = answer[:, KB : KB + out_ref.shape[1]]


def in_vmem(count):
    return [pl.BlockSpec(memory_space=pltpu.VMEM) for operand in range(count)]


def in_smem(count):
    return [pl.BlockSpec(memory_space=pltpu.SMEM) for operand in range(count)]


def work(microseconds):
    return pl.CostEstimate(flops=0, bytes_accessed=microseconds * 3_600_000, transcendentals=0)


def params(rows=0):
    return pltpu.CompilerParams(vmem_limit_bytes=min(56 << 20, (16 << 20) + 2 * rows * LANES * 4))


def call_facts(counts, attitude, owners, slots, devices):
    shape = (COUNT + 1,) + owners.shape
    return pl.pallas_call(
        functools.partial(facts_kernel, attitude.shape[1] // KB),
        out_shape=[
            jax.ShapeDtypeStruct(shape, jnp.int32),
            jax.ShapeDtypeStruct((devices,) + attitude.shape, jnp.float32),
        ],
        in_specs=in_smem(1) + in_vmem(3),
        out_specs=in_vmem(2),
        compiler_params=pltpu.CompilerParams(vmem_limit_bytes=62 << 20),
        cost_estimate=work(1),
        name="facts",
    )(counts, attitude, owners, slots)


def call_normals(axes, facts, phase, knot_offset, partials, devices, spread):
    f32 = jnp.float32
    half = jax.ShapeDtypeStruct((devices // 2 * spread * ROWS, LANES), f32)
    blocks = devices * spread
    return pl.pallas_call(
        functools.partial(normal_kernel, axes),
        out_shape=[half, half],
        in_specs=in_smem(1) + in_vmem(3),
        out_specs=in_vmem(2),
        scratch_shapes=[
            pltpu.VMEM(((blocks + 1) * 8, LANES), f32),
            pltpu.VMEM((8 * 16, LANES), f32),
            pltpu.VMEM((16, 8, LANES), f32),
            pltpu.VMEM((8, LANES), jnp.int32),
        ],
        compiler_params=params(blocks * 13),
        cost_estimate=work(8),
        name="normals",
    )(facts, phase, knot_offset, partials)


def call_add(axes, group, families):
    members = 1 << len(group)
    rows = sum(count for arrays, count in families)
    out = jax.ShapeDtypeStruct((rows, LANES), jnp.float32)
    arrays = [array for family, count in families for array in family]
    return pl.pallas_call(
        functools.partial(
            add_kernel, axes, group, [(len(family), count) for family, count in families]
        ),
        out_shape=[out] * members,
        in_specs=in_vmem(len(arrays)),
        out_specs=in_vmem(members),
        compiler_params=params(rows * members * 3),
        cost_estimate=work(0),
        name="shares",
    )(*arrays)


def call_factors(facts, star_partials):
    return pl.pallas_call(
        factor_kernel,
        out_shape=jax.ShapeDtypeStruct((len(ENTRIES), 8, LANES), jnp.float32),
        in_specs=in_smem(1) + in_vmem(1),
        out_specs=in_vmem(1)[0],
        scratch_shapes=[pltpu.VMEM((len(ENTRIES), 8, LANES), jnp.float32)],
        compiler_params=params(),
        cost_estimate=work(20),
        name="factors",
    )(facts, star_partials)


def call_stars(
    axes,
    facts,
    attitude,
    factors,
    phase,
    knot_offset,
    partials,
    star_partials,
    observed,
    devices,
    spread,
):
    f32 = jnp.float32
    tiles = (spread + 7) // 8
    transits, stars = phase.shape
    half = jax.ShapeDtypeStruct((devices // 2 * tiles * 4, LANES), f32)
    return pl.pallas_call(
        functools.partial(star_kernel, axes),
        out_shape=[
            jax.ShapeDtypeStruct((5, stars), f32),
            half,
            half,
        ],
        in_specs=in_smem(1) + in_vmem(7),
        out_specs=in_vmem(3),
        scratch_shapes=[
            pltpu.VMEM(((devices + 1) * tiles * 8, LANES), f32),
            pltpu.VMEM((transits // 8, 32, LANES), f32),
            pltpu.VMEM((transits, stars), f32),
            pltpu.VMEM((5, 8, LANES), f32),
            pltpu.VMEM((5, 8, LANES), f32),
            pltpu.VMEM((8 * 16, LANES), f32),
            pltpu.VMEM((4, 8, LANES), f32),
            pltpu.VMEM((8, LANES), jnp.int32),
        ],
        compiler_params=params((devices + 1) * tiles * 12),
        cost_estimate=work(10),
        name="stars",
    )(
        facts,
        attitude,
        factors,
        phase,
        knot_offset,
        partials,
        star_partials,
        observed,
    )


def swap(arrays, group, axes, devices):
    arrived = []
    for other, array in enumerate(arrays, start=1):
        mask = sum(1 << bit for place, bit in enumerate(reversed(group)) if (other >> place) & 1)
        arrived.append(lax.ppermute(array, axes, [(i, i ^ mask) for i in range(devices)]))
    return arrived


def per_device(
    attitude,
    star_partials,
    attitude_partials,
    observed,
    phase,
    knot_offset,
    cell_counts,
    interval_owner,
    block_slot,
):
    axes = ("cells", "tm")
    devices = lax.axis_size("cells") * lax.axis_size("tm")
    levels = devices.bit_length() - 1
    cells = cell_counts.shape[0]
    transits = observed.shape[0]
    blocks = attitude.shape[1] // KB
    spread = blocks + 2
    tiles = (spread + 7) // 8
    width = tiles * LANES

    owners = interval_owner.reshape(cells, transits)
    facts, wide = call_facts(cell_counts, attitude, owners, block_slot, devices)
    whole = lax.all_to_all(wide, axes, split_axis=0, concat_axis=0, tiled=True)
    bits = list(range(devices.bit_length() - 1))
    groups = [bits[:1]] + [bits[start : start + 2] for start in range(1, len(bits), 2)]
    last = len(groups) - 1
    left = [devices >> (group[-1] + 1) for group in groups]
    chunks = (spread * ROWS, tiles * 4)

    def advance(arrays, chunk, index):
        kept, *sent = call_add(axes, groups[index], [(arrays, chunk * left[index])])
        return [kept] + swap(sent, groups[index], axes, devices)

    factors = call_factors(facts, star_partials)
    facts, factors = lax.optimization_barrier((facts, factors))
    kept, sent = call_normals(
        axes, facts, phase, knot_offset, attitude_partials, devices, spread
    )
    kept, sent, whole = lax.optimization_barrier((kept, sent, whole))
    normals = [kept] + swap([sent], groups[0], axes, devices)
    *normals, whole = lax.optimization_barrier((*normals, whole))
    star_step, kept, sent = call_stars(
        axes,
        facts,
        whole,
        factors,
        phase,
        knot_offset,
        attitude_partials,
        star_partials,
        observed,
        devices,
        spread,
    )
    normals = advance(normals, chunks[0], 1)
    *normals, kept, sent = lax.optimization_barrier((*normals, kept, sent))
    for index in range(2, last):
        normals = advance(normals, chunks[0], index)
    gradients = [kept] + swap([sent], groups[0], axes, devices)
    for index in range(1, last):
        gradients = advance(gradients, chunks[1], index)
    families = [(normals, chunks[0] * left[last]), (gradients, chunks[1] * left[last])]
    kept, *sent = call_add(axes, groups[last], families)
    parts = [kept] + swap(sent, groups[last], axes, devices)
    attitude_step = pl.pallas_call(
        functools.partial(sweep_kernel, spread, axes),
        out_shape=jax.ShapeDtypeStruct((4, blocks * KB), jnp.float32),
        in_specs=in_vmem(len(parts)),
        out_specs=in_vmem(1)[0],
        scratch_shapes=[
            pltpu.VMEM(kept.shape, jnp.float32),
            pltpu.VMEM((4, 16, width), jnp.float32),
        ],
        compiler_params=params(),
        cost_estimate=work(2),
        name="sweeps",
    )(*parts)
    return (star_step, attitude_step)


def solution(mesh):
    split_axes = ("cells", "tm")
    placed = (
        P(None, split_axes),
        P(None, None, split_axes),
        P(None, None, split_axes),
        P(None, split_axes),
        P(None, split_axes),
        P(None, split_axes),
        P(split_axes),
        P(split_axes, None, None),
        P(split_axes, None),
    )
    return jax.shard_map(
        per_device,
        mesh=mesh,
        in_specs=placed,
        out_specs=(P(None, split_axes), P(None, split_axes)),
        check_vma=False,
    )
```

```python
import functools

import jax
import jax.numpy as jnp
from jax import lax
from jax.experimental import pallas as pl
from jax.experimental.pallas import tpu as pltpu
from jax.sharding import PartitionSpec as P

CS = 128
KB = 16
ITERS = 6
LANES = 128
PAIRS = tuple((m, n) for m in range(4) for n in range(m, 4))
HOME, HALO, HOME_LANES, HALO_LANES, OWNER, SLOT, COUNT = range(7)
ROWS = 5
UNROLL = 8

smoothing = 16.0
damping = 2.0
relaxation = 0.5
star_prior = 1.0


def spline_basis(phase):
    square = phase * phase
    cube = square * phase
    rest = 1.0 - phase
    return (
        rest * rest * rest * (1.0 / 6.0),
        (3.0 * cube - 6.0 * square + 4.0) * (1.0 / 6.0),
        (-3.0 * cube + 3.0 * square + 3.0 * phase + 1.0) * (1.0 / 6.0),
        cube * (1.0 / 6.0),
    )


def cholesky_factor(matrix, size):
    lower = [[None for column in range(size)] for row in range(size)]
    inverse = [None for column in range(size)]
    for column in range(size):
        total = matrix[column][column]
        for inner in range(column):
            total = total - lower[column][inner] * lower[column][inner]
        inverse[column] = 1.0 / jnp.sqrt(total)
        for row in range(column + 1, size):
            accum = matrix[row][column]
            for inner in range(column):
                accum = accum - lower[row][inner] * lower[column][inner]
            lower[row][column] = accum * inverse[column]
    return lower, inverse


def cholesky_solve(lower, inverse, rhs, size):
    forward = []
    for row in range(size):
        accum = rhs[row]
        for inner in range(row):
            accum = accum - lower[row][inner] * forward[inner]
        forward.append(accum * inverse[row])
    answer = [None for row in range(size)]
    for row in reversed(range(size)):
        accum = forward[row]
        for inner in range(row + 1, size):
            accum = accum - lower[inner][row] * answer[inner]
        answer[row] = accum * inverse[row]
    return answer


def split(value):
    high = value.astype(jnp.bfloat16)
    low = (value - high.astype(jnp.float32)).astype(jnp.bfloat16)
    return high, low


def over_groups(cells, groups, body, unroll):
    def cell_body(cell, carry):
        def group_body(index, inner):
            body(cell, index)
            return inner

        return lax.fori_loop(0, groups, group_body, carry, unroll=unroll)

    lax.fori_loop(0, cells, cell_body, 0)


def pair_rows(value):
    return jnp.broadcast_to(value, (KB, LANES))


def product(weights, matrix_high, matrix_low):
    return lax.dot_general(
        weights,
        jnp.concatenate([matrix_high, matrix_low], axis=1),
        (((1,), (1,)), ((), ())),
        preferred_element_type=jnp.float32,
    )


def facts_kernel(blocks, counts, attitude_ref, owners_ref, slots_ref, facts_ref, wide_ref):
    devices = wide_ref.shape[0]
    levels = devices.bit_length() - 1
    spread = blocks + 2
    lanes = (spread + 7) // 8 * 8
    owners = owners_ref[...]
    slots = slots_ref[...]
    cells = owners.shape[0]

    def reverse(owner):
        reversed_bits = jnp.zeros_like(owner)
        for bit in range(levels):
            reversed_bits = reversed_bits | (((owner >> bit) & 1) << (levels - 1 - bit))
        return reversed_bits

    first = slots == 0
    final = slots == blocks - 1
    neighbour = owners + jnp.where(first, -1, jnp.where(final, 1, 0))
    nowhere = (neighbour == owners) | (neighbour < 0) | (neighbour >= devices)
    home_owner = reverse(owners)
    halo_owner = jnp.where(nowhere, devices, reverse(neighbour))
    home_place = slots + 1
    halo_place = jnp.where(first & ~nowhere, spread - 1, 0)
    facts_ref[HOME] = home_owner * spread + home_place
    facts_ref[HALO] = halo_owner * spread + halo_place
    facts_ref[HOME_LANES] = home_owner * lanes + home_place
    facts_ref[HALO_LANES] = halo_owner * lanes + halo_place
    facts_ref[OWNER] = owners
    facts_ref[SLOT] = slots
    for cell in range(cells):
        facts_ref[COUNT, cell : cell + 1, :] = jnp.full((1, owners.shape[1]), counts[cell], jnp.int32)
    attitude = attitude_ref[...]

    def copy(index, carry):
        wide_ref[index] = attitude
        return carry

    lax.fori_loop(0, devices, copy, 0, unroll=8)


def normal_kernel(
    axes,
    facts,
    phase_ref,
    offset_ref,
    axis_ref,
    kept_ref,
    sent_ref,
    total,
    weights,
    basis,
    offsets,
):
    transits, stars = phase_ref.shape
    cells = stars // LANES
    knots = lax.broadcasted_iota(jnp.int32, (KB, LANES), 0)
    total[...] = jnp.zeros_like(total)
    weights[...] = jnp.zeros_like(weights)
    groups = transits // 8

    def group(cell, index):
        first = pl.multiple_of(index * 8, 8)
        rows = pl.ds(first, 8)
        columns = pl.ds(pl.multiple_of(cell * LANES, LANES), LANES)
        number = first + lax.broadcasted_iota(jnp.int32, (8, LANES), 0)
        live = jnp.where(number < facts[COUNT, cell, 0], 1.0, 0.0)
        values = spline_basis(phase_ref[rows, columns])
        for shift in range(4):
            for order in range(4 - shift):
                basis[shift * 4 + order] = values[order] * values[order + shift]
        offsets[...] = offset_ref[rows, columns]
        parts = [axis_ref[m, rows, columns] for m in range(4)]
        lively = [part * live for part in parts]
        for place, (m, n) in enumerate(PAIRS):
            row = place if place < ROWS else place + 3
            weights[pl.ds(row, 8, stride=16), :] = lively[m] * parts[n]
        for j in range(8):
            relative = knots - pair_rows(offsets[pl.ds(j, 1), :])
            hits = [relative == order for order in range(4)]
            highs, lows = [], []
            for shift in range(4):
                piece = jnp.zeros((KB, LANES), jnp.float32)
                for order in range(4 - shift):
                    value = pair_rows(basis[shift * 4 + order, pl.ds(j, 1), :])
                    piece = jnp.where(hits[order], value, piece)
                high, low = split(piece)
                highs.append(high)
                lows.append(low)
            weight_high, weight_low = split(weights[pl.ds(j * 16, 16), :])
            left = jnp.concatenate([weight_high, weight_low], axis=0)
            right = jnp.concatenate([weight_high, jnp.zeros_like(weight_low)], axis=0)
            result = product(
                jnp.concatenate([left, right], axis=1),
                jnp.concatenate(highs, axis=0),
                jnp.concatenate(lows, axis=0),
            )
            band = jnp.concatenate(
                [result[0:8] + result[16:24], result[8:16] + result[24:32]], axis=1
            )
            for place in (facts[HOME, cell, first + j], facts[HALO, cell, first + j]):
                block = pl.ds(pl.multiple_of(place * 8, 8), 8)
                total[block, :] = total[block, :] + band

    over_groups(cells, groups, group, UNROLL)

    mine = lax.axis_index(axes) & 1
    half = kept_ref.shape[0] // ROWS * 8

    def pack(index, carry):
        target = pl.multiple_of(index * 8 * ROWS, 8)
        for out_ref, part in ((kept_ref, mine), (sent_ref, 1 - mine)):
            source = pl.multiple_of(part * half + index * 64, 64)
            for j in range(8):
                out_ref[pl.ds(target + j * ROWS, ROWS), :] = total[pl.ds(source + j * 8, ROWS), :]
        return carry

    lax.fori_loop(0, half // 64, pack, 0)


ENTRIES = tuple((row, column) for row in range(5) for column in range(row + 1))


def factor_kernel(facts, star_ref, factors_ref, sums):
    transits, stars = star_ref.shape[1:]
    sums[...] = jnp.zeros_like(sums)

    def cell_body(cell, carry):
        columns = pl.ds(pl.multiple_of(cell * LANES, LANES), LANES)

        def add(index, accumulated):
            first = pl.multiple_of(index * 8, 8)
            number = first + lax.broadcasted_iota(jnp.int32, (8, LANES), 0)
            live = jnp.where(number < facts[COUNT, cell, 0], 1.0, 0.0)
            parts = [star_ref[row, pl.ds(first, 8), columns] for row in range(5)]
            lively = [part * live for part in parts]
            return tuple(
                old + lively[row] * parts[column] for old, (row, column) in zip(accumulated, ENTRIES)
            )

        start = tuple(jnp.zeros((8, LANES), jnp.float32) for entry in ENTRIES)
        accumulated = lax.fori_loop(0, transits // 8, add, start, unroll=4)
        for entry in range(len(ENTRIES)):
            sums[entry, pl.ds(cell, 1), :] = jnp.sum(accumulated[entry], axis=0, keepdims=True)
        return carry

    lax.fori_loop(0, stars // LANES, cell_body, 0)
    normal = [[None for column in range(5)] for row in range(5)]
    for entry, (row, column) in enumerate(ENTRIES):
        normal[row][column] = sums[entry] + (star_prior if row == column else 0.0)
    lower, inverse = cholesky_factor(normal, 5)
    for entry, (row, column) in enumerate(ENTRIES):
        factors_ref[entry] = inverse[row] if row == column else lower[row][column]


def star_kernel(
    axes,
    facts,
    attitude_ref,
    factors_ref,
    phase_ref,
    offset_ref,
    axis_ref,
    star_ref,
    observed_ref,
    step_ref,
    kept_ref,
    sent_ref,
    total,
    table,
    first_order,
    sums,
    steps,
    weights,
    basis,
    offsets,
):
    transits, stars = phase_ref.shape
    cells = stars // LANES
    groups = transits // 8
    knots = lax.broadcasted_iota(jnp.int32, (KB, LANES), 0)
    lanes_block = lax.broadcasted_iota(jnp.int32, (8, LANES), 1) // KB
    total[...] = jnp.zeros_like(total)
    weights[...] = jnp.zeros_like(weights)
    sums[...] = jnp.zeros_like(sums)
    sublane = lax.broadcasted_iota(jnp.int32, (8, LANES), 0)

    def predict_cell(cell, carry):
        columns = pl.ds(pl.multiple_of(cell * LANES, LANES), LANES)

        def predict(index, accumulated):
            first = pl.multiple_of(index * 8, 8)
            rows = pl.ds(first, 8)
            shift = jnp.zeros((8, LANES), jnp.int32)
            for j in range(8):
                owner = facts[OWNER, cell, first + j]
                slot = facts[SLOT, cell, first + j]
                column = pl.multiple_of((slot >> 3) * LANES, LANES)
                table[index, pl.ds(j, 4, stride=8), :] = attitude_ref[owner, :, pl.ds(column, LANES)]
                shift = jnp.where(sublane == j, (slot & 7) * KB, shift)
            number = first + lax.broadcasted_iota(jnp.int32, (8, LANES), 0)
            live = jnp.where(number < facts[COUNT, cell, 0], 1.0, 0.0)
            values = spline_basis(phase_ref[rows, columns])
            offset = offset_ref[rows, columns] + shift
            places = [offset + order for order in range(4)]
            predicted = jnp.zeros((8, LANES), jnp.float32)
            for m in range(4):
                spline = jnp.zeros((8, LANES), jnp.float32)
                looked = table[index, m * 8 : m * 8 + 8, :]
                for order in range(4):
                    found = jnp.take_along_axis(looked, places[order], axis=1)
                    spline = spline + found * values[order]
                predicted = predicted + spline * axis_ref[m, rows, columns]
            first_value = live * (observed_ref[rows, columns] - predicted)
            first_order[rows, columns] = first_value
            parts = [star_ref[row, rows, columns] for row in range(5)]
            return tuple(old + part * first_value for old, part in zip(accumulated, parts))

        start = tuple(jnp.zeros((8, LANES), jnp.float32) for row in range(5))
        accumulated = lax.fori_loop(0, groups, predict, start, unroll=8)
        for entry in range(5):
            sums[entry, pl.ds(cell, 1), :] = jnp.sum(accumulated[entry], axis=0, keepdims=True)
        return carry

    lax.fori_loop(0, cells, predict_cell, 0)

    lower = [[None for column in range(5)] for row in range(5)]
    for entry, (row, column) in enumerate(ENTRIES):
        lower[row][column] = factors_ref[entry]
    inverse = [lower[row][row] for row in range(5)]
    answer = cholesky_solve(lower, inverse, [sums[row] for row in range(5)], 5)
    for row in range(5):
        steps[row] = answer[row]
        for cell in range(cells):
            step_ref[row : row + 1, cell * LANES : (cell + 1) * LANES] = answer[row][
                cell : cell + 1
            ]

    def group(cell, index):
        first = pl.multiple_of(index * 8, 8)
        rows = pl.ds(first, 8)
        columns = pl.ds(pl.multiple_of(cell * LANES, LANES), LANES)
        number = first + lax.broadcasted_iota(jnp.int32, (8, LANES), 0)
        live = jnp.where(number < facts[COUNT, cell, 0], 1.0, 0.0)
        fitted = jnp.zeros((8, LANES), jnp.float32)
        for row in range(5):
            step = jnp.broadcast_to(steps[row, pl.ds(cell, 1), :], (8, LANES))
            fitted = fitted + star_ref[row, rows, columns] * step
        second = first_order[rows, columns] - live * fitted
        for m in range(4):
            value = axis_ref[m, rows, columns] * second
            high = value.astype(jnp.bfloat16).astype(jnp.float32)
            weights[pl.ds(m, 8, stride=16), :] = high
            weights[pl.ds(4 + m, 8, stride=16), :] = value - high
        values = spline_basis(phase_ref[rows, columns])
        for order in range(4):
            basis[order] = values[order]
        offsets[...] = offset_ref[rows, columns]
        for j in range(8):
            relative = knots - pair_rows(offsets[pl.ds(j, 1), :])
            piece = jnp.zeros((KB, LANES), jnp.float32)
            for order in range(4):
                value = pair_rows(basis[order, pl.ds(j, 1), :])
                piece = jnp.where(relative == order, value, piece)
            high, low = split(piece)
            weight = weights[pl.ds(j * 16, 16), :]
            right = jnp.where(knots < 4, weight, 0.0)
            result = product(
                jnp.concatenate([weight, right], axis=1).astype(jnp.bfloat16),
                jnp.concatenate([high] * 4, axis=0),
                jnp.concatenate([low] * 4, axis=0),
            )[0:8]
            result = jnp.concatenate([result, result], axis=1)
            for place in (facts[HOME_LANES, cell, first + j], facts[HALO_LANES, cell, first + j]):
                chosen = jnp.where(lanes_block == (place & 7), result, 0.0)
                block = pl.ds(pl.multiple_of((place >> 3) * 8, 8), 8)
                total[block, :] = total[block, :] + chosen

    over_groups(cells, groups, group, UNROLL)

    mine = lax.axis_index(axes) & 1
    half = kept_ref.shape[0] * 2

    def pack(index, carry):
        target = pl.multiple_of(index * 8, 8)
        for out_ref, part in ((kept_ref, mine), (sent_ref, 1 - mine)):
            source = pl.multiple_of(part * half + index * 16, 16)
            for j in range(2):
                tile = total[pl.ds(source + j * 8, 8), :]
                out_ref[pl.ds(target + j * 4, 4), :] = tile[0:4] + tile[4:8]
        return carry

    lax.fori_loop(0, half // 16, pack, 0)


def share_of(axes, group):
    me = lax.axis_index(axes)
    mine = 0
    for bit in group:
        mine = mine * 2 + ((me >> bit) & 1)
    return mine


def add_kernel(axes, group, families, *refs):
    mine = share_of(axes, group)
    members = 1 << len(group)
    outputs = refs[-members:]
    first = 0
    base = 0
    for count, rows in families:
        inputs = refs[first : first + count]
        first += count
        step = 40 if rows % 40 == 0 else rows
        for other, out_ref in enumerate(outputs):
            start = (mine ^ other) * rows

            def add(index, carry, out_ref=out_ref, inputs=inputs, start=start, step=step, base=base):
                source = pl.ds(start + index * step, step)
                added = inputs[0][source, :]
                for ref in inputs[1:]:
                    added = added + ref[source, :]
                out_ref[pl.ds(base + index * step, step), :] = added
                return carry

            if step == rows:
                add(0, 0)
            else:
                lax.fori_loop(0, rows // step, add, 0)
        base += rows


def sweep_kernel(spread, axes, *refs):
    *parts, out_ref, band_ref, band = refs
    added = parts[0][...]
    for part in parts[1:]:
        added = added + part[...]
    band_ref[...] = added
    width = band.shape[2]
    tiles = width // LANES
    lane_block = lax.broadcasted_iota(jnp.int32, (8, LANES), 1) // KB
    filler = jnp.zeros((8 - ROWS, LANES), jnp.float32)
    for half in range(2):
        for shift in range(4):
            start = half * 64 + shift * KB
            for tile in range(tiles):
                merged = jnp.zeros((8, LANES), jnp.float32)
                for place in range(min(8, spread - tile * 8)):
                    block = tile * 8 + place
                    piece = jnp.concatenate(
                        [band_ref[block * ROWS : (block + 1) * ROWS, :], filler], axis=0
                    )
                    moved = (place * KB - start) % LANES
                    if moved:
                        piece = pltpu.roll(piece, moved, axis=1)
                    merged = jnp.where(lane_block == place, piece, merged)
                band[shift, half * 8 : half * 8 + 8, tile * LANES : (tile + 1) * LANES] = merged
    index = {}
    for place, (m, n) in enumerate(PAIRS):
        row = place if place < ROWS else place + 3
        index[(m, n)] = row
        index[(n, m)] = row

    def row_of(shift, m, n):
        return band[shift, index[(m, n)] : index[(m, n)] + 1, :]

    ahead = [
        [jnp.concatenate([row_of(shift, m, n) for n in range(4)], axis=0) for m in range(4)]
        for shift in range(4)
    ]
    behind = [
        [pltpu.roll(ahead[shift][m], shift, axis=1) if shift else None for m in range(4)]
        for shift in range(4)
    ]
    shifted = 2.0 * smoothing + damping
    diagonal = [
        [row_of(0, row, column) + (shifted if row == column else 0.0) for column in range(4)]
        for row in range(4)
    ]
    lower, inverse = cholesky_factor(diagonal, 4)
    gradient = jnp.concatenate(
        [
            band_ref[spread * ROWS + tile * 4 : spread * ROWS + (tile + 1) * 4, :]
            for tile in range(tiles)
        ],
        axis=1,
    )
    lane = lax.broadcasted_iota(jnp.int32, (4, width), 1)
    me = lax.axis_index(axes)
    start = jnp.where(me == 0, KB, 0)
    stop = jnp.where(me == lax.axis_size(axes) - 1, (spread - 1) * KB, spread * KB)
    keep = jnp.where((lane >= start) & (lane < stop), relaxation, 0.0)
    answer = jnp.zeros((4, width), jnp.float32)
    for sweep in range(ITERS):
        misfit = gradient
        if sweep:
            moved = {}
            for shift in range(1, 4):
                moved[shift] = pltpu.roll(answer, width - shift, axis=1)
                moved[-shift] = pltpu.roll(answer, shift, axis=1)
            applied = []
            for m in range(4):
                terms = ahead[0][m] * answer
                for shift in range(1, 4):
                    terms = terms + ahead[shift][m] * moved[shift]
                    terms = terms + behind[shift][m] * moved[-shift]
                applied.append(jnp.sum(terms, axis=0, keepdims=True))
            regular = smoothing * (2.0 * answer - moved[-1] - moved[1]) + damping * answer
            misfit = gradient - regular - jnp.concatenate(applied, axis=0)
        correction = cholesky_solve(lower, inverse, [misfit[m : m + 1] for m in range(4)], 4)
        answer = answer + keep * jnp.concatenate(correction, axis=0)
    out_ref[...] = answer[:, KB : KB + out_ref.shape[1]]


def in_vmem(count):
    return [pl.BlockSpec(memory_space=pltpu.VMEM) for operand in range(count)]


def in_smem(count):
    return [pl.BlockSpec(memory_space=pltpu.SMEM) for operand in range(count)]


def work(microseconds):
    return pl.CostEstimate(flops=0, bytes_accessed=microseconds * 3_600_000, transcendentals=0)


def params(rows=0):
    return pltpu.CompilerParams(vmem_limit_bytes=min(56 << 20, (16 << 20) + 2 * rows * LANES * 4))


def call_facts(counts, attitude, owners, slots, devices):
    shape = (COUNT + 1,) + owners.shape
    return pl.pallas_call(
        functools.partial(facts_kernel, attitude.shape[1] // KB),
        out_shape=[
            jax.ShapeDtypeStruct(shape, jnp.int32),
            jax.ShapeDtypeStruct((devices,) + attitude.shape, jnp.float32),
        ],
        in_specs=in_smem(1) + in_vmem(3),
        out_specs=in_vmem(2),
        compiler_params=pltpu.CompilerParams(vmem_limit_bytes=62 << 20),
        cost_estimate=work(1),
        name="facts",
    )(counts, attitude, owners, slots)


def call_normals(axes, facts, phase, knot_offset, partials, devices, spread):
    f32 = jnp.float32
    half = jax.ShapeDtypeStruct((devices // 2 * spread * ROWS, LANES), f32)
    blocks = devices * spread
    return pl.pallas_call(
        functools.partial(normal_kernel, axes),
        out_shape=[half, half],
        in_specs=in_smem(1) + in_vmem(3),
        out_specs=in_vmem(2),
        scratch_shapes=[
            pltpu.VMEM(((blocks + 1) * 8, LANES), f32),
            pltpu.VMEM((8 * 16, LANES), f32),
            pltpu.VMEM((16, 8, LANES), f32),
            pltpu.VMEM((8, LANES), jnp.int32),
        ],
        compiler_params=params(blocks * 13),
        cost_estimate=work(8),
        name="normals",
    )(facts, phase, knot_offset, partials)


def call_add(axes, group, families):
    members = 1 << len(group)
    rows = sum(count for arrays, count in families)
    out = jax.ShapeDtypeStruct((rows, LANES), jnp.float32)
    arrays = [array for family, count in families for array in family]
    return pl.pallas_call(
        functools.partial(
            add_kernel, axes, group, [(len(family), count) for family, count in families]
        ),
        out_shape=[out] * members,
        in_specs=in_vmem(len(arrays)),
        out_specs=in_vmem(members),
        compiler_params=params(rows * members * 3),
        cost_estimate=work(0),
        name="shares",
    )(*arrays)


def call_factors(facts, star_partials):
    return pl.pallas_call(
        factor_kernel,
        out_shape=jax.ShapeDtypeStruct((len(ENTRIES), 8, LANES), jnp.float32),
        in_specs=in_smem(1) + in_vmem(1),
        out_specs=in_vmem(1)[0],
        scratch_shapes=[pltpu.VMEM((len(ENTRIES), 8, LANES), jnp.float32)],
        compiler_params=params(),
        cost_estimate=work(20),
        name="factors",
    )(facts, star_partials)


def call_stars(
    axes,
    facts,
    attitude,
    factors,
    phase,
    knot_offset,
    partials,
    star_partials,
    observed,
    devices,
    spread,
):
    f32 = jnp.float32
    tiles = (spread + 7) // 8
    transits, stars = phase.shape
    half = jax.ShapeDtypeStruct((devices // 2 * tiles * 4, LANES), f32)
    return pl.pallas_call(
        functools.partial(star_kernel, axes),
        out_shape=[
            jax.ShapeDtypeStruct((5, stars), f32),
            half,
            half,
        ],
        in_specs=in_smem(1) + in_vmem(7),
        out_specs=in_vmem(3),
        scratch_shapes=[
            pltpu.VMEM(((devices + 1) * tiles * 8, LANES), f32),
            pltpu.VMEM((transits // 8, 32, LANES), f32),
            pltpu.VMEM((transits, stars), f32),
            pltpu.VMEM((5, 8, LANES), f32),
            pltpu.VMEM((5, 8, LANES), f32),
            pltpu.VMEM((8 * 16, LANES), f32),
            pltpu.VMEM((4, 8, LANES), f32),
            pltpu.VMEM((8, LANES), jnp.int32),
        ],
        compiler_params=params((devices + 1) * tiles * 12),
        cost_estimate=work(10),
        name="stars",
    )(
        facts,
        attitude,
        factors,
        phase,
        knot_offset,
        partials,
        star_partials,
        observed,
    )


def swap(arrays, group, axes, devices):
    arrived = []
    for other, array in enumerate(arrays, start=1):
        mask = sum(1 << bit for place, bit in enumerate(reversed(group)) if (other >> place) & 1)
        arrived.append(lax.ppermute(array, axes, [(i, i ^ mask) for i in range(devices)]))
    return arrived


def per_device(
    attitude,
    star_partials,
    attitude_partials,
    observed,
    phase,
    knot_offset,
    cell_counts,
    interval_owner,
    block_slot,
):
    axes = ("cells", "tm")
    devices = lax.axis_size("cells") * lax.axis_size("tm")
    levels = devices.bit_length() - 1
    cells = cell_counts.shape[0]
    transits = observed.shape[0]
    blocks = attitude.shape[1] // KB
    spread = blocks + 2
    tiles = (spread + 7) // 8
    width = tiles * LANES

    owners = interval_owner.reshape(cells, transits)
    facts, wide = call_facts(cell_counts, attitude, owners, block_slot, devices)
    whole = lax.all_to_all(wide, axes, split_axis=0, concat_axis=0, tiled=True)
    bits = list(range(devices.bit_length() - 1))
    pairs = [bits[start : start + 2] for start in range(3, len(bits), 2)]
    groups = [bits[:1], bits[1:3]] + pairs
    band_groups = [bits[:1], bits[1:2], bits[2:3]] + pairs
    chunks = (spread * ROWS, tiles * 4)

    def rows(kind, group):
        return chunks[kind] * (devices >> (group[-1] + 1))

    def share(arrays, kind, group):
        return call_add(axes, group, [(arrays, rows(kind, group))])

    def advance(arrays, kind, group):
        kept, *sent = share(arrays, kind, group)
        return [kept] + swap(sent, group, axes, devices)

    factors = call_factors(facts, star_partials)
    facts, factors = lax.optimization_barrier((facts, factors))
    kept, sent = call_normals(
        axes, facts, phase, knot_offset, attitude_partials, devices, spread
    )
    kept, sent, whole = lax.optimization_barrier((kept, sent, whole))
    normals = [kept] + swap([sent], band_groups[0], axes, devices)
    kept, *sent = share(normals, 0, band_groups[1])
    facts, whole, kept, *sent = lax.optimization_barrier((facts, whole, kept, *sent))
    normals = [kept] + swap(sent, band_groups[1], axes, devices)
    star_step, kept, sent = call_stars(
        axes,
        facts,
        whole,
        factors,
        phase,
        knot_offset,
        attitude_partials,
        star_partials,
        observed,
        devices,
        spread,
    )
    gradients = [kept] + swap([sent], groups[0], axes, devices)
    count = len(normals)
    both = lax.optimization_barrier((*normals, *gradients))
    normals, gradients = both[:count], both[count:]
    for group in band_groups[2:-1]:
        normals = advance(normals, 0, group)
    for group in groups[1:-1]:
        gradients = advance(gradients, 1, group)
    final = groups[-1]
    families = [(normals, rows(0, final)), (gradients, rows(1, final))]
    kept, *sent = call_add(axes, final, families)
    parts = [kept] + swap(sent, final, axes, devices)
    attitude_step = pl.pallas_call(
        functools.partial(sweep_kernel, spread, axes),
        out_shape=jax.ShapeDtypeStruct((4, blocks * KB), jnp.float32),
        in_specs=in_vmem(len(parts)),
        out_specs=in_vmem(1)[0],
        scratch_shapes=[
            pltpu.VMEM(kept.shape, jnp.float32),
            pltpu.VMEM((4, 16, width), jnp.float32),
        ],
        compiler_params=params(),
        cost_estimate=work(2),
        name="sweeps",
    )(*parts)
    return (star_step, attitude_step)


def solution(mesh):
    split_axes = ("cells", "tm")
    placed = (
        P(None, split_axes),
        P(None, None, split_axes),
        P(None, None, split_axes),
        P(None, split_axes),
        P(None, split_axes),
        P(None, split_axes),
        P(split_axes),
        P(split_axes, None, None),
        P(split_axes, None),
    )
    return jax.shard_map(
        per_device,
        mesh=mesh,
        in_specs=placed,
        out_specs=(P(None, split_axes), P(None, split_axes)),
        check_vma=False,
    )
```

```python
import functools

import jax
import jax.numpy as jnp
from jax import lax
from jax.experimental import pallas as pl
from jax.experimental.pallas import tpu as pltpu
from jax.sharding import PartitionSpec as P

CS = 128
KB = 16
ITERS = 6
LANES = 128
PAIRS = tuple((m, n) for m in range(4) for n in range(m, 4))
HOME, HALO, HOME_LANES, HALO_LANES, OWNER, SLOT, COUNT = range(7)
ROWS = 5
UNROLL = 8

smoothing = 16.0
damping = 2.0
relaxation = 0.5
star_prior = 1.0


def spline_basis(phase):
    square = phase * phase
    cube = square * phase
    rest = 1.0 - phase
    return (
        rest * rest * rest * (1.0 / 6.0),
        (3.0 * cube - 6.0 * square + 4.0) * (1.0 / 6.0),
        (-3.0 * cube + 3.0 * square + 3.0 * phase + 1.0) * (1.0 / 6.0),
        cube * (1.0 / 6.0),
    )


def cholesky_factor(matrix, size):
    lower = [[None for column in range(size)] for row in range(size)]
    inverse = [None for column in range(size)]
    for column in range(size):
        total = matrix[column][column]
        for inner in range(column):
            total = total - lower[column][inner] * lower[column][inner]
        inverse[column] = 1.0 / jnp.sqrt(total)
        for row in range(column + 1, size):
            accum = matrix[row][column]
            for inner in range(column):
                accum = accum - lower[row][inner] * lower[column][inner]
            lower[row][column] = accum * inverse[column]
    return lower, inverse


def cholesky_solve(lower, inverse, rhs, size):
    forward = []
    for row in range(size):
        accum = rhs[row]
        for inner in range(row):
            accum = accum - lower[row][inner] * forward[inner]
        forward.append(accum * inverse[row])
    answer = [None for row in range(size)]
    for row in reversed(range(size)):
        accum = forward[row]
        for inner in range(row + 1, size):
            accum = accum - lower[inner][row] * answer[inner]
        answer[row] = accum * inverse[row]
    return answer


def split(value):
    high = value.astype(jnp.bfloat16)
    low = (value - high.astype(jnp.float32)).astype(jnp.bfloat16)
    return high, low


def over_groups(cells, groups, body):
    def cell_body(cell, carry):
        def some(index, inner):
            for slot in range(UNROLL):
                body(cell, index * UNROLL + slot, slot)
            return inner

        return lax.fori_loop(0, groups // UNROLL, some, carry)

    lax.fori_loop(0, cells, cell_body, 0)


def pair_rows(value):
    return jnp.broadcast_to(value, (KB, LANES))


def product(weights, matrix_high, matrix_low):
    return lax.dot_general(
        weights,
        jnp.concatenate([matrix_high, matrix_low], axis=1),
        (((1,), (1,)), ((), ())),
        preferred_element_type=jnp.float32,
    )


def facts_kernel(blocks, counts, attitude_ref, owners_ref, slots_ref, facts_ref, wide_ref):
    devices = wide_ref.shape[0]
    levels = devices.bit_length() - 1
    spread = blocks + 2
    lanes = (spread + 7) // 8 * 8
    owners = owners_ref[...]
    slots = slots_ref[...]
    cells = owners.shape[0]

    def reverse(owner):
        reversed_bits = jnp.zeros_like(owner)
        for bit in range(levels):
            reversed_bits = reversed_bits | (((owner >> bit) & 1) << (levels - 1 - bit))
        return reversed_bits

    def reverse_band(owner):
        bits = [(owner >> bit) & 1 for bit in range(levels)]
        swapped = bits[0] != bits[3]
        order = [bits[0], bits[3], jnp.where(swapped, bits[2], bits[1])]
        order += [jnp.where(swapped, bits[1], bits[2])] + bits[4:]
        place = jnp.zeros_like(owner)
        for bit in order:
            place = place * 2 + bit
        return place

    first = slots == 0
    final = slots == blocks - 1
    neighbour = owners + jnp.where(first, -1, jnp.where(final, 1, 0))
    nowhere = (neighbour == owners) | (neighbour < 0) | (neighbour >= devices)
    home_owner = reverse(owners)
    halo_owner = jnp.where(nowhere, devices, reverse(neighbour))
    home_band = reverse_band(owners)
    halo_band = jnp.where(nowhere, devices, reverse_band(neighbour))
    home_place = slots + 1
    halo_place = jnp.where(first & ~nowhere, spread - 1, 0)
    facts_ref[HOME] = home_band * spread + home_place
    facts_ref[HALO] = halo_band * spread + halo_place
    facts_ref[HOME_LANES] = home_owner * lanes + home_place
    facts_ref[HALO_LANES] = halo_owner * lanes + halo_place
    facts_ref[OWNER] = owners
    facts_ref[SLOT] = slots
    for cell in range(cells):
        facts_ref[COUNT, cell : cell + 1, :] = jnp.full((1, owners.shape[1]), counts[cell], jnp.int32)
    attitude = attitude_ref[...]

    def copy(index, carry):
        wide_ref[index] = attitude
        return carry

    lax.fori_loop(0, devices, copy, 0, unroll=8)


def clear_kernel(out_ref):
    out_ref[...] = jnp.zeros_like(out_ref)


def normal_kernel(
    axes,
    facts_ref,
    factors_ref,
    phase_ref,
    offset_ref,
    axis_ref,
    clear_ref,
    kept_ref,
    sent_ref,
    facts_out,
    phase_out,
    offset_out,
    axis_out,
    total,
    weights,
    basis,
    offsets,
    facts,
    semaphore,
):
    scalars = pltpu.make_async_copy(facts_ref, facts, semaphore)
    scalars.start()
    facts_out[...] = facts_ref[...]
    phase_out[...] = phase_ref[...]
    offset_out[...] = offset_ref[...]
    axis_out[...] = axis_ref[...]
    transits, stars = phase_ref.shape
    cells = stars // LANES
    knots = lax.broadcasted_iota(jnp.int32, (KB, LANES), 0)
    total[...] = jnp.zeros_like(total)
    weights[...] = clear_ref[...]
    scalars.wait()
    groups = transits // 8

    def group(cell, index, slot):
        first = pl.multiple_of(index * 8, 8)
        rows = pl.ds(first, 8)
        columns = pl.ds(pl.multiple_of(cell * LANES, LANES), LANES)
        number = first + lax.broadcasted_iota(jnp.int32, (8, LANES), 0)
        live = jnp.where(number < facts[COUNT, cell, 0], 1.0, 0.0)
        values = spline_basis(phase_ref[rows, columns])
        for shift in range(4):
            for order in range(4 - shift):
                basis[slot, shift * 4 + order] = values[order] * values[order + shift]
        offsets[slot] = offset_ref[rows, columns]
        parts = [axis_ref[m, rows, columns] for m in range(4)]
        lively = [part * live for part in parts]
        for place, (m, n) in enumerate(PAIRS):
            row = place if place < ROWS else place + 3
            weights[slot, pl.ds(row, 8, stride=16), :] = lively[m] * parts[n]
        for j in range(8):
            relative = knots - pair_rows(offsets[slot, pl.ds(j, 1), :])
            hits = [relative == order for order in range(4)]
            highs, lows = [], []
            for shift in range(4):
                piece = jnp.zeros((KB, LANES), jnp.float32)
                for order in range(4 - shift):
                    value = pair_rows(basis[slot, shift * 4 + order, pl.ds(j, 1), :])
                    piece = jnp.where(hits[order], value, piece)
                high, low = split(piece)
                highs.append(high)
                lows.append(low)
            weight_high, weight_low = split(weights[slot, pl.ds(j * 16, 16), :])
            left = jnp.concatenate([weight_high, weight_low], axis=0)
            right = jnp.concatenate([weight_high, jnp.zeros_like(weight_low)], axis=0)
            result = product(
                jnp.concatenate([left, right], axis=1),
                jnp.concatenate(highs, axis=0),
                jnp.concatenate(lows, axis=0),
            )
            band = jnp.concatenate(
                [result[0:8] + result[16:24], result[8:16] + result[24:32]], axis=1
            )
            for place in (facts[HOME, cell, first + j], facts[HALO, cell, first + j]):
                block = pl.ds(pl.multiple_of(place * 8, 8), 8)
                total[block, :] = total[block, :] + band

    over_groups(cells, groups, group)

    mine = lax.axis_index(axes) & 1
    half = kept_ref.shape[0] // ROWS * 8

    def pack(index, carry):
        target = pl.multiple_of(index * 8 * ROWS, 8)
        for out_ref, part in ((kept_ref, mine), (sent_ref, 1 - mine)):
            source = pl.multiple_of(part * half + index * 64, 64)
            for j in range(8):
                out_ref[pl.ds(target + j * ROWS, ROWS), :] = total[pl.ds(source + j * 8, ROWS), :]
        return carry

    lax.fori_loop(0, half // 64, pack, 0)


ENTRIES = tuple((row, column) for row in range(5) for column in range(row + 1))


def factor_kernel(facts_ref, star_ref, factors_ref, sums):
    transits, stars = star_ref.shape[1:]
    sums[...] = jnp.zeros_like(sums)

    for cell in range(stars // LANES):
        columns = pl.ds(cell * LANES, LANES)
        count = facts_ref[COUNT, cell : cell + 1, :]
        count = jnp.concatenate([count] * (LANES // transits), axis=1)
        count = jnp.broadcast_to(count, (8, LANES))

        def add(index, accumulated, columns=columns, count=count):
            first = pl.multiple_of(index * 8, 8)
            number = first + lax.broadcasted_iota(jnp.int32, (8, LANES), 0)
            live = jnp.where(number < count, 1.0, 0.0)
            parts = [star_ref[row, pl.ds(first, 8), columns] for row in range(5)]
            lively = [part * live for part in parts]
            return tuple(
                old + lively[row] * parts[column] for old, (row, column) in zip(accumulated, ENTRIES)
            )

        start = tuple(jnp.zeros((8, LANES), jnp.float32) for entry in ENTRIES)
        accumulated = lax.fori_loop(0, transits // 8, add, start, unroll=4)
        for entry in range(len(ENTRIES)):
            sums[entry, pl.ds(cell, 1), :] = jnp.sum(accumulated[entry], axis=0, keepdims=True)
    normal = [[None for column in range(5)] for row in range(5)]
    for entry, (row, column) in enumerate(ENTRIES):
        normal[row][column] = sums[entry] + (star_prior if row == column else 0.0)
    lower, inverse = cholesky_factor(normal, 5)
    for entry, (row, column) in enumerate(ENTRIES):
        factors_ref[entry] = inverse[row] if row == column else lower[row][column]


def star_kernel(
    facts,
    attitude_ref,
    factors_ref,
    phase_ref,
    offset_ref,
    axis_ref,
    star_ref,
    observed_ref,
    step_ref,
    second_ref,
    table,
    sums,
):
    transits, stars = phase_ref.shape
    cells = stars // LANES
    groups = transits // 8
    sums[...] = jnp.zeros_like(sums)
    sublane = lax.broadcasted_iota(jnp.int32, (8, LANES), 0)

    def predict_cell(cell, carry):
        columns = pl.ds(pl.multiple_of(cell * LANES, LANES), LANES)

        def predict(index, accumulated):
            first = pl.multiple_of(index * 8, 8)
            rows = pl.ds(first, 8)
            shift = jnp.zeros((8, LANES), jnp.int32)
            for j in range(8):
                owner = facts[OWNER, cell, first + j]
                slot = facts[SLOT, cell, first + j]
                column = pl.multiple_of((slot >> 3) * LANES, LANES)
                table[index, pl.ds(j, 4, stride=8), :] = attitude_ref[owner, :, pl.ds(column, LANES)]
                shift = jnp.where(sublane == j, (slot & 7) * KB, shift)
            number = first + lax.broadcasted_iota(jnp.int32, (8, LANES), 0)
            live = jnp.where(number < facts[COUNT, cell, 0], 1.0, 0.0)
            values = spline_basis(phase_ref[rows, columns])
            offset = offset_ref[rows, columns] + shift
            places = [offset + order for order in range(4)]
            predicted = jnp.zeros((8, LANES), jnp.float32)
            for m in range(4):
                spline = jnp.zeros((8, LANES), jnp.float32)
                looked = table[index, m * 8 : m * 8 + 8, :]
                for order in range(4):
                    found = jnp.take_along_axis(looked, places[order], axis=1)
                    spline = spline + found * values[order]
                predicted = predicted + spline * axis_ref[m, rows, columns]
            first_value = live * (observed_ref[rows, columns] - predicted)
            second_ref[rows, columns] = first_value
            parts = [star_ref[row, rows, columns] for row in range(5)]
            return tuple(old + part * first_value for old, part in zip(accumulated, parts))

        start = tuple(jnp.zeros((8, LANES), jnp.float32) for row in range(5))
        accumulated = lax.fori_loop(0, groups, predict, start, unroll=8)
        for entry in range(5):
            sums[entry, pl.ds(cell, 1), :] = jnp.sum(accumulated[entry], axis=0, keepdims=True)
        return carry

    lax.fori_loop(0, cells, predict_cell, 0)

    lower = [[None for column in range(5)] for row in range(5)]
    for entry, (row, column) in enumerate(ENTRIES):
        lower[row][column] = factors_ref[entry]
    inverse = [lower[row][row] for row in range(5)]
    answer = cholesky_solve(lower, inverse, [sums[row] for row in range(5)], 5)
    for row in range(5):
        sums[row] = answer[row]
        for cell in range(cells):
            step_ref[row : row + 1, cell * LANES : (cell + 1) * LANES] = answer[row][
                cell : cell + 1
            ]

    def correct(cell, carry):
        columns = pl.ds(pl.multiple_of(cell * LANES, LANES), LANES)
        own = [jnp.broadcast_to(sums[row, pl.ds(cell, 1), :], (8, LANES)) for row in range(5)]
        for index in range(groups):
            rows = pl.ds(index * 8, 8)
            number = index * 8 + sublane
            live = jnp.where(number < facts[COUNT, cell, 0], 1.0, 0.0)
            fitted = star_ref[0, rows, columns] * own[0]
            for row in range(1, 5):
                fitted = fitted + star_ref[row, rows, columns] * own[row]
            second_ref[rows, columns] = second_ref[rows, columns] - live * fitted
        return carry

    lax.fori_loop(0, cells, correct, 0)


def gradient_kernel(
    axes,
    facts,
    phase_ref,
    offset_ref,
    axis_ref,
    second_ref,
    kept_ref,
    sent_ref,
    total,
    weights,
    basis,
    offsets,
):
    transits, stars = phase_ref.shape
    cells = stars // LANES
    groups = transits // 8
    knots = lax.broadcasted_iota(jnp.int32, (KB, LANES), 0)
    lanes_block = lax.broadcasted_iota(jnp.int32, (8, LANES), 1) // KB
    total[...] = jnp.zeros_like(total)
    weights[...] = jnp.zeros_like(weights)

    def group(cell, index, slot):
        first = pl.multiple_of(index * 8, 8)
        rows = pl.ds(first, 8)
        columns = pl.ds(pl.multiple_of(cell * LANES, LANES), LANES)
        second = second_ref[rows, columns]
        for m in range(4):
            value = axis_ref[m, rows, columns] * second
            high = value.astype(jnp.bfloat16).astype(jnp.float32)
            weights[slot, pl.ds(m, 8, stride=16), :] = high
            weights[slot, pl.ds(4 + m, 8, stride=16), :] = value - high
        values = spline_basis(phase_ref[rows, columns])
        for order in range(4):
            basis[slot, order] = values[order]
        offsets[slot] = offset_ref[rows, columns]
        for j in range(8):
            relative = knots - pair_rows(offsets[slot, pl.ds(j, 1), :])
            piece = jnp.zeros((KB, LANES), jnp.float32)
            for order in range(4):
                value = pair_rows(basis[slot, order, pl.ds(j, 1), :])
                piece = jnp.where(relative == order, value, piece)
            high, low = split(piece)
            weight = weights[slot, pl.ds(j * 16, 16), :]
            right = jnp.where(knots < 4, weight, 0.0)
            result = product(
                jnp.concatenate([weight, right], axis=1).astype(jnp.bfloat16),
                jnp.concatenate([high] * 4, axis=0),
                jnp.concatenate([low] * 4, axis=0),
            )[0:8]
            result = jnp.concatenate([result, result], axis=1)
            for place in (facts[HOME_LANES, cell, first + j], facts[HALO_LANES, cell, first + j]):
                chosen = jnp.where(lanes_block == (place & 7), result, 0.0)
                block = pl.ds(pl.multiple_of((place >> 3) * 8, 8), 8)
                total[block, :] = total[block, :] + chosen

    over_groups(cells, groups, group)

    mine = lax.axis_index(axes) & 1
    half = kept_ref.shape[0] * 2

    def pack(index, carry):
        target = pl.multiple_of(index * 8, 8)
        for out_ref, part in ((kept_ref, mine), (sent_ref, 1 - mine)):
            source = pl.multiple_of(part * half + index * 16, 16)
            for j in range(2):
                tile = total[pl.ds(source + j * 8, 8), :]
                out_ref[pl.ds(target + j * 4, 4), :] = tile[0:4] + tile[4:8]
        return carry

    lax.fori_loop(0, half // 16, pack, 0)


def share_of(axes, group):
    me = lax.axis_index(axes)
    mine = 0
    for bit in group:
        mine = mine * 2 + ((me >> bit) & 1)
    return mine


def add_rows(out_ref, base, inputs, start, rows):
    step = 40 if rows % 40 == 0 else rows

    def add(index, carry):
        source = pl.ds(start + index * step, step)
        added = inputs[0][source, :]
        for ref in inputs[1:]:
            added = added + ref[source, :]
        out_ref[pl.ds(base + index * step, step), :] = added
        return carry

    if step == rows:
        add(0, 0)
    else:
        lax.fori_loop(0, rows // step, add, 0)


def order_of(members):
    return {2: ((1,), (1,)), 4: ((1, 3, 2), (2, 1, 3))}[members]


def add_kernel(axes, group, families, *refs):
    mine = share_of(axes, group)
    members = 1 << len(group)
    odd = lax.axis_index(axes) & 1
    others = [0] + [jnp.where(odd == 1, second, first) for first, second in zip(*order_of(members))]
    outputs = refs[-members:]
    first = 0
    base = 0
    for counts, rows in families:
        segments = []
        for count in counts:
            segments.append(refs[first : first + count])
            first += count
        within = members // len(segments)
        for other, out_ref in zip(others, outputs):
            which = mine ^ other
            for number, inputs in enumerate(segments):
                if len(segments) == 1:
                    add_rows(out_ref, base, inputs, which * rows, rows)
                else:

                    @pl.when(which // within == number)
                    def _(out_ref=out_ref, inputs=inputs, which=which, base=base, rows=rows):
                        add_rows(out_ref, base, inputs, (which % within) * rows, rows)

        base += rows


def cut_kernel(axes, cuts, count, *refs):
    me = lax.axis_index(axes)
    odd = me & 1
    outputs = refs[count:]
    for place, (inputs, base, rows, bit) in enumerate(cuts):
        mine = (me >> jnp.where(odd == 1, 3 - bit, bit)) & 1
        arrays = [refs[index] for index in inputs]
        add_rows(outputs[2 * place], 0, arrays, base + mine * rows, rows)
        add_rows(outputs[2 * place + 1], 0, arrays, base + (1 - mine) * rows, rows)


def sweep_kernel(spread, axes, *refs):
    *parts, out_ref, band_ref, band = refs
    added = parts[0][...]
    for part in parts[1:]:
        added = added + part[...]
    band_ref[...] = added
    width = band.shape[2]
    tiles = width // LANES
    lane_block = lax.broadcasted_iota(jnp.int32, (8, LANES), 1) // KB
    filler = jnp.zeros((8 - ROWS, LANES), jnp.float32)
    for half in range(2):
        for shift in range(4):
            start = half * 64 + shift * KB
            for tile in range(tiles):
                merged = jnp.zeros((8, LANES), jnp.float32)
                for place in range(min(8, spread - tile * 8)):
                    block = tile * 8 + place
                    piece = jnp.concatenate(
                        [band_ref[block * ROWS : (block + 1) * ROWS, :], filler], axis=0
                    )
                    moved = (place * KB - start) % LANES
                    if moved:
                        piece = pltpu.roll(piece, moved, axis=1)
                    merged = jnp.where(lane_block == place, piece, merged)
                band[shift, half * 8 : half * 8 + 8, tile * LANES : (tile + 1) * LANES] = merged
    index = {}
    for place, (m, n) in enumerate(PAIRS):
        row = place if place < ROWS else place + 3
        index[(m, n)] = row
        index[(n, m)] = row

    def row_of(shift, m, n):
        return band[shift, index[(m, n)] : index[(m, n)] + 1, :]

    ahead = [
        [jnp.concatenate([row_of(shift, m, n) for n in range(4)], axis=0) for m in range(4)]
        for shift in range(4)
    ]
    behind = [
        [pltpu.roll(ahead[shift][m], shift, axis=1) if shift else None for m in range(4)]
        for shift in range(4)
    ]
    shifted = 2.0 * smoothing + damping
    diagonal = [
        [row_of(0, row, column) + (shifted if row == column else 0.0) for column in range(4)]
        for row in range(4)
    ]
    lower, inverse = cholesky_factor(diagonal, 4)
    gradient = jnp.concatenate(
        [
            band_ref[spread * ROWS + tile * 4 : spread * ROWS + (tile + 1) * 4, :]
            for tile in range(tiles)
        ],
        axis=1,
    )
    lane = lax.broadcasted_iota(jnp.int32, (4, width), 1)
    me = lax.axis_index(axes)
    start = jnp.where(me == 0, KB, 0)
    stop = jnp.where(me == lax.axis_size(axes) - 1, (spread - 1) * KB, spread * KB)
    keep = jnp.where((lane >= start) & (lane < stop), relaxation, 0.0)
    answer = jnp.zeros((4, width), jnp.float32)
    for sweep in range(ITERS):
        misfit = gradient
        if sweep:
            moved = {}
            for shift in range(1, 4):
                moved[shift] = pltpu.roll(answer, width - shift, axis=1)
                moved[-shift] = pltpu.roll(answer, shift, axis=1)
            applied = []
            for m in range(4):
                terms = ahead[0][m] * answer
                for shift in range(1, 4):
                    terms = terms + ahead[shift][m] * moved[shift]
                    terms = terms + behind[shift][m] * moved[-shift]
                applied.append(jnp.sum(terms, axis=0, keepdims=True))
            regular = smoothing * (2.0 * answer - moved[-1] - moved[1]) + damping * answer
            misfit = gradient - regular - jnp.concatenate(applied, axis=0)
        correction = cholesky_solve(lower, inverse, [misfit[m : m + 1] for m in range(4)], 4)
        answer = answer + keep * jnp.concatenate(correction, axis=0)
    out_ref[...] = answer[:, KB : KB + out_ref.shape[1]]


def in_vmem(count):
    return [pl.BlockSpec(memory_space=pltpu.VMEM) for operand in range(count)]


def in_smem(count):
    return [pl.BlockSpec(memory_space=pltpu.SMEM) for operand in range(count)]


def work(microseconds):
    return pl.CostEstimate(flops=0, bytes_accessed=microseconds * 3_600_000, transcendentals=0)


def params(rows=0):
    return pltpu.CompilerParams(vmem_limit_bytes=min(56 << 20, (8 << 20) + 2 * rows * LANES * 4))


def call_facts(counts, attitude, owners, slots, devices):
    shape = (COUNT + 1,) + owners.shape
    return pl.pallas_call(
        functools.partial(facts_kernel, attitude.shape[1] // KB),
        out_shape=[
            jax.ShapeDtypeStruct(shape, jnp.int32),
            jax.ShapeDtypeStruct((devices,) + attitude.shape, jnp.float32),
        ],
        in_specs=in_smem(1) + in_vmem(3),
        out_specs=in_vmem(2),
        compiler_params=pltpu.CompilerParams(vmem_limit_bytes=62 << 20),
        cost_estimate=work(1),
        name="facts",
    )(counts, attitude, owners, slots)


def call_clear():
    return pl.pallas_call(
        clear_kernel,
        out_shape=jax.ShapeDtypeStruct((UNROLL, 8 * 16, LANES), jnp.float32),
        out_specs=in_vmem(1)[0],
        compiler_params=params(),
        cost_estimate=work(200),
        name="clear",
    )()


def call_normals(axes, facts, factors, phase, knot_offset, partials, clear, devices, spread):
    f32 = jnp.float32
    half = jax.ShapeDtypeStruct((devices // 2 * spread * ROWS, LANES), f32)
    blocks = devices * spread
    return pl.pallas_call(
        functools.partial(normal_kernel, axes),
        out_shape=[half, half]
        + [jax.ShapeDtypeStruct(x.shape, x.dtype) for x in (facts, phase, knot_offset, partials)],
        in_specs=in_vmem(6),
        out_specs=in_vmem(6),
        scratch_shapes=[
            pltpu.VMEM(((blocks + 1) * 8, LANES), f32),
            pltpu.VMEM((UNROLL, 8 * 16, LANES), f32),
            pltpu.VMEM((UNROLL, 16, 8, LANES), f32),
            pltpu.VMEM((UNROLL, 8, LANES), jnp.int32),
            pltpu.SMEM(facts.shape, jnp.int32),
            pltpu.SemaphoreType.DMA,
        ],
        compiler_params=params(blocks * 13),
        cost_estimate=work(100),
        name="normals",
    )(facts, factors, phase, knot_offset, partials, clear)


def call_add(axes, group, families):
    members = 1 << len(group)
    rows = sum(count for segments, count in families)
    out = jax.ShapeDtypeStruct((rows, LANES), jnp.float32)
    arrays = [array for segments, count in families for segment in segments for array in segment]
    shapes = [([len(segment) for segment in segments], count) for segments, count in families]
    return pl.pallas_call(
        functools.partial(add_kernel, axes, group, shapes),
        out_shape=[out] * members,
        in_specs=in_vmem(len(arrays)),
        out_specs=in_vmem(members),
        compiler_params=params(rows * members * 3),
        cost_estimate=work(0),
        name="shares",
    )(*arrays)


def call_cut(axes, arrays, cuts):
    outs = [
        jax.ShapeDtypeStruct((rows, LANES), jnp.float32) for inputs, base, rows, bit in cuts for half in range(2)
    ]
    return pl.pallas_call(
        functools.partial(cut_kernel, axes, cuts, len(arrays)),
        out_shape=outs,
        in_specs=in_vmem(len(arrays)),
        out_specs=in_vmem(len(outs)),
        compiler_params=params(sum(out.shape[0] for out in outs) * 3),
        cost_estimate=work(0),
        name="halves",
    )(*arrays)


def call_factors(facts, star_partials):
    return pl.pallas_call(
        factor_kernel,
        out_shape=jax.ShapeDtypeStruct((len(ENTRIES), 8, LANES), jnp.float32),
        in_specs=in_vmem(2),
        out_specs=in_vmem(1)[0],
        scratch_shapes=[pltpu.VMEM((len(ENTRIES), 8, LANES), jnp.float32)],
        compiler_params=params(),
        cost_estimate=work(200),
        name="factors",
    )(facts, star_partials)


def call_stars(facts, attitude, factors, phase, knot_offset, partials, star_partials, observed):
    f32 = jnp.float32
    transits, stars = phase.shape
    return pl.pallas_call(
        star_kernel,
        out_shape=[
            jax.ShapeDtypeStruct((5, stars), f32),
            jax.ShapeDtypeStruct((transits, stars), f32),
        ],
        in_specs=in_smem(1) + in_vmem(7),
        out_specs=in_vmem(2),
        scratch_shapes=[
            pltpu.VMEM((transits // 8, 32, LANES), f32),
            pltpu.VMEM((5, 8, LANES), f32),
        ],
        compiler_params=params(),
        cost_estimate=work(5),
        name="stars",
    )(facts, attitude, factors, phase, knot_offset, partials, star_partials, observed)


def call_gradients(axes, facts, phase, knot_offset, partials, second, devices, spread):
    f32 = jnp.float32
    tiles = (spread + 7) // 8
    half = jax.ShapeDtypeStruct((devices // 2 * tiles * 4, LANES), f32)
    return pl.pallas_call(
        functools.partial(gradient_kernel, axes),
        out_shape=[half, half],
        in_specs=in_smem(1) + in_vmem(4),
        out_specs=in_vmem(2),
        scratch_shapes=[
            pltpu.VMEM(((devices + 1) * tiles * 8, LANES), f32),
            pltpu.VMEM((UNROLL, 8 * 16, LANES), f32),
            pltpu.VMEM((UNROLL, 4, 8, LANES), f32),
            pltpu.VMEM((UNROLL, 8, LANES), jnp.int32),
        ],
        compiler_params=params((devices + 1) * tiles * 12),
        cost_estimate=work(5),
        name="gradients",
    )(facts, phase, knot_offset, partials, second)


def swap(arrays, group, axes, devices):
    def mask(other):
        return sum(1 << bit for place, bit in enumerate(reversed(group)) if (other >> place) & 1)

    even, odd = order_of(len(arrays) + 1)
    arrived = []
    for array, first, second in zip(arrays, even, odd):
        pairs = [(i, i ^ mask(second if i & 1 else first)) for i in range(devices)]
        arrived.append(lax.ppermute(array, axes, pairs))
    return arrived


def hop(array, bit, axes, devices):
    pairs = [(i, i ^ (1 << (3 - bit if bit and i & 1 else bit))) for i in range(devices)]
    return lax.ppermute(array, axes, pairs)


def per_device(
    attitude,
    star_partials,
    attitude_partials,
    observed,
    phase,
    knot_offset,
    cell_counts,
    interval_owner,
    block_slot,
):
    axes = ("cells", "tm")
    devices = lax.axis_size("cells") * lax.axis_size("tm")
    levels = devices.bit_length() - 1
    cells = cell_counts.shape[0]
    transits = observed.shape[0]
    blocks = attitude.shape[1] // KB
    spread = blocks + 2
    tiles = (spread + 7) // 8
    width = tiles * LANES

    owners = interval_owner.reshape(cells, transits)
    facts, wide = call_facts(cell_counts, attitude, owners, block_slot, devices)
    whole = lax.all_to_all(wide, axes, split_axis=0, concat_axis=0, tiled=True)
    bits = list(range(devices.bit_length() - 1))
    later = [bits[start : start + 2] for start in range(3, len(bits), 2)]
    groups = [bits[:1], bits[1:3]] + later
    final = later[-1]
    chunks = (spread * ROWS, tiles * 4)

    def rows(kind, group):
        return chunks[kind] * (devices >> (group[-1] + 1))

    def advance(segments, kind, group):
        kept, *sent = call_add(axes, group, [(segments, rows(kind, group))])
        return [[kept] + swap(sent, group, axes, devices)]

    def turn(array, bit):
        return hop(array, bit, axes, devices)

    clear = call_clear()
    clear, facts = lax.optimization_barrier((clear, facts))
    factors = call_factors(facts, star_partials)
    kept, sent, facts, phase, knot_offset, attitude_partials = call_normals(
        axes, facts, factors, phase, knot_offset, attitude_partials, clear, devices, spread
    )
    kept, sent, whole = lax.optimization_barrier((kept, sent, whole))
    arrived = turn(sent, 0)
    star_step, second = call_stars(
        facts, whole, factors, phase, knot_offset, attitude_partials, star_partials, observed
    )
    kept, arrived, second = lax.optimization_barrier((kept, arrived, second))
    size = kept.shape[0] // 4
    halves = call_cut(
        axes, [kept, arrived], [([0, 1], 0, size, 1), ([0, 1], 2 * size, size, 2)]
    )
    second, *halves = lax.optimization_barrier((second, *halves))
    low = [halves[0], turn(halves[1], 1)]
    high = [halves[2], turn(halves[3], 2)]
    kept, sent = call_gradients(
        axes, facts, phase, knot_offset, attitude_partials, second, devices, spread
    )
    gradients = [kept, turn(sent, 0)]
    both = lax.optimization_barrier((*low, *high, *gradients))
    halves = call_cut(axes, both[:4], [([0, 1], 0, size // 2, 2), ([2, 3], 0, size // 2, 1)])
    normals = [[halves[0], turn(halves[1], 2)], [halves[2], turn(halves[3], 1)]]
    gradients = [both[4:]]
    for group in groups[1:-1]:
        gradients = advance(gradients, 1, group)
    for group in later[:-1]:
        normals = advance(normals, 0, group)
    families = [(normals, rows(0, final)), (gradients, rows(1, final))]
    kept, *sent = call_add(axes, final, families)
    parts = [kept] + swap(sent, final, axes, devices)
    attitude_step = pl.pallas_call(
        functools.partial(sweep_kernel, spread, axes),
        out_shape=jax.ShapeDtypeStruct((4, blocks * KB), jnp.float32),
        in_specs=in_vmem(len(parts)),
        out_specs=in_vmem(1)[0],
        scratch_shapes=[
            pltpu.VMEM(kept.shape, jnp.float32),
            pltpu.VMEM((4, 16, width), jnp.float32),
        ],
        compiler_params=params(),
        cost_estimate=work(2),
        name="sweeps",
    )(*parts)
    return (star_step, attitude_step)


def solution(mesh):
    split_axes = ("cells", "tm")
    placed = (
        P(None, split_axes),
        P(None, None, split_axes),
        P(None, None, split_axes),
        P(None, split_axes),
        P(None, split_axes),
        P(None, split_axes),
        P(split_axes),
        P(split_axes, None, None),
        P(split_axes, None),
    )
    return jax.shard_map(
        per_device,
        mesh=mesh,
        in_specs=placed,
        out_specs=(P(None, split_axes), P(None, split_axes)),
        check_vma=False,
    )
```

```python
import functools

import jax
import jax.numpy as jnp
from jax import lax
from jax.experimental import pallas as pl
from jax.experimental.pallas import tpu as pltpu
from jax.sharding import PartitionSpec as P

CS = 128
KB = 16
ITERS = 6
LANES = 128
PAIRS = tuple((m, n) for m in range(4) for n in range(m, 4))
HOME, HALO, HOME_LANES, HALO_LANES, OWNER, SLOT, COUNT = range(7)
ROWS = 5
UNROLL = 8

smoothing = 16.0
damping = 2.0
relaxation = 0.5
star_prior = 1.0


def spline_basis(phase):
    square = phase * phase
    cube = square * phase
    rest = 1.0 - phase
    return (
        rest * rest * rest * (1.0 / 6.0),
        (3.0 * cube - 6.0 * square + 4.0) * (1.0 / 6.0),
        (-3.0 * cube + 3.0 * square + 3.0 * phase + 1.0) * (1.0 / 6.0),
        cube * (1.0 / 6.0),
    )


def cholesky_factor(matrix, size):
    lower = [[None for column in range(size)] for row in range(size)]
    inverse = [None for column in range(size)]
    for column in range(size):
        total = matrix[column][column]
        for inner in range(column):
            total = total - lower[column][inner] * lower[column][inner]
        inverse[column] = 1.0 / jnp.sqrt(total)
        for row in range(column + 1, size):
            accum = matrix[row][column]
            for inner in range(column):
                accum = accum - lower[row][inner] * lower[column][inner]
            lower[row][column] = accum * inverse[column]
    return lower, inverse


def cholesky_solve(lower, inverse, rhs, size):
    forward = []
    for row in range(size):
        accum = rhs[row]
        for inner in range(row):
            accum = accum - lower[row][inner] * forward[inner]
        forward.append(accum * inverse[row])
    answer = [None for row in range(size)]
    for row in reversed(range(size)):
        accum = forward[row]
        for inner in range(row + 1, size):
            accum = accum - lower[inner][row] * answer[inner]
        answer[row] = accum * inverse[row]
    return answer


def split(value):
    high = value.astype(jnp.bfloat16)
    low = (value - high.astype(jnp.float32)).astype(jnp.bfloat16)
    return high, low


def over_groups(cells, groups, body):
    def cell_body(cell, carry):
        def some(index, inner):
            for slot in range(UNROLL):
                body(cell, index * UNROLL + slot, slot)
            return inner

        return lax.fori_loop(0, groups // UNROLL, some, carry)

    lax.fori_loop(0, cells, cell_body, 0)


def pair_rows(value):
    return jnp.broadcast_to(value, (KB, LANES))


def product(weights, matrix_high, matrix_low):
    return lax.dot_general(
        weights,
        jnp.concatenate([matrix_high, matrix_low], axis=1),
        (((1,), (1,)), ((), ())),
        preferred_element_type=jnp.float32,
    )


def facts_kernel(blocks, counts, attitude_ref, owners_ref, slots_ref, facts_ref, wide_ref):
    devices = wide_ref.shape[0]
    levels = devices.bit_length() - 1
    spread = blocks + 2
    lanes = (spread + 7) // 8 * 8
    owners = owners_ref[...]
    slots = slots_ref[...]
    cells = owners.shape[0]

    def reverse(owner):
        reversed_bits = jnp.zeros_like(owner)
        for bit in range(levels):
            reversed_bits = reversed_bits | (((owner >> bit) & 1) << (levels - 1 - bit))
        return reversed_bits

    def reverse_band(owner):
        bits = [(owner >> bit) & 1 for bit in range(levels)]
        swapped = bits[0] != bits[3]
        order = [bits[0], bits[3], jnp.where(swapped, bits[2], bits[1])]
        order += [jnp.where(swapped, bits[1], bits[2])] + bits[4:]
        place = jnp.zeros_like(owner)
        for bit in order:
            place = place * 2 + bit
        return place

    first = slots == 0
    final = slots == blocks - 1
    neighbour = owners + jnp.where(first, -1, jnp.where(final, 1, 0))
    nowhere = (neighbour == owners) | (neighbour < 0) | (neighbour >= devices)
    home_owner = reverse(owners)
    halo_owner = jnp.where(nowhere, devices, reverse(neighbour))
    home_band = reverse_band(owners)
    halo_band = jnp.where(nowhere, devices, reverse_band(neighbour))
    home_place = slots + 1
    halo_place = jnp.where(first & ~nowhere, spread - 1, 0)
    facts_ref[HOME] = home_band * spread + home_place
    facts_ref[HALO] = halo_band * spread + halo_place
    facts_ref[HOME_LANES] = home_owner * lanes + home_place
    facts_ref[HALO_LANES] = halo_owner * lanes + halo_place
    facts_ref[OWNER] = owners
    facts_ref[SLOT] = slots
    for cell in range(cells):
        facts_ref[COUNT, cell : cell + 1, :] = jnp.full((1, owners.shape[1]), counts[cell], jnp.int32)
    attitude = attitude_ref[...]

    def copy(index, carry):
        wide_ref[index] = attitude
        return carry

    lax.fori_loop(0, devices, copy, 0, unroll=8)


def clear_kernel(out_ref):
    out_ref[...] = jnp.zeros_like(out_ref)


def normal_kernel(
    axes,
    facts_ref,
    factors_ref,
    phase_ref,
    offset_ref,
    axis_ref,
    clear_ref,
    kept_ref,
    sent_ref,
    facts_out,
    phase_out,
    offset_out,
    axis_out,
    total,
    weights,
    basis,
    offsets,
    facts,
    semaphore,
):
    scalars = pltpu.make_async_copy(facts_ref, facts, semaphore)
    scalars.start()
    facts_out[...] = facts_ref[...]
    phase_out[...] = phase_ref[...]
    offset_out[...] = offset_ref[...]
    axis_out[...] = axis_ref[...]
    transits, stars = phase_ref.shape
    cells = stars // LANES
    knots = lax.broadcasted_iota(jnp.int32, (KB, LANES), 0)
    total[...] = jnp.zeros_like(total)
    weights[...] = clear_ref[...]
    scalars.wait()
    groups = transits // 8

    def group(cell, index, slot):
        first = pl.multiple_of(index * 8, 8)
        rows = pl.ds(first, 8)
        columns = pl.ds(pl.multiple_of(cell * LANES, LANES), LANES)
        number = first + lax.broadcasted_iota(jnp.int32, (8, LANES), 0)
        live = jnp.where(number < facts[COUNT, cell, 0], 1.0, 0.0)
        values = spline_basis(phase_ref[rows, columns])
        for shift in range(4):
            for order in range(4 - shift):
                basis[slot, shift * 4 + order] = values[order] * values[order + shift]
        offsets[slot] = offset_ref[rows, columns]
        parts = [axis_ref[m, rows, columns] for m in range(4)]
        lively = [part * live for part in parts]
        for place, (m, n) in enumerate(PAIRS):
            row = place if place < ROWS else place + 3
            weights[slot, pl.ds(row, 8, stride=16), :] = lively[m] * parts[n]
        for j in range(8):
            relative = knots - pair_rows(offsets[slot, pl.ds(j, 1), :])
            hits = [relative == order for order in range(4)]
            highs, lows = [], []
            for shift in range(4):
                piece = jnp.zeros((KB, LANES), jnp.float32)
                for order in range(4 - shift):
                    value = pair_rows(basis[slot, shift * 4 + order, pl.ds(j, 1), :])
                    piece = jnp.where(hits[order], value, piece)
                high, low = split(piece)
                highs.append(high)
                lows.append(low)
            weight_high, weight_low = split(weights[slot, pl.ds(j * 16, 16), :])
            left = jnp.concatenate([weight_high, weight_low], axis=0)
            right = jnp.concatenate([weight_high, jnp.zeros_like(weight_low)], axis=0)
            result = product(
                jnp.concatenate([left, right], axis=1),
                jnp.concatenate(highs, axis=0),
                jnp.concatenate(lows, axis=0),
            )
            band = jnp.concatenate(
                [result[0:8] + result[16:24], result[8:16] + result[24:32]], axis=1
            )
            for place in (facts[HOME, cell, first + j], facts[HALO, cell, first + j]):
                block = pl.ds(pl.multiple_of(place * 8, 8), 8)
                total[block, :] = total[block, :] + band

    over_groups(cells, groups, group)

    mine = lax.axis_index(axes) & 1
    half = kept_ref.shape[0] // ROWS * 8

    def pack(index, carry):
        target = pl.multiple_of(index * 8 * ROWS, 8)
        for out_ref, part in ((kept_ref, mine), (sent_ref, 1 - mine)):
            source = pl.multiple_of(part * half + index * 64, 64)
            for j in range(8):
                out_ref[pl.ds(target + j * ROWS, ROWS), :] = total[pl.ds(source + j * 8, ROWS), :]
        return carry

    lax.fori_loop(0, half // 64, pack, 0)


ENTRIES = tuple((row, column) for row in range(5) for column in range(row + 1))


def factor_kernel(facts_ref, star_ref, factors_ref, sums):
    transits, stars = star_ref.shape[1:]
    sums[...] = jnp.zeros_like(sums)

    for cell in range(stars // LANES):
        columns = pl.ds(cell * LANES, LANES)
        count = facts_ref[COUNT, cell : cell + 1, :]
        count = jnp.concatenate([count] * (LANES // transits), axis=1)
        count = jnp.broadcast_to(count, (8, LANES))

        def add(index, accumulated, columns=columns, count=count):
            first = pl.multiple_of(index * 8, 8)
            number = first + lax.broadcasted_iota(jnp.int32, (8, LANES), 0)
            live = jnp.where(number < count, 1.0, 0.0)
            parts = [star_ref[row, pl.ds(first, 8), columns] for row in range(5)]
            lively = [part * live for part in parts]
            return tuple(
                old + lively[row] * parts[column] for old, (row, column) in zip(accumulated, ENTRIES)
            )

        start = tuple(jnp.zeros((8, LANES), jnp.float32) for entry in ENTRIES)
        accumulated = lax.fori_loop(0, transits // 8, add, start, unroll=4)
        for entry in range(len(ENTRIES)):
            sums[entry, pl.ds(cell, 1), :] = jnp.sum(accumulated[entry], axis=0, keepdims=True)
    normal = [[None for column in range(5)] for row in range(5)]
    for entry, (row, column) in enumerate(ENTRIES):
        normal[row][column] = sums[entry] + (star_prior if row == column else 0.0)
    lower, inverse = cholesky_factor(normal, 5)
    for entry, (row, column) in enumerate(ENTRIES):
        factors_ref[entry] = inverse[row] if row == column else lower[row][column]


def star_kernel(
    facts,
    attitude_ref,
    factors_ref,
    phase_ref,
    offset_ref,
    axis_ref,
    star_ref,
    observed_ref,
    step_ref,
    second_ref,
    table,
    sums,
):
    transits, stars = phase_ref.shape
    cells = stars // LANES
    groups = transits // 8
    sums[...] = jnp.zeros_like(sums)
    sublane = lax.broadcasted_iota(jnp.int32, (8, LANES), 0)

    def predict_cell(cell, carry):
        columns = pl.ds(pl.multiple_of(cell * LANES, LANES), LANES)

        def predict(index, accumulated):
            first = pl.multiple_of(index * 8, 8)
            rows = pl.ds(first, 8)
            shift = jnp.zeros((8, LANES), jnp.int32)
            for j in range(8):
                owner = facts[OWNER, cell, first + j]
                slot = facts[SLOT, cell, first + j]
                column = pl.multiple_of((slot >> 3) * LANES, LANES)
                table[index, pl.ds(j, 4, stride=8), :] = attitude_ref[owner, :, pl.ds(column, LANES)]
                shift = jnp.where(sublane == j, (slot & 7) * KB, shift)
            number = first + lax.broadcasted_iota(jnp.int32, (8, LANES), 0)
            live = jnp.where(number < facts[COUNT, cell, 0], 1.0, 0.0)
            values = spline_basis(phase_ref[rows, columns])
            offset = offset_ref[rows, columns] + shift
            places = [offset + order for order in range(4)]
            predicted = jnp.zeros((8, LANES), jnp.float32)
            for m in range(4):
                spline = jnp.zeros((8, LANES), jnp.float32)
                looked = table[index, m * 8 : m * 8 + 8, :]
                for order in range(4):
                    found = jnp.take_along_axis(looked, places[order], axis=1)
                    spline = spline + found * values[order]
                predicted = predicted + spline * axis_ref[m, rows, columns]
            first_value = live * (observed_ref[rows, columns] - predicted)
            second_ref[rows, columns] = first_value
            parts = [star_ref[row, rows, columns] for row in range(5)]
            return tuple(old + part * first_value for old, part in zip(accumulated, parts))

        start = tuple(jnp.zeros((8, LANES), jnp.float32) for row in range(5))
        accumulated = lax.fori_loop(0, groups, predict, start, unroll=8)
        for entry in range(5):
            sums[entry, pl.ds(cell, 1), :] = jnp.sum(accumulated[entry], axis=0, keepdims=True)
        return carry

    lax.fori_loop(0, cells, predict_cell, 0)

    lower = [[None for column in range(5)] for row in range(5)]
    for entry, (row, column) in enumerate(ENTRIES):
        lower[row][column] = factors_ref[entry]
    inverse = [lower[row][row] for row in range(5)]
    answer = cholesky_solve(lower, inverse, [sums[row] for row in range(5)], 5)
    for row in range(5):
        sums[row] = answer[row]
        for cell in range(cells):
            step_ref[row : row + 1, cell * LANES : (cell + 1) * LANES] = answer[row][
                cell : cell + 1
            ]

    def correct(cell, carry):
        columns = pl.ds(pl.multiple_of(cell * LANES, LANES), LANES)
        own = [jnp.broadcast_to(sums[row, pl.ds(cell, 1), :], (8, LANES)) for row in range(5)]
        for index in range(groups):
            rows = pl.ds(index * 8, 8)
            number = index * 8 + sublane
            live = jnp.where(number < facts[COUNT, cell, 0], 1.0, 0.0)
            fitted = star_ref[0, rows, columns] * own[0]
            for row in range(1, 5):
                fitted = fitted + star_ref[row, rows, columns] * own[row]
            second_ref[rows, columns] = second_ref[rows, columns] - live * fitted
        return carry

    lax.fori_loop(0, cells, correct, 0)


def gradient_kernel(
    axes,
    facts,
    phase_ref,
    offset_ref,
    axis_ref,
    second_ref,
    kept_ref,
    sent_ref,
    total,
    weights,
    basis,
    offsets,
):
    transits, stars = phase_ref.shape
    cells = stars // LANES
    groups = transits // 8
    knots = lax.broadcasted_iota(jnp.int32, (KB, LANES), 0)
    lanes_block = lax.broadcasted_iota(jnp.int32, (8, LANES), 1) // KB
    total[...] = jnp.zeros_like(total)
    weights[...] = jnp.zeros_like(weights)

    def group(cell, index, slot):
        first = pl.multiple_of(index * 8, 8)
        rows = pl.ds(first, 8)
        columns = pl.ds(pl.multiple_of(cell * LANES, LANES), LANES)
        second = second_ref[rows, columns]
        for m in range(4):
            value = axis_ref[m, rows, columns] * second
            high = value.astype(jnp.bfloat16).astype(jnp.float32)
            weights[slot, pl.ds(m, 8, stride=16), :] = high
            weights[slot, pl.ds(4 + m, 8, stride=16), :] = value - high
        values = spline_basis(phase_ref[rows, columns])
        for order in range(4):
            basis[slot, order] = values[order]
        offsets[slot] = offset_ref[rows, columns]
        for j in range(8):
            relative = knots - pair_rows(offsets[slot, pl.ds(j, 1), :])
            piece = jnp.zeros((KB, LANES), jnp.float32)
            for order in range(4):
                value = pair_rows(basis[slot, order, pl.ds(j, 1), :])
                piece = jnp.where(relative == order, value, piece)
            high, low = split(piece)
            weight = weights[slot, pl.ds(j * 16, 16), :]
            right = jnp.where(knots < 4, weight, 0.0)
            result = product(
                jnp.concatenate([weight, right], axis=1).astype(jnp.bfloat16),
                jnp.concatenate([high] * 4, axis=0),
                jnp.concatenate([low] * 4, axis=0),
            )[0:8]
            result = jnp.concatenate([result, result], axis=1)
            for place in (facts[HOME_LANES, cell, first + j], facts[HALO_LANES, cell, first + j]):
                chosen = jnp.where(lanes_block == (place & 7), result, 0.0)
                block = pl.ds(pl.multiple_of((place >> 3) * 8, 8), 8)
                total[block, :] = total[block, :] + chosen

    over_groups(cells, groups, group)

    mine = lax.axis_index(axes) & 1
    half = kept_ref.shape[0] * 2

    def pack(index, carry):
        target = pl.multiple_of(index * 8, 8)
        for out_ref, part in ((kept_ref, mine), (sent_ref, 1 - mine)):
            source = pl.multiple_of(part * half + index * 16, 16)
            for j in range(2):
                tile = total[pl.ds(source + j * 8, 8), :]
                out_ref[pl.ds(target + j * 4, 4), :] = tile[0:4] + tile[4:8]
        return carry

    lax.fori_loop(0, half // 16, pack, 0)


def share_of(axes, group):
    me = lax.axis_index(axes)
    mine = 0
    for bit in group:
        mine = mine * 2 + ((me >> bit) & 1)
    return mine


def add_rows(out_ref, base, inputs, start, rows):
    step = 40 if rows % 40 == 0 else rows

    def add(index, carry):
        terms = [ref[pl.ds(offset + start + index * step, step), :] for ref, offset in inputs]
        added = terms[0]
        for term in terms[1:]:
            added = added + term
        out_ref[pl.ds(base + index * step, step), :] = added
        return carry

    if step == rows:
        add(0, 0)
    else:
        lax.fori_loop(0, rows // step, add, 0)


def order_of(members):
    return {2: ((1,), (1,)), 4: ((3, 2, 1), (1, 3, 2))}[members]


def add_kernel(axes, group, families, *refs):
    mine = share_of(axes, group)
    members = 1 << len(group)
    odd = lax.axis_index(axes) & 1
    others = [0] + [jnp.where(odd == 1, second, first) for first, second in zip(*order_of(members))]
    outputs = refs[-members:]
    first = 0
    base = 0
    for offsets, rows in families:
        segments = []
        for begins in offsets:
            segments.append(list(zip(refs[first : first + len(begins)], begins)))
            first += len(begins)
        within = members // len(segments)
        for other, out_ref in zip(others, outputs):
            which = mine ^ other
            for number, inputs in enumerate(segments):
                if len(segments) == 1:
                    add_rows(out_ref, base, inputs, which * rows, rows)
                else:

                    @pl.when(which // within == number)
                    def _(out_ref=out_ref, inputs=inputs, which=which, base=base, rows=rows):
                        add_rows(out_ref, base, inputs, (which % within) * rows, rows)

        base += rows


def cut_kernel(axes, cuts, count, *refs):
    me = lax.axis_index(axes)
    odd = me & 1
    outputs = refs[count:]
    for place, (inputs, base, rows, bit) in enumerate(cuts):
        mine = (me >> jnp.where(odd == 1, 3 - bit, bit)) & 1
        arrays = [(refs[index], 0) for index in inputs]
        add_rows(outputs[2 * place], 0, arrays, base + mine * rows, rows)
        add_rows(outputs[2 * place + 1], 0, arrays, base + (1 - mine) * rows, rows)


def meet_kernel(axes, size, rows, *refs):
    low, high, gradients = refs[0:2], refs[2:4], refs[4:6]
    own_low, own_high, own_rows, first, second, third = refs[6:]
    me = lax.axis_index(axes)
    odd = me & 1
    mine = share_of(axes, [1, 2])
    zip_low, zip_high, zip_rows = [[(ref, 0) for ref in pair] for pair in (low, high, gradients)]
    keep_low = (me >> (2 - odd)) & 1
    keep_high = (me >> (1 + odd)) & 1
    add_rows(first, 0, zip_rows, (mine ^ (1 + odd)) * rows, rows)
    add_rows(first, rows, zip_low, (1 - keep_low) * size, size)
    add_rows(second, 0, zip_rows, (mine ^ (2 - odd)) * rows, rows)
    add_rows(second, rows, zip_high, (1 - keep_high) * size, size)
    add_rows(third, 0, zip_rows, (mine ^ 3) * rows, rows)
    add_rows(own_low, 0, zip_low, keep_low * size, size)
    add_rows(own_high, 0, zip_high, keep_high * size, size)
    add_rows(own_rows, 0, zip_rows, mine * rows, rows)


def sweep_kernel(spread, axes, *refs):
    *parts, out_ref, band_ref, band = refs
    added = parts[0][...]
    for part in parts[1:]:
        added = added + part[...]
    band_ref[...] = added
    width = band.shape[2]
    tiles = width // LANES
    lane_block = lax.broadcasted_iota(jnp.int32, (8, LANES), 1) // KB
    filler = jnp.zeros((8 - ROWS, LANES), jnp.float32)
    for half in range(2):
        for shift in range(4):
            start = half * 64 + shift * KB
            for tile in range(tiles):
                merged = jnp.zeros((8, LANES), jnp.float32)
                for place in range(min(8, spread - tile * 8)):
                    block = tile * 8 + place
                    piece = jnp.concatenate(
                        [band_ref[block * ROWS : (block + 1) * ROWS, :], filler], axis=0
                    )
                    moved = (place * KB - start) % LANES
                    if moved:
                        piece = pltpu.roll(piece, moved, axis=1)
                    merged = jnp.where(lane_block == place, piece, merged)
                band[shift, half * 8 : half * 8 + 8, tile * LANES : (tile + 1) * LANES] = merged
    index = {}
    for place, (m, n) in enumerate(PAIRS):
        row = place if place < ROWS else place + 3
        index[(m, n)] = row
        index[(n, m)] = row

    def row_of(shift, m, n):
        return band[shift, index[(m, n)] : index[(m, n)] + 1, :]

    ahead = [
        [jnp.concatenate([row_of(shift, m, n) for n in range(4)], axis=0) for m in range(4)]
        for shift in range(4)
    ]
    behind = [
        [pltpu.roll(ahead[shift][m], shift, axis=1) if shift else None for m in range(4)]
        for shift in range(4)
    ]
    shifted = 2.0 * smoothing + damping
    diagonal = [
        [row_of(0, row, column) + (shifted if row == column else 0.0) for column in range(4)]
        for row in range(4)
    ]
    lower, inverse = cholesky_factor(diagonal, 4)
    gradient = jnp.concatenate(
        [
            band_ref[spread * ROWS + tile * 4 : spread * ROWS + (tile + 1) * 4, :]
            for tile in range(tiles)
        ],
        axis=1,
    )
    lane = lax.broadcasted_iota(jnp.int32, (4, width), 1)
    me = lax.axis_index(axes)
    start = jnp.where(me == 0, KB, 0)
    stop = jnp.where(me == lax.axis_size(axes) - 1, (spread - 1) * KB, spread * KB)
    keep = jnp.where((lane >= start) & (lane < stop), relaxation, 0.0)
    answer = jnp.zeros((4, width), jnp.float32)
    for sweep in range(ITERS):
        misfit = gradient
        if sweep:
            moved = {}
            for shift in range(1, 4):
                moved[shift] = pltpu.roll(answer, width - shift, axis=1)
                moved[-shift] = pltpu.roll(answer, shift, axis=1)
            applied = []
            for m in range(4):
                terms = ahead[0][m] * answer
                for shift in range(1, 4):
                    terms = terms + ahead[shift][m] * moved[shift]
                    terms = terms + behind[shift][m] * moved[-shift]
                applied.append(jnp.sum(terms, axis=0, keepdims=True))
            regular = smoothing * (2.0 * answer - moved[-1] - moved[1]) + damping * answer
            misfit = gradient - regular - jnp.concatenate(applied, axis=0)
        correction = cholesky_solve(lower, inverse, [misfit[m : m + 1] for m in range(4)], 4)
        answer = answer + keep * jnp.concatenate(correction, axis=0)
    out_ref[...] = answer[:, KB : KB + out_ref.shape[1]]


def in_vmem(count):
    return [pl.BlockSpec(memory_space=pltpu.VMEM) for operand in range(count)]


def in_smem(count):
    return [pl.BlockSpec(memory_space=pltpu.SMEM) for operand in range(count)]


def work(microseconds):
    return pl.CostEstimate(flops=0, bytes_accessed=microseconds * 3_600_000, transcendentals=0)


def params(rows=0):
    return pltpu.CompilerParams(vmem_limit_bytes=min(56 << 20, (8 << 20) + 2 * rows * LANES * 4))


def call_facts(counts, attitude, owners, slots, devices):
    shape = (COUNT + 1,) + owners.shape
    return pl.pallas_call(
        functools.partial(facts_kernel, attitude.shape[1] // KB),
        out_shape=[
            jax.ShapeDtypeStruct(shape, jnp.int32),
            jax.ShapeDtypeStruct((devices,) + attitude.shape, jnp.float32),
        ],
        in_specs=in_smem(1) + in_vmem(3),
        out_specs=in_vmem(2),
        compiler_params=pltpu.CompilerParams(vmem_limit_bytes=62 << 20),
        cost_estimate=work(1),
        name="facts",
    )(counts, attitude, owners, slots)


def call_clear():
    return pl.pallas_call(
        clear_kernel,
        out_shape=jax.ShapeDtypeStruct((UNROLL, 8 * 16, LANES), jnp.float32),
        out_specs=in_vmem(1)[0],
        compiler_params=params(),
        cost_estimate=work(200),
        name="clear",
    )()


def call_normals(axes, facts, factors, phase, knot_offset, partials, clear, devices, spread):
    f32 = jnp.float32
    half = jax.ShapeDtypeStruct((devices // 2 * spread * ROWS, LANES), f32)
    blocks = devices * spread
    return pl.pallas_call(
        functools.partial(normal_kernel, axes),
        out_shape=[half, half]
        + [jax.ShapeDtypeStruct(x.shape, x.dtype) for x in (facts, phase, knot_offset, partials)],
        in_specs=in_vmem(6),
        out_specs=in_vmem(6),
        scratch_shapes=[
            pltpu.VMEM(((blocks + 1) * 8, LANES), f32),
            pltpu.VMEM((UNROLL, 8 * 16, LANES), f32),
            pltpu.VMEM((UNROLL, 16, 8, LANES), f32),
            pltpu.VMEM((UNROLL, 8, LANES), jnp.int32),
            pltpu.SMEM(facts.shape, jnp.int32),
            pltpu.SemaphoreType.DMA,
        ],
        compiler_params=params(blocks * 13),
        cost_estimate=work(100),
        name="normals",
    )(facts, factors, phase, knot_offset, partials, clear)


def call_add(axes, group, families):
    members = 1 << len(group)
    rows = sum(count for segments, count in families)
    out = jax.ShapeDtypeStruct((rows, LANES), jnp.float32)
    arrays = [pair[0] for segments, count in families for segment in segments for pair in segment]
    shapes = [
        ([[begin for array, begin in segment] for segment in segments], count)
        for segments, count in families
    ]
    return pl.pallas_call(
        functools.partial(add_kernel, axes, group, shapes),
        out_shape=[out] * members,
        in_specs=in_vmem(len(arrays)),
        out_specs=in_vmem(members),
        compiler_params=params(rows * members * 3),
        cost_estimate=work(0),
        name="shares",
    )(*arrays)


def call_cut(axes, arrays, cuts):
    outs = [
        jax.ShapeDtypeStruct((rows, LANES), jnp.float32) for inputs, base, rows, bit in cuts for half in range(2)
    ]
    return pl.pallas_call(
        functools.partial(cut_kernel, axes, cuts, len(arrays)),
        out_shape=outs,
        in_specs=in_vmem(len(arrays)),
        out_specs=in_vmem(len(outs)),
        compiler_params=params(sum(out.shape[0] for out in outs) * 3),
        cost_estimate=work(0),
        name="halves",
    )(*arrays)


def call_meet(axes, arrays, size, rows):
    counts = (size, size, rows, rows + size, rows + size, rows)
    return pl.pallas_call(
        functools.partial(meet_kernel, axes, size, rows),
        out_shape=[jax.ShapeDtypeStruct((count, LANES), jnp.float32) for count in counts],
        in_specs=in_vmem(len(arrays)),
        out_specs=in_vmem(len(counts)),
        compiler_params=params(sum(counts) * 3),
        cost_estimate=work(0),
        name="meet",
    )(*arrays)


def call_factors(facts, star_partials):
    return pl.pallas_call(
        factor_kernel,
        out_shape=jax.ShapeDtypeStruct((len(ENTRIES), 8, LANES), jnp.float32),
        in_specs=in_vmem(2),
        out_specs=in_vmem(1)[0],
        scratch_shapes=[pltpu.VMEM((len(ENTRIES), 8, LANES), jnp.float32)],
        compiler_params=params(),
        cost_estimate=work(200),
        name="factors",
    )(facts, star_partials)


def call_stars(facts, attitude, factors, phase, knot_offset, partials, star_partials, observed):
    f32 = jnp.float32
    transits, stars = phase.shape
    return pl.pallas_call(
        star_kernel,
        out_shape=[
            jax.ShapeDtypeStruct((5, stars), f32),
            jax.ShapeDtypeStruct((transits, stars), f32),
        ],
        in_specs=in_smem(1) + in_vmem(7),
        out_specs=in_vmem(2),
        scratch_shapes=[
            pltpu.VMEM((transits // 8, 32, LANES), f32),
            pltpu.VMEM((5, 8, LANES), f32),
        ],
        compiler_params=params(),
        cost_estimate=work(5),
        name="stars",
    )(facts, attitude, factors, phase, knot_offset, partials, star_partials, observed)


def call_gradients(axes, facts, phase, knot_offset, partials, second, devices, spread):
    f32 = jnp.float32
    tiles = (spread + 7) // 8
    half = jax.ShapeDtypeStruct((devices // 2 * tiles * 4, LANES), f32)
    return pl.pallas_call(
        functools.partial(gradient_kernel, axes),
        out_shape=[half, half],
        in_specs=in_smem(1) + in_vmem(4),
        out_specs=in_vmem(2),
        scratch_shapes=[
            pltpu.VMEM(((devices + 1) * tiles * 8, LANES), f32),
            pltpu.VMEM((UNROLL, 8 * 16, LANES), f32),
            pltpu.VMEM((UNROLL, 4, 8, LANES), f32),
            pltpu.VMEM((UNROLL, 8, LANES), jnp.int32),
        ],
        compiler_params=params((devices + 1) * tiles * 12),
        cost_estimate=work(5),
        name="gradients",
    )(facts, phase, knot_offset, partials, second)


def swap(arrays, group, axes, devices):
    def mask(other):
        return sum(1 << bit for place, bit in enumerate(reversed(group)) if (other >> place) & 1)

    even, odd = order_of(len(arrays) + 1)
    arrived = []
    for array, first, second in zip(arrays, even, odd):
        pairs = [(i, i ^ mask(second if i & 1 else first)) for i in range(devices)]
        arrived.append(lax.ppermute(array, axes, pairs))
    return arrived


def hop(array, bit, axes, devices):
    pairs = [(i, i ^ (1 << (3 - bit if bit and i & 1 else bit))) for i in range(devices)]
    return lax.ppermute(array, axes, pairs)


def per_device(
    attitude,
    star_partials,
    attitude_partials,
    observed,
    phase,
    knot_offset,
    cell_counts,
    interval_owner,
    block_slot,
):
    axes = ("cells", "tm")
    devices = lax.axis_size("cells") * lax.axis_size("tm")
    levels = devices.bit_length() - 1
    cells = cell_counts.shape[0]
    transits = observed.shape[0]
    blocks = attitude.shape[1] // KB
    spread = blocks + 2
    tiles = (spread + 7) // 8
    width = tiles * LANES

    owners = interval_owner.reshape(cells, transits)
    facts, wide = call_facts(cell_counts, attitude, owners, block_slot, devices)
    whole = lax.all_to_all(wide, axes, split_axis=0, concat_axis=0, tiled=True)
    bits = list(range(devices.bit_length() - 1))
    later = [bits[start : start + 2] for start in range(3, len(bits), 2)]
    groups = [bits[:1], bits[1:3]] + later
    final = later[-1]
    chunks = (spread * ROWS, tiles * 4)

    def rows(kind, group):
        return chunks[kind] * (devices >> (group[-1] + 1))

    def advance(segments, kind, group):
        kept, *sent = call_add(axes, group, [(segments, rows(kind, group))])
        return [[(array, 0) for array in [kept] + swap(sent, group, axes, devices)]]

    def turn(array, bit):
        return hop(array, bit, axes, devices)

    clear = call_clear()
    clear, facts = lax.optimization_barrier((clear, facts))
    factors = call_factors(facts, star_partials)
    kept, sent, facts, phase, knot_offset, attitude_partials = call_normals(
        axes, facts, factors, phase, knot_offset, attitude_partials, clear, devices, spread
    )
    kept, sent, whole = lax.optimization_barrier((kept, sent, whole))
    arrived = turn(sent, 0)
    star_step, second = call_stars(
        facts, whole, factors, phase, knot_offset, attitude_partials, star_partials, observed
    )
    kept, arrived, second = lax.optimization_barrier((kept, arrived, second))
    size = kept.shape[0] // 4
    halves = call_cut(
        axes, [kept, arrived], [([0, 1], 0, size, 1), ([0, 1], 2 * size, size, 2)]
    )
    second, *halves = lax.optimization_barrier((second, *halves))
    low = [halves[0], turn(halves[1], 1)]
    high = [halves[2], turn(halves[3], 2)]
    kept, sent = call_gradients(
        axes, facts, phase, knot_offset, attitude_partials, second, devices, spread
    )
    gradients = [kept, turn(sent, 0)]
    both = lax.optimization_barrier((*low, *high, *gradients))
    count = rows(1, groups[1])
    own_low, own_high, own_rows, *sent = call_meet(axes, both, size // 2, count)
    first = turn(sent[0], 2)
    second = turn(sent[1], 1)
    third = lax.ppermute(sent[2], axes, [(i, i ^ 6) for i in range(devices)])
    normals = [[(own_low, 0), (first, count)], [(own_high, 0), (second, count)]]
    gradients = [[(own_rows, 0), (first, 0), (second, 0), (third, 0)]]
    for group in later[:-1]:
        gradients = advance(gradients, 1, group)
    for group in later[:-1]:
        normals = advance(normals, 0, group)
    families = [(normals, rows(0, final)), (gradients, rows(1, final))]
    kept, *sent = call_add(axes, final, families)
    parts = [kept] + swap(sent, final, axes, devices)
    attitude_step = pl.pallas_call(
        functools.partial(sweep_kernel, spread, axes),
        out_shape=jax.ShapeDtypeStruct((4, blocks * KB), jnp.float32),
        in_specs=in_vmem(len(parts)),
        out_specs=in_vmem(1)[0],
        scratch_shapes=[
            pltpu.VMEM(kept.shape, jnp.float32),
            pltpu.VMEM((4, 16, width), jnp.float32),
        ],
        compiler_params=params(),
        cost_estimate=work(2),
        name="sweeps",
    )(*parts)
    return (star_step, attitude_step)


def solution(mesh):
    split_axes = ("cells", "tm")
    placed = (
        P(None, split_axes),
        P(None, None, split_axes),
        P(None, None, split_axes),
        P(None, split_axes),
        P(None, split_axes),
        P(None, split_axes),
        P(split_axes),
        P(split_axes, None, None),
        P(split_axes, None),
    )
    return jax.shard_map(
        per_device,
        mesh=mesh,
        in_specs=placed,
        out_specs=(P(None, split_axes), P(None, split_axes)),
        check_vma=False,
    )
```

```python
import functools

import jax
import jax.numpy as jnp
from jax import lax
from jax.experimental import pallas as pl
from jax.experimental.pallas import tpu as pltpu
from jax.sharding import PartitionSpec as P

CS = 128
KB = 16
ITERS = 6
LANES = 128
PAIRS = tuple((m, n) for m in range(4) for n in range(m, 4))
HOME, HOME_LANES, OWNER, SLOT, COUNT = range(5)
ROWS = 5
UNROLL = 8

smoothing = 16.0
damping = 2.0
relaxation = 0.5
star_prior = 1.0


def spline_basis(phase):
    square = phase * phase
    cube = square * phase
    rest = 1.0 - phase
    return (
        rest * rest * rest * (1.0 / 6.0),
        (3.0 * cube - 6.0 * square + 4.0) * (1.0 / 6.0),
        (-3.0 * cube + 3.0 * square + 3.0 * phase + 1.0) * (1.0 / 6.0),
        cube * (1.0 / 6.0),
    )


def cholesky_factor(matrix, size):
    lower = [[None for column in range(size)] for row in range(size)]
    inverse = [None for column in range(size)]
    for column in range(size):
        total = matrix[column][column]
        for inner in range(column):
            total = total - lower[column][inner] * lower[column][inner]
        inverse[column] = 1.0 / jnp.sqrt(total)
        for row in range(column + 1, size):
            accum = matrix[row][column]
            for inner in range(column):
                accum = accum - lower[row][inner] * lower[column][inner]
            lower[row][column] = accum * inverse[column]
    return lower, inverse


def cholesky_solve(lower, inverse, rhs, size):
    forward = []
    for row in range(size):
        accum = rhs[row]
        for inner in range(row):
            accum = accum - lower[row][inner] * forward[inner]
        forward.append(accum * inverse[row])
    answer = [None for row in range(size)]
    for row in reversed(range(size)):
        accum = forward[row]
        for inner in range(row + 1, size):
            accum = accum - lower[inner][row] * answer[inner]
        answer[row] = accum * inverse[row]
    return answer


def split(value):
    high = value.astype(jnp.bfloat16)
    low = (value - high.astype(jnp.float32)).astype(jnp.bfloat16)
    return high, low


def over_groups(cells, groups, body):
    def cell_body(cell, carry):
        def some(index, inner):
            for slot in range(UNROLL):
                body(cell, index * UNROLL + slot, slot)
            return inner

        return lax.fori_loop(0, groups // UNROLL, some, carry)

    lax.fori_loop(0, cells, cell_body, 0)


def pair_rows(value):
    return jnp.broadcast_to(value, (KB, LANES))


def product(weights, matrix_high, matrix_low):
    return lax.dot_general(
        weights,
        jnp.concatenate([matrix_high, matrix_low], axis=1),
        (((1,), (1,)), ((), ())),
        preferred_element_type=jnp.float32,
    )


def reversed_place(owner, levels):
    place = owner * 0
    for bit in range(levels):
        place = place * 2 + ((owner >> bit) & 1)
    return place


def band_place(owner, levels):
    bits = [(owner >> bit) & 1 for bit in range(levels)]
    differ = bits[0] ^ bits[3]
    third = bits[1] ^ (differ * (bits[1] ^ bits[2]))
    place = owner * 0
    for bit in [bits[0], bits[3], third, bits[1] ^ bits[2] ^ third] + bits[4:]:
        place = place * 2 + bit
    return place


def facts_kernel(blocks, counts, attitude_ref, owners_ref, slots_ref, facts_ref, wide_ref):
    devices = wide_ref.shape[0]
    levels = devices.bit_length() - 1
    spread = blocks + 2
    lanes = (spread + 7) // 8 * 8
    owners = owners_ref[...]
    slots = slots_ref[...]
    cells = owners.shape[0]

    facts_ref[HOME] = band_place(owners, levels) * spread + slots + 1
    facts_ref[HOME_LANES] = reversed_place(owners, levels) * lanes + slots + 1
    facts_ref[OWNER] = owners
    facts_ref[SLOT] = slots
    for cell in range(cells):
        facts_ref[COUNT, cell : cell + 1, :] = jnp.full((1, owners.shape[1]), counts[cell], jnp.int32)
    attitude = attitude_ref[...]

    def copy(index, carry):
        wide_ref[index] = attitude
        return carry

    lax.fori_loop(0, devices, copy, 0, unroll=8)


def clear_kernel(out_ref):
    out_ref[...] = jnp.zeros_like(out_ref)


def normal_kernel(
    axes,
    facts_ref,
    factors_ref,
    phase_ref,
    offset_ref,
    axis_ref,
    clear_ref,
    kept_ref,
    sent_ref,
    facts_out,
    phase_out,
    offset_out,
    axis_out,
    total,
    weights,
    basis,
    offsets,
    facts,
    semaphore,
):
    scalars = pltpu.make_async_copy(facts_ref, facts, semaphore)
    scalars.start()
    facts_out[...] = facts_ref[...]
    phase_out[...] = phase_ref[...]
    offset_out[...] = offset_ref[...]
    axis_out[...] = axis_ref[...]
    transits, stars = phase_ref.shape
    cells = stars // LANES
    knots = lax.broadcasted_iota(jnp.int32, (KB, LANES), 0)
    total[...] = jnp.zeros_like(total)
    weights[...] = clear_ref[...]
    scalars.wait()
    groups = transits // 8

    def group(cell, index, slot):
        first = pl.multiple_of(index * 8, 8)
        rows = pl.ds(first, 8)
        columns = pl.ds(pl.multiple_of(cell * LANES, LANES), LANES)
        number = first + lax.broadcasted_iota(jnp.int32, (8, LANES), 0)
        live = jnp.where(number < facts[COUNT, cell, 0], 1.0, 0.0)
        values = spline_basis(phase_ref[rows, columns])
        for shift in range(4):
            for order in range(4 - shift):
                basis[slot, shift * 4 + order] = values[order] * values[order + shift]
        offsets[slot] = offset_ref[rows, columns]
        parts = [axis_ref[m, rows, columns] for m in range(4)]
        lively = [part * live for part in parts]
        for place, (m, n) in enumerate(PAIRS):
            row = place if place < ROWS else place + 3
            weights[slot, pl.ds(row, 8, stride=16), :] = lively[m] * parts[n]
        for j in range(8):
            relative = knots - pair_rows(offsets[slot, pl.ds(j, 1), :])
            hits = [relative == order for order in range(4)]
            highs, lows = [], []
            for shift in range(4):
                piece = jnp.zeros((KB, LANES), jnp.float32)
                for order in range(4 - shift):
                    value = pair_rows(basis[slot, shift * 4 + order, pl.ds(j, 1), :])
                    piece = jnp.where(hits[order], value, piece)
                high, low = split(piece)
                highs.append(high)
                lows.append(low)
            weight_high, weight_low = split(weights[slot, pl.ds(j * 16, 16), :])
            left = jnp.concatenate([weight_high, weight_low], axis=0)
            right = jnp.concatenate([weight_high, jnp.zeros_like(weight_low)], axis=0)
            result = product(
                jnp.concatenate([left, right], axis=1),
                jnp.concatenate(highs, axis=0),
                jnp.concatenate(lows, axis=0),
            )
            band = jnp.concatenate(
                [result[0:8] + result[16:24], result[8:16] + result[24:32]], axis=1
            )
            block = pl.ds(pl.multiple_of(facts[HOME, cell, first + j] * 8, 8), 8)
            total[block, :] = total[block, :] + band

    over_groups(cells, groups, group)

    levels = lax.axis_size(axes).bit_length() - 1
    places = [band_place(owner, levels) for owner in range(1 << levels)]
    spread = total.shape[0] // 8 // len(places)
    for lower, upper in zip(places[:-1], places[1:]):
        start, stop = upper * spread * 8, (lower + 1) * spread * 8
        total[start : start + 8, :] = total[stop - 16 : stop - 8, :]
        total[stop - 8 : stop, :] = total[start + 8 : start + 16, :]
    mine = lax.axis_index(axes) & 1
    half = kept_ref.shape[0] // ROWS * 8

    def pack(index, carry):
        target = pl.multiple_of(index * 8 * ROWS, 8)
        for out_ref, part in ((kept_ref, mine), (sent_ref, 1 - mine)):
            source = pl.multiple_of(part * half + index * 64, 64)
            for j in range(8):
                out_ref[pl.ds(target + j * ROWS, ROWS), :] = total[pl.ds(source + j * 8, ROWS), :]
        return carry

    lax.fori_loop(0, half // 64, pack, 0)


ENTRIES = tuple((row, column) for row in range(5) for column in range(row + 1))


def factor_kernel(facts_ref, star_ref, factors_ref, sums):
    transits, stars = star_ref.shape[1:]
    sums[...] = jnp.zeros_like(sums)

    for cell in range(stars // LANES):
        columns = pl.ds(cell * LANES, LANES)
        count = facts_ref[COUNT, cell : cell + 1, :]
        count = jnp.concatenate([count] * (LANES // transits), axis=1)
        count = jnp.broadcast_to(count, (8, LANES))

        def add(index, accumulated, columns=columns, count=count):
            first = pl.multiple_of(index * 8, 8)
            number = first + lax.broadcasted_iota(jnp.int32, (8, LANES), 0)
            live = jnp.where(number < count, 1.0, 0.0)
            parts = [star_ref[row, pl.ds(first, 8), columns] for row in range(5)]
            lively = [part * live for part in parts]
            return tuple(
                old + lively[row] * parts[column] for old, (row, column) in zip(accumulated, ENTRIES)
            )

        start = tuple(jnp.zeros((8, LANES), jnp.float32) for entry in ENTRIES)
        accumulated = lax.fori_loop(0, transits // 8, add, start, unroll=4)
        for entry in range(len(ENTRIES)):
            sums[entry, pl.ds(cell, 1), :] = jnp.sum(accumulated[entry], axis=0, keepdims=True)
    normal = [[None for column in range(5)] for row in range(5)]
    for entry, (row, column) in enumerate(ENTRIES):
        normal[row][column] = sums[entry] + (star_prior if row == column else 0.0)
    lower, inverse = cholesky_factor(normal, 5)
    for entry, (row, column) in enumerate(ENTRIES):
        factors_ref[entry] = inverse[row] if row == column else lower[row][column]


def star_kernel(
    facts,
    attitude_ref,
    factors_ref,
    phase_ref,
    offset_ref,
    axis_ref,
    star_ref,
    observed_ref,
    step_ref,
    second_ref,
    table,
    sums,
):
    transits, stars = phase_ref.shape
    cells = stars // LANES
    groups = transits // 8
    sums[...] = jnp.zeros_like(sums)
    sublane = lax.broadcasted_iota(jnp.int32, (8, LANES), 0)

    def predict_cell(cell, carry):
        columns = pl.ds(pl.multiple_of(cell * LANES, LANES), LANES)

        def predict(index, accumulated):
            first = pl.multiple_of(index * 8, 8)
            rows = pl.ds(first, 8)
            shift = jnp.zeros((8, LANES), jnp.int32)
            for j in range(8):
                owner = facts[OWNER, cell, first + j]
                slot = facts[SLOT, cell, first + j]
                column = pl.multiple_of((slot >> 3) * LANES, LANES)
                table[index, pl.ds(j, 4, stride=8), :] = attitude_ref[owner, :, pl.ds(column, LANES)]
                shift = jnp.where(sublane == j, (slot & 7) * KB, shift)
            number = first + lax.broadcasted_iota(jnp.int32, (8, LANES), 0)
            live = jnp.where(number < facts[COUNT, cell, 0], 1.0, 0.0)
            values = spline_basis(phase_ref[rows, columns])
            offset = offset_ref[rows, columns] + shift
            places = [offset + order for order in range(4)]
            predicted = jnp.zeros((8, LANES), jnp.float32)
            for m in range(4):
                spline = jnp.zeros((8, LANES), jnp.float32)
                looked = table[index, m * 8 : m * 8 + 8, :]
                for order in range(4):
                    found = jnp.take_along_axis(looked, places[order], axis=1)
                    spline = spline + found * values[order]
                predicted = predicted + spline * axis_ref[m, rows, columns]
            first_value = live * (observed_ref[rows, columns] - predicted)
            second_ref[rows, columns] = first_value
            parts = [star_ref[row, rows, columns] for row in range(5)]
            return tuple(old + part * first_value for old, part in zip(accumulated, parts))

        start = tuple(jnp.zeros((8, LANES), jnp.float32) for row in range(5))
        accumulated = lax.fori_loop(0, groups, predict, start, unroll=8)
        for entry in range(5):
            sums[entry, pl.ds(cell, 1), :] = jnp.sum(accumulated[entry], axis=0, keepdims=True)
        return carry

    lax.fori_loop(0, cells, predict_cell, 0)

    lower = [[None for column in range(5)] for row in range(5)]
    for entry, (row, column) in enumerate(ENTRIES):
        lower[row][column] = factors_ref[entry]
    inverse = [lower[row][row] for row in range(5)]
    answer = cholesky_solve(lower, inverse, [sums[row] for row in range(5)], 5)
    for row in range(5):
        sums[row] = answer[row]
        for cell in range(cells):
            step_ref[row : row + 1, cell * LANES : (cell + 1) * LANES] = answer[row][
                cell : cell + 1
            ]

    def correct(cell, carry):
        columns = pl.ds(pl.multiple_of(cell * LANES, LANES), LANES)
        own = [jnp.broadcast_to(sums[row, pl.ds(cell, 1), :], (8, LANES)) for row in range(5)]
        for index in range(groups):
            rows = pl.ds(index * 8, 8)
            number = index * 8 + sublane
            live = jnp.where(number < facts[COUNT, cell, 0], 1.0, 0.0)
            fitted = star_ref[0, rows, columns] * own[0]
            for row in range(1, 5):
                fitted = fitted + star_ref[row, rows, columns] * own[row]
            second_ref[rows, columns] = second_ref[rows, columns] - live * fitted
        return carry

    lax.fori_loop(0, cells, correct, 0)


def gradient_kernel(
    axes,
    facts_ref,
    phase_ref,
    offset_ref,
    axis_ref,
    second_ref,
    step_ref,
    kept_ref,
    sent_ref,
    step_hbm,
    total,
    weights,
    basis,
    offsets,
    facts,
    semaphores,
):
    scalars = pltpu.make_async_copy(facts_ref, facts, semaphores.at[0])
    scalars.start()
    result_copy = pltpu.make_async_copy(step_ref, step_hbm, semaphores.at[1])
    result_copy.start()
    transits, stars = phase_ref.shape
    cells = stars // LANES
    groups = transits // 8
    knots = lax.broadcasted_iota(jnp.int32, (KB, LANES), 0)
    lanes_block = lax.broadcasted_iota(jnp.int32, (8, LANES), 1) // KB
    total[...] = jnp.zeros_like(total)
    weights[...] = jnp.zeros_like(weights)
    scalars.wait()

    def group(cell, index, slot):
        first = pl.multiple_of(index * 8, 8)
        rows = pl.ds(first, 8)
        columns = pl.ds(pl.multiple_of(cell * LANES, LANES), LANES)
        second = second_ref[rows, columns]
        for m in range(4):
            value = axis_ref[m, rows, columns] * second
            high = value.astype(jnp.bfloat16).astype(jnp.float32)
            weights[slot, pl.ds(m, 8, stride=16), :] = high
            weights[slot, pl.ds(4 + m, 8, stride=16), :] = value - high
        values = spline_basis(phase_ref[rows, columns])
        for order in range(4):
            basis[slot, order] = values[order]
        offsets[slot] = offset_ref[rows, columns]
        for j in range(8):
            relative = knots - pair_rows(offsets[slot, pl.ds(j, 1), :])
            piece = jnp.zeros((KB, LANES), jnp.float32)
            for order in range(4):
                value = pair_rows(basis[slot, order, pl.ds(j, 1), :])
                piece = jnp.where(relative == order, value, piece)
            high, low = split(piece)
            weight = weights[slot, pl.ds(j * 16, 16), :]
            right = jnp.where(knots < 4, weight, 0.0)
            result = product(
                jnp.concatenate([weight, right], axis=1).astype(jnp.bfloat16),
                jnp.concatenate([high] * 4, axis=0),
                jnp.concatenate([low] * 4, axis=0),
            )[0:8]
            result = jnp.concatenate([result, result], axis=1)
            place = facts[HOME_LANES, cell, first + j]
            chosen = jnp.where(lanes_block == (place & 7), result, 0.0)
            block = pl.ds(pl.multiple_of((place >> 3) * 8, 8), 8)
            total[block, :] = total[block, :] + chosen

    over_groups(cells, groups, group)

    levels = lax.axis_size(axes).bit_length() - 1
    places = [reversed_place(owner, levels) for owner in range(1 << levels)]
    rows = total.shape[0] // len(places)
    for lower, upper in zip(places[:-1], places[1:]):
        start, stop = upper * rows, (lower + 1) * rows
        ending, opening = total[stop - 8 : stop, :], total[start : start + 8, :]
        total[start : start + 8, :] = opening + jnp.where(lanes_block == 0, ending, 0.0)
        total[stop - 8 : stop, :] = ending + jnp.where(lanes_block == 1, opening, 0.0)
    mine = lax.axis_index(axes) & 1
    half = kept_ref.shape[0] * 2

    def pack(index, carry):
        target = pl.multiple_of(index * 8, 8)
        for out_ref, part in ((kept_ref, mine), (sent_ref, 1 - mine)):
            source = pl.multiple_of(part * half + index * 16, 16)
            for j in range(2):
                tile = total[pl.ds(source + j * 8, 8), :]
                out_ref[pl.ds(target + j * 4, 4), :] = tile[0:4] + tile[4:8]
        return carry

    lax.fori_loop(0, half // 16, pack, 0)
    result_copy.wait()


def share_of(axes, group):
    me = lax.axis_index(axes)
    mine = 0
    for bit in group:
        mine = mine * 2 + ((me >> bit) & 1)
    return mine


def add_rows(out_ref, base, inputs, start, rows):
    step = 40 if rows % 40 == 0 else rows

    def add(index, carry):
        terms = [ref[pl.ds(offset + start + index * step, step), :] for ref, offset in inputs]
        added = terms[0]
        for term in terms[1:]:
            added = added + term
        out_ref[pl.ds(base + index * step, step), :] = added
        return carry

    if step == rows:
        add(0, 0)
    else:
        lax.fori_loop(0, rows // step, add, 0)


def order_of(members):
    return {2: ((1,), (1,)), 4: ((3, 2, 1), (1, 3, 2))}[members]


def add_kernel(axes, group, families, *refs):
    mine = share_of(axes, group)
    members = 1 << len(group)
    odd = lax.axis_index(axes) & 1
    others = [0] + [jnp.where(odd == 1, second, first) for first, second in zip(*order_of(members))]
    outputs = refs[-members:]
    first = 0
    base = 0
    for offsets, rows in families:
        segments = []
        for begins in offsets:
            segments.append(list(zip(refs[first : first + len(begins)], begins)))
            first += len(begins)
        within = members // len(segments)
        for other, out_ref in zip(others, outputs):
            which = mine ^ other
            for number, inputs in enumerate(segments):
                if len(segments) == 1:
                    add_rows(out_ref, base, inputs, which * rows, rows)
                else:

                    @pl.when(which // within == number)
                    def _(out_ref=out_ref, inputs=inputs, which=which, base=base, rows=rows):
                        add_rows(out_ref, base, inputs, (which % within) * rows, rows)

        base += rows


def cut_kernel(axes, cuts, count, *refs):
    me = lax.axis_index(axes)
    odd = me & 1
    outputs = refs[count:]
    for place, (inputs, base, rows, bit) in enumerate(cuts):
        mine = (me >> jnp.where(odd == 1, 3 - bit, bit)) & 1
        arrays = [(refs[index], 0) for index in inputs]
        add_rows(outputs[2 * place], 0, arrays, base + mine * rows, rows)
        add_rows(outputs[2 * place + 1], 0, arrays, base + (1 - mine) * rows, rows)


def meet_kernel(axes, size, rows, *refs):
    low, high, gradients = refs[0:2], refs[2:4], refs[4:6]
    own_low, own_high, own_rows, first, second, third = refs[6:]
    me = lax.axis_index(axes)
    odd = me & 1
    mine = share_of(axes, [1, 2])
    zip_low, zip_high, zip_rows = [[(ref, 0) for ref in pair] for pair in (low, high, gradients)]
    keep_low = (me >> (2 - odd)) & 1
    keep_high = (me >> (1 + odd)) & 1
    add_rows(first, 0, zip_rows, (mine ^ (1 + odd)) * rows, rows)
    add_rows(first, rows, zip_low, (1 - keep_low) * size, size)
    add_rows(second, 0, zip_rows, (mine ^ (2 - odd)) * rows, rows)
    add_rows(second, rows, zip_high, (1 - keep_high) * size, size)
    add_rows(third, 0, zip_rows, (mine ^ 3) * rows, rows)
    add_rows(own_low, 0, zip_low, keep_low * size, size)
    add_rows(own_high, 0, zip_high, keep_high * size, size)
    add_rows(own_rows, 0, zip_rows, mine * rows, rows)


def sweep_kernel(spread, axes, *refs):
    *parts, out_ref, band_ref, band = refs
    added = parts[0][...]
    for part in parts[1:]:
        added = added + part[...]
    band_ref[...] = added
    width = band.shape[2]
    tiles = width // LANES
    lane_block = lax.broadcasted_iota(jnp.int32, (8, LANES), 1) // KB
    filler = jnp.zeros((8 - ROWS, LANES), jnp.float32)
    for half in range(2):
        for shift in range(4):
            start = half * 64 + shift * KB
            for tile in range(tiles):
                merged = jnp.zeros((8, LANES), jnp.float32)
                for place in range(min(8, spread - tile * 8)):
                    block = tile * 8 + place
                    piece = jnp.concatenate(
                        [band_ref[block * ROWS : (block + 1) * ROWS, :], filler], axis=0
                    )
                    moved = (place * KB - start) % LANES
                    if moved:
                        piece = pltpu.roll(piece, moved, axis=1)
                    merged = jnp.where(lane_block == place, piece, merged)
                band[shift, half * 8 : half * 8 + 8, tile * LANES : (tile + 1) * LANES] = merged
    index = {}
    for place, (m, n) in enumerate(PAIRS):
        row = place if place < ROWS else place + 3
        index[(m, n)] = row
        index[(n, m)] = row

    def row_of(shift, m, n):
        return band[shift, index[(m, n)] : index[(m, n)] + 1, :]

    def square(entry):
        return jnp.concatenate([entry(m, n) for m in range(4) for n in range(4)], axis=0)

    diagonal = [
        [
            row_of(0, row, column) + (2.0 * smoothing + damping if row == column else 0.0)
            for column in range(4)
        ]
        for row in range(4)
    ]
    lower, inverse = cholesky_factor(diagonal, 4)
    one = jnp.ones((1, width), jnp.float32)
    zero = jnp.zeros((1, width), jnp.float32)
    columns = [
        cholesky_solve(lower, inverse, [one if row == column else zero for row in range(4)], 4)
        for column in range(4)
    ]
    solve = square(lambda m, n: columns[n][m])
    sublane = lax.broadcasted_iota(jnp.int32, (16, width), 0)
    same = (sublane >> 2) == (sublane & 3)
    operator = {0: square(lambda m, n: diagonal[m][n])}
    for shift in range(1, 4):
        ahead = square(lambda m, n: row_of(shift, m, n))
        operator[shift] = ahead
        operator[-shift] = pltpu.roll(ahead, shift, axis=1)
    for shift in (1, -1):
        operator[shift] = operator[shift] - jnp.where(same, smoothing, 0.0)
    own = jnp.concatenate(
        [
            band_ref[spread * ROWS + tile * 4 : spread * ROWS + (tile + 1) * 4, :]
            for tile in range(tiles)
        ],
        axis=1,
    )
    gradient = square(lambda m, n: own[m : m + 1])
    lane = lax.broadcasted_iota(jnp.int32, (8, width), 1)
    me = lax.axis_index(axes)
    start = jnp.where(me == 0, KB, 0)
    stop = jnp.where(me == lax.axis_size(axes) - 1, (spread - 1) * KB, spread * KB)
    keep = jnp.where((lane >= start) & (lane < stop), relaxation, 0.0)
    place = lax.broadcasted_iota(jnp.int32, (8, width), 0)
    odd = (place & 1) == 1
    late = (place & 2) == 2

    def over_columns(value):
        value = value + jnp.where(odd, pltpu.roll(value, 1, axis=0), pltpu.roll(value, 7, axis=0))
        return value + jnp.where(late, pltpu.roll(value, 2, axis=0), pltpu.roll(value, 6, axis=0))

    answer = jnp.zeros((8, width), jnp.float32)
    for sweep in range(ITERS):
        misfit = [gradient[0:8], gradient[8:16]]
        if sweep:
            moved = {0: answer}
            for shift in range(1, 4):
                moved[shift] = pltpu.roll(answer, width - shift, axis=1)
                moved[-shift] = pltpu.roll(answer, shift, axis=1)
            for half in range(2):
                rows = slice(half * 8, half * 8 + 8)
                terms = [operator[shift][rows] * moved[shift] for shift in range(-3, 4)]
                applied = ((terms[0] + terms[1]) + (terms[2] + terms[3])) + (
                    (terms[4] + terms[5]) + terms[6]
                )
                misfit[half] = misfit[half] - over_columns(applied)
        correction = solve[0:8] * misfit[0] + solve[8:16] * misfit[1]
        correction = correction + pltpu.roll(correction, 4, axis=0)
        answer = answer + keep * correction
    out_ref[...] = answer[0:4, KB : KB + out_ref.shape[1]]


def in_vmem(count):
    return [pl.BlockSpec(memory_space=pltpu.VMEM) for operand in range(count)]


def in_smem(count):
    return [pl.BlockSpec(memory_space=pltpu.SMEM) for operand in range(count)]


def work(microseconds):
    return pl.CostEstimate(flops=0, bytes_accessed=microseconds * 3_600_000, transcendentals=0)


def params(rows=0):
    return pltpu.CompilerParams(vmem_limit_bytes=min(56 << 20, (8 << 20) + 2 * rows * LANES * 4))


def call_facts(counts, attitude, owners, slots, devices):
    shape = (COUNT + 1,) + owners.shape
    return pl.pallas_call(
        functools.partial(facts_kernel, attitude.shape[1] // KB),
        out_shape=[
            jax.ShapeDtypeStruct(shape, jnp.int32),
            jax.ShapeDtypeStruct((devices,) + attitude.shape, jnp.float32),
        ],
        in_specs=in_smem(1) + in_vmem(3),
        out_specs=in_vmem(2),
        compiler_params=pltpu.CompilerParams(vmem_limit_bytes=62 << 20),
        cost_estimate=work(1),
        name="facts",
    )(counts, attitude, owners, slots)


def call_clear():
    return pl.pallas_call(
        clear_kernel,
        out_shape=jax.ShapeDtypeStruct((UNROLL, 8 * 16, LANES), jnp.float32),
        out_specs=in_vmem(1)[0],
        compiler_params=params(),
        cost_estimate=work(200),
        name="clear",
    )()


def call_normals(axes, facts, factors, phase, knot_offset, partials, clear, devices, spread):
    f32 = jnp.float32
    half = jax.ShapeDtypeStruct((devices // 2 * spread * ROWS, LANES), f32)
    blocks = devices * spread
    return pl.pallas_call(
        functools.partial(normal_kernel, axes),
        out_shape=[half, half]
        + [jax.ShapeDtypeStruct(x.shape, x.dtype) for x in (facts, phase, knot_offset, partials)],
        in_specs=in_vmem(6),
        out_specs=in_vmem(6),
        scratch_shapes=[
            pltpu.VMEM((blocks * 8, LANES), f32),
            pltpu.VMEM((UNROLL, 8 * 16, LANES), f32),
            pltpu.VMEM((UNROLL, 16, 8, LANES), f32),
            pltpu.VMEM((UNROLL, 8, LANES), jnp.int32),
            pltpu.SMEM(facts.shape, jnp.int32),
            pltpu.SemaphoreType.DMA,
        ],
        compiler_params=params(blocks * 13),
        cost_estimate=work(100),
        name="normals",
    )(facts, factors, phase, knot_offset, partials, clear)


def call_add(axes, group, families):
    members = 1 << len(group)
    rows = sum(count for segments, count in families)
    out = jax.ShapeDtypeStruct((rows, LANES), jnp.float32)
    arrays = [pair[0] for segments, count in families for segment in segments for pair in segment]
    shapes = [
        ([[begin for array, begin in segment] for segment in segments], count)
        for segments, count in families
    ]
    return pl.pallas_call(
        functools.partial(add_kernel, axes, group, shapes),
        out_shape=[out] * members,
        in_specs=in_vmem(len(arrays)),
        out_specs=in_vmem(members),
        compiler_params=params(rows * members * 3),
        cost_estimate=work(0),
        name="shares",
    )(*arrays)


def call_cut(axes, arrays, cuts):
    outs = [
        jax.ShapeDtypeStruct((rows, LANES), jnp.float32) for inputs, base, rows, bit in cuts for half in range(2)
    ]
    return pl.pallas_call(
        functools.partial(cut_kernel, axes, cuts, len(arrays)),
        out_shape=outs,
        in_specs=in_vmem(len(arrays)),
        out_specs=in_vmem(len(outs)),
        compiler_params=params(sum(out.shape[0] for out in outs) * 3),
        cost_estimate=work(0),
        name="halves",
    )(*arrays)


def call_meet(axes, arrays, size, rows):
    counts = (size, size, rows, rows + size, rows + size, rows)
    return pl.pallas_call(
        functools.partial(meet_kernel, axes, size, rows),
        out_shape=[jax.ShapeDtypeStruct((count, LANES), jnp.float32) for count in counts],
        in_specs=in_vmem(len(arrays)),
        out_specs=in_vmem(len(counts)),
        compiler_params=params(sum(counts) * 3),
        cost_estimate=work(0),
        name="meet",
    )(*arrays)


def call_factors(facts, star_partials):
    return pl.pallas_call(
        factor_kernel,
        out_shape=jax.ShapeDtypeStruct((len(ENTRIES), 8, LANES), jnp.float32),
        in_specs=in_vmem(2),
        out_specs=in_vmem(1)[0],
        scratch_shapes=[pltpu.VMEM((len(ENTRIES), 8, LANES), jnp.float32)],
        compiler_params=params(),
        cost_estimate=work(200),
        name="factors",
    )(facts, star_partials)


def call_stars(facts, attitude, factors, phase, knot_offset, partials, star_partials, observed):
    f32 = jnp.float32
    transits, stars = phase.shape
    return pl.pallas_call(
        star_kernel,
        out_shape=[
            jax.ShapeDtypeStruct((5, stars), f32),
            jax.ShapeDtypeStruct((transits, stars), f32),
        ],
        in_specs=in_smem(1) + in_vmem(7),
        out_specs=in_vmem(2),
        scratch_shapes=[
            pltpu.VMEM((transits // 8, 32, LANES), f32),
            pltpu.VMEM((5, 8, LANES), f32),
        ],
        compiler_params=params(),
        cost_estimate=work(5),
        name="stars",
    )(facts, attitude, factors, phase, knot_offset, partials, star_partials, observed)


def call_gradients(axes, facts, phase, knot_offset, partials, second, step, devices, spread):
    f32 = jnp.float32
    tiles = (spread + 7) // 8
    half = jax.ShapeDtypeStruct((devices // 2 * tiles * 4, LANES), f32)
    return pl.pallas_call(
        functools.partial(gradient_kernel, axes),
        out_shape=[half, half, jax.ShapeDtypeStruct(step.shape, f32)],
        in_specs=in_vmem(6),
        out_specs=in_vmem(2) + [pl.BlockSpec(memory_space=pltpu.HBM)],
        scratch_shapes=[
            pltpu.VMEM((devices * tiles * 8, LANES), f32),
            pltpu.VMEM((UNROLL, 8 * 16, LANES), f32),
            pltpu.VMEM((UNROLL, 4, 8, LANES), f32),
            pltpu.VMEM((UNROLL, 8, LANES), jnp.int32),
            pltpu.SMEM(facts.shape, jnp.int32),
            pltpu.SemaphoreType.DMA((2,)),
        ],
        compiler_params=params((devices + 1) * tiles * 12),
        cost_estimate=work(5),
        name="gradients",
    )(facts, phase, knot_offset, partials, second, step)


def swap(arrays, group, axes, devices):
    def mask(other):
        return sum(1 << bit for place, bit in enumerate(reversed(group)) if (other >> place) & 1)

    even, odd = order_of(len(arrays) + 1)
    arrived = []
    for array, first, second in zip(arrays, even, odd):
        pairs = [(i, i ^ mask(second if i & 1 else first)) for i in range(devices)]
        arrived.append(lax.ppermute(array, axes, pairs))
    return arrived


def hop(array, bit, axes, devices):
    pairs = [(i, i ^ (1 << (3 - bit if bit and i & 1 else bit))) for i in range(devices)]
    return lax.ppermute(array, axes, pairs)


def per_device(
    attitude,
    star_partials,
    attitude_partials,
    observed,
    phase,
    knot_offset,
    cell_counts,
    interval_owner,
    block_slot,
):
    axes = ("cells", "tm")
    devices = lax.axis_size("cells") * lax.axis_size("tm")
    levels = devices.bit_length() - 1
    cells = cell_counts.shape[0]
    transits = observed.shape[0]
    blocks = attitude.shape[1] // KB
    spread = blocks + 2
    tiles = (spread + 7) // 8
    width = tiles * LANES

    owners = interval_owner.reshape(cells, transits)
    facts, wide = call_facts(cell_counts, attitude, owners, block_slot, devices)
    whole = lax.all_to_all(wide, axes, split_axis=0, concat_axis=0, tiled=True)
    bits = list(range(devices.bit_length() - 1))
    later = [bits[start : start + 2] for start in range(3, len(bits), 2)]
    groups = [bits[:1], bits[1:3]] + later
    final = later[-1]
    chunks = (spread * ROWS, tiles * 4)

    def rows(kind, group):
        return chunks[kind] * (devices >> (group[-1] + 1))

    def advance(segments, kind, group):
        kept, *sent = call_add(axes, group, [(segments, rows(kind, group))])
        return [[(array, 0) for array in [kept] + swap(sent, group, axes, devices)]]

    def turn(array, bit):
        return hop(array, bit, axes, devices)

    clear = call_clear()
    clear, facts = lax.optimization_barrier((clear, facts))
    factors = call_factors(facts, star_partials)
    kept, sent, facts, phase, knot_offset, attitude_partials = call_normals(
        axes, facts, factors, phase, knot_offset, attitude_partials, clear, devices, spread
    )
    kept, sent, whole = lax.optimization_barrier((kept, sent, whole))
    arrived = turn(sent, 0)
    step, second = call_stars(
        facts, whole, factors, phase, knot_offset, attitude_partials, star_partials, observed
    )
    kept, arrived, second = lax.optimization_barrier((kept, arrived, second))
    size = kept.shape[0] // 4
    halves = call_cut(
        axes, [kept, arrived], [([0, 1], 0, size, 1), ([0, 1], 2 * size, size, 2)]
    )
    second, *halves = lax.optimization_barrier((second, *halves))
    low = [halves[0], turn(halves[1], 1)]
    high = [halves[2], turn(halves[3], 2)]
    kept, sent, star_step = call_gradients(
        axes, facts, phase, knot_offset, attitude_partials, second, step, devices, spread
    )
    gradients = [kept, turn(sent, 0)]
    both = lax.optimization_barrier((*low, *high, *gradients))
    count = rows(1, groups[1])
    own_low, own_high, own_rows, *sent = call_meet(axes, both, size // 2, count)
    first = turn(sent[0], 2)
    second = turn(sent[1], 1)
    third = lax.ppermute(sent[2], axes, [(i, i ^ 6) for i in range(devices)])
    normals = [[(own_low, 0), (first, count)], [(own_high, 0), (second, count)]]
    gradients = [[(own_rows, 0), (first, 0), (second, 0), (third, 0)]]
    for group in later[:-1]:
        gradients = advance(gradients, 1, group)
    for group in later[:-1]:
        normals = advance(normals, 0, group)
    families = [(normals, rows(0, final)), (gradients, rows(1, final))]
    kept, *sent = call_add(axes, final, families)
    parts = [kept] + swap(sent, final, axes, devices)
    attitude_step = pl.pallas_call(
        functools.partial(sweep_kernel, spread, axes),
        out_shape=jax.ShapeDtypeStruct((4, blocks * KB), jnp.float32),
        in_specs=in_vmem(len(parts)),
        out_specs=in_vmem(1)[0],
        scratch_shapes=[
            pltpu.VMEM(kept.shape, jnp.float32),
            pltpu.VMEM((4, 16, width), jnp.float32),
        ],
        compiler_params=params(),
        cost_estimate=work(2),
        name="sweeps",
    )(*parts)
    return (star_step, attitude_step)


def solution(mesh):
    split_axes = ("cells", "tm")
    placed = (
        P(None, split_axes),
        P(None, None, split_axes),
        P(None, None, split_axes),
        P(None, split_axes),
        P(None, split_axes),
        P(None, split_axes),
        P(split_axes),
        P(split_axes, None, None),
        P(split_axes, None),
    )
    return jax.shard_map(
        per_device,
        mesh=mesh,
        in_specs=placed,
        out_specs=(P(None, split_axes), P(None, split_axes)),
        check_vma=False,
    )
```

```python
import functools

import jax
import jax.numpy as jnp
from jax import lax
from jax.experimental import pallas as pl
from jax.experimental.pallas import tpu as pltpu
from jax.sharding import PartitionSpec as P

CS = 128
KB = 16
ITERS = 6
LANES = 128
PAIRS = tuple((m, n) for m in range(4) for n in range(m, 4))
HOME, HOME_LANES, OWNER, SLOT, COUNT = range(5)
ROWS = 5
UNROLL = 8

smoothing = 16.0
damping = 2.0
relaxation = 0.5
star_prior = 1.0


def spline_basis(phase):
    square = phase * phase
    cube = square * phase
    rest = 1.0 - phase
    return (
        rest * rest * rest * (1.0 / 6.0),
        (3.0 * cube - 6.0 * square + 4.0) * (1.0 / 6.0),
        (-3.0 * cube + 3.0 * square + 3.0 * phase + 1.0) * (1.0 / 6.0),
        cube * (1.0 / 6.0),
    )


def cholesky_factor(matrix, size):
    lower = [[None for column in range(size)] for row in range(size)]
    inverse = [None for column in range(size)]
    for column in range(size):
        total = matrix[column][column]
        for inner in range(column):
            total = total - lower[column][inner] * lower[column][inner]
        inverse[column] = 1.0 / jnp.sqrt(total)
        for row in range(column + 1, size):
            accum = matrix[row][column]
            for inner in range(column):
                accum = accum - lower[row][inner] * lower[column][inner]
            lower[row][column] = accum * inverse[column]
    return lower, inverse


def cholesky_solve(lower, inverse, rhs, size):
    forward = []
    for row in range(size):
        accum = rhs[row]
        for inner in range(row):
            accum = accum - lower[row][inner] * forward[inner]
        forward.append(accum * inverse[row])
    answer = [None for row in range(size)]
    for row in reversed(range(size)):
        accum = forward[row]
        for inner in range(row + 1, size):
            accum = accum - lower[inner][row] * answer[inner]
        answer[row] = accum * inverse[row]
    return answer


def split(value):
    high = value.astype(jnp.bfloat16)
    low = (value - high.astype(jnp.float32)).astype(jnp.bfloat16)
    return high, low


def over_groups(cells, groups, body):
    def cell_body(cell, carry):
        def some(index, inner):
            for slot in range(UNROLL):
                body(cell, index * UNROLL + slot, slot)
            return inner

        return lax.fori_loop(0, groups // UNROLL, some, carry)

    lax.fori_loop(0, cells, cell_body, 0)


def pair_rows(value):
    return jnp.broadcast_to(value, (KB, LANES))


def product(weights, matrix_high, matrix_low):
    return lax.dot_general(
        weights,
        jnp.concatenate([matrix_high, matrix_low], axis=1),
        (((1,), (1,)), ((), ())),
        preferred_element_type=jnp.float32,
    )


def reversed_place(owner, levels):
    place = owner * 0
    for bit in range(levels):
        place = place * 2 + ((owner >> bit) & 1)
    return place


def band_place(owner, levels):
    bits = [(owner >> bit) & 1 for bit in range(levels)]
    differ = bits[0] ^ bits[3]
    third = bits[1] ^ (differ * (bits[1] ^ bits[2]))
    place = owner * 0
    for bit in [bits[0], bits[3], third, bits[1] ^ bits[2] ^ third] + bits[4:]:
        place = place * 2 + bit
    return place


def facts_kernel(blocks, counts, attitude_ref, owners_ref, slots_ref, facts_ref, wide_ref):
    devices = wide_ref.shape[0]
    levels = devices.bit_length() - 1
    spread = blocks + 2
    lanes = (spread + 7) // 8 * 8
    owners = owners_ref[...]
    slots = slots_ref[...]
    cells = owners.shape[0]

    facts_ref[HOME] = band_place(owners, levels) * spread + slots + 1
    facts_ref[HOME_LANES] = reversed_place(owners, levels) * lanes + slots + 1
    facts_ref[OWNER] = owners
    facts_ref[SLOT] = slots
    for cell in range(cells):
        facts_ref[COUNT, cell : cell + 1, :] = jnp.full((1, owners.shape[1]), counts[cell], jnp.int32)
    attitude = attitude_ref[...]

    def copy(index, carry):
        wide_ref[index] = attitude
        return carry

    lax.fori_loop(0, devices, copy, 0, unroll=8)


def clear_kernel(out_ref):
    out_ref[...] = jnp.zeros_like(out_ref)


def normal_kernel(
    axes,
    facts_ref,
    factors_ref,
    phase_ref,
    offset_ref,
    axis_ref,
    clear_ref,
    kept_ref,
    sent_ref,
    facts_out,
    phase_out,
    offset_out,
    axis_out,
    total,
    weights,
    basis,
    offsets,
    facts,
    semaphore,
):
    scalars = pltpu.make_async_copy(facts_ref, facts, semaphore)
    scalars.start()
    facts_out[...] = facts_ref[...]
    phase_out[...] = phase_ref[...]
    offset_out[...] = offset_ref[...]
    axis_out[...] = axis_ref[...]
    transits, stars = phase_ref.shape
    cells = stars // LANES
    knots = lax.broadcasted_iota(jnp.int32, (KB, LANES), 0)
    total[...] = jnp.zeros_like(total)
    weights[...] = clear_ref[...]
    scalars.wait()
    groups = transits // 8

    def group(cell, index, slot):
        first = pl.multiple_of(index * 8, 8)
        rows = pl.ds(first, 8)
        columns = pl.ds(pl.multiple_of(cell * LANES, LANES), LANES)
        number = first + lax.broadcasted_iota(jnp.int32, (8, LANES), 0)
        live = jnp.where(number < facts[COUNT, cell, 0], 1.0, 0.0)
        values = spline_basis(phase_ref[rows, columns])
        for shift in range(4):
            for order in range(4 - shift):
                basis[slot, shift * 4 + order] = values[order] * values[order + shift]
        offsets[slot] = offset_ref[rows, columns]
        parts = [axis_ref[m, rows, columns] for m in range(4)]
        lively = [part * live for part in parts]
        for place, (m, n) in enumerate(PAIRS):
            row = place if place < ROWS else place + 3
            weights[slot, pl.ds(row, 8, stride=16), :] = lively[m] * parts[n]
        for j in range(8):
            relative = knots - pair_rows(offsets[slot, pl.ds(j, 1), :])
            hits = [relative == order for order in range(4)]
            highs, lows = [], []
            for shift in range(4):
                piece = jnp.zeros((KB, LANES), jnp.float32)
                for order in range(4 - shift):
                    value = pair_rows(basis[slot, shift * 4 + order, pl.ds(j, 1), :])
                    piece = jnp.where(hits[order], value, piece)
                high, low = split(piece)
                highs.append(high)
                lows.append(low)
            weight_high, weight_low = split(weights[slot, pl.ds(j * 16, 16), :])
            left = jnp.concatenate([weight_high, weight_low], axis=0)
            right = jnp.concatenate([weight_high, jnp.zeros_like(weight_low)], axis=0)
            result = product(
                jnp.concatenate([left, right], axis=1),
                jnp.concatenate(highs, axis=0),
                jnp.concatenate(lows, axis=0),
            )
            band = jnp.concatenate(
                [result[0:8] + result[16:24], result[8:16] + result[24:32]], axis=1
            )
            block = pl.ds(pl.multiple_of(facts[HOME, cell, first + j] * 8, 8), 8)
            total[block, :] = total[block, :] + band

    over_groups(cells, groups, group)

    levels = lax.axis_size(axes).bit_length() - 1
    places = [band_place(owner, levels) for owner in range(1 << levels)]
    spread = total.shape[0] // 8 // len(places)
    for lower, upper in zip(places[:-1], places[1:]):
        start, stop = upper * spread * 8, (lower + 1) * spread * 8
        total[start : start + 8, :] = total[stop - 16 : stop - 8, :]
        total[stop - 8 : stop, :] = total[start + 8 : start + 16, :]
    mine = lax.axis_index(axes) & 1
    count = len(places) // 2
    chunk = kept_ref.shape[0] // count
    filler = jnp.zeros((chunk - spread * ROWS, LANES), jnp.float32)

    def pack(index, carry):
        target = pl.ds(pl.multiple_of(index * chunk, 8), chunk)
        for out_ref, part in ((kept_ref, mine), (sent_ref, 1 - mine)):
            source = pl.multiple_of((part * count + index) * spread * 8, 8)
            pieces = [total[pl.ds(source + j * 8, 8), :][0:ROWS] for j in range(spread)]
            out_ref[target, :] = jnp.concatenate(pieces + [filler], axis=0)
        return carry

    lax.fori_loop(0, count, pack, 0)


ENTRIES = tuple((row, column) for row in range(5) for column in range(row + 1))


def factor_kernel(facts_ref, star_ref, factors_ref, sums):
    transits, stars = star_ref.shape[1:]
    sums[...] = jnp.zeros_like(sums)

    for cell in range(stars // LANES):
        columns = pl.ds(cell * LANES, LANES)
        count = facts_ref[COUNT, cell : cell + 1, :]
        count = jnp.concatenate([count] * (LANES // transits), axis=1)
        count = jnp.broadcast_to(count, (8, LANES))

        def add(index, accumulated, columns=columns, count=count):
            first = pl.multiple_of(index * 8, 8)
            number = first + lax.broadcasted_iota(jnp.int32, (8, LANES), 0)
            live = jnp.where(number < count, 1.0, 0.0)
            parts = [star_ref[row, pl.ds(first, 8), columns] for row in range(5)]
            lively = [part * live for part in parts]
            return tuple(
                old + lively[row] * parts[column] for old, (row, column) in zip(accumulated, ENTRIES)
            )

        start = tuple(jnp.zeros((8, LANES), jnp.float32) for entry in ENTRIES)
        accumulated = lax.fori_loop(0, transits // 8, add, start, unroll=4)
        for entry in range(len(ENTRIES)):
            sums[entry, pl.ds(cell, 1), :] = jnp.sum(accumulated[entry], axis=0, keepdims=True)
    normal = [[None for column in range(5)] for row in range(5)]
    for entry, (row, column) in enumerate(ENTRIES):
        normal[row][column] = sums[entry] + (star_prior if row == column else 0.0)
    lower, inverse = cholesky_factor(normal, 5)
    for entry, (row, column) in enumerate(ENTRIES):
        factors_ref[entry] = inverse[row] if row == column else lower[row][column]


def star_kernel(
    facts,
    attitude_ref,
    factors_ref,
    phase_ref,
    offset_ref,
    axis_ref,
    star_ref,
    observed_ref,
    step_ref,
    second_ref,
    table,
    sums,
):
    transits, stars = phase_ref.shape
    cells = stars // LANES
    groups = transits // 8
    sums[...] = jnp.zeros_like(sums)
    sublane = lax.broadcasted_iota(jnp.int32, (8, LANES), 0)

    def predict_cell(cell, carry):
        columns = pl.ds(pl.multiple_of(cell * LANES, LANES), LANES)

        def predict(index, accumulated):
            first = pl.multiple_of(index * 8, 8)
            rows = pl.ds(first, 8)
            shift = jnp.zeros((8, LANES), jnp.int32)
            for j in range(8):
                owner = facts[OWNER, cell, first + j]
                slot = facts[SLOT, cell, first + j]
                column = pl.multiple_of((slot >> 3) * LANES, LANES)
                table[index, pl.ds(j, 4, stride=8), :] = attitude_ref[owner, :, pl.ds(column, LANES)]
                shift = jnp.where(sublane == j, (slot & 7) * KB, shift)
            number = first + lax.broadcasted_iota(jnp.int32, (8, LANES), 0)
            live = jnp.where(number < facts[COUNT, cell, 0], 1.0, 0.0)
            values = spline_basis(phase_ref[rows, columns])
            offset = offset_ref[rows, columns] + shift
            places = [offset + order for order in range(4)]
            predicted = jnp.zeros((8, LANES), jnp.float32)
            for m in range(4):
                spline = jnp.zeros((8, LANES), jnp.float32)
                looked = table[index, m * 8 : m * 8 + 8, :]
                for order in range(4):
                    found = jnp.take_along_axis(looked, places[order], axis=1)
                    spline = spline + found * values[order]
                predicted = predicted + spline * axis_ref[m, rows, columns]
            first_value = live * (observed_ref[rows, columns] - predicted)
            second_ref[rows, columns] = first_value
            parts = [star_ref[row, rows, columns] for row in range(5)]
            return tuple(old + part * first_value for old, part in zip(accumulated, parts))

        start = tuple(jnp.zeros((8, LANES), jnp.float32) for row in range(5))
        accumulated = lax.fori_loop(0, groups, predict, start, unroll=8)
        for entry in range(5):
            sums[entry, pl.ds(cell, 1), :] = jnp.sum(accumulated[entry], axis=0, keepdims=True)
        return carry

    lax.fori_loop(0, cells, predict_cell, 0)

    lower = [[None for column in range(5)] for row in range(5)]
    for entry, (row, column) in enumerate(ENTRIES):
        lower[row][column] = factors_ref[entry]
    inverse = [lower[row][row] for row in range(5)]
    answer = cholesky_solve(lower, inverse, [sums[row] for row in range(5)], 5)
    for row in range(5):
        sums[row] = answer[row]
        for cell in range(cells):
            step_ref[row : row + 1, cell * LANES : (cell + 1) * LANES] = answer[row][
                cell : cell + 1
            ]

    def correct(cell, carry):
        columns = pl.ds(pl.multiple_of(cell * LANES, LANES), LANES)
        own = [jnp.broadcast_to(sums[row, pl.ds(cell, 1), :], (8, LANES)) for row in range(5)]
        for index in range(groups):
            rows = pl.ds(index * 8, 8)
            number = index * 8 + sublane
            live = jnp.where(number < facts[COUNT, cell, 0], 1.0, 0.0)
            fitted = star_ref[0, rows, columns] * own[0]
            for row in range(1, 5):
                fitted = fitted + star_ref[row, rows, columns] * own[row]
            second_ref[rows, columns] = second_ref[rows, columns] - live * fitted
        return carry

    lax.fori_loop(0, cells, correct, 0)


def gradient_kernel(
    axes,
    facts_ref,
    phase_ref,
    offset_ref,
    axis_ref,
    second_ref,
    step_ref,
    kept_ref,
    sent_ref,
    step_hbm,
    total,
    weights,
    basis,
    offsets,
    facts,
    semaphores,
):
    scalars = pltpu.make_async_copy(facts_ref, facts, semaphores.at[0])
    scalars.start()
    result_copy = pltpu.make_async_copy(step_ref, step_hbm, semaphores.at[1])
    result_copy.start()
    transits, stars = phase_ref.shape
    cells = stars // LANES
    groups = transits // 8
    knots = lax.broadcasted_iota(jnp.int32, (KB, LANES), 0)
    lanes_block = lax.broadcasted_iota(jnp.int32, (8, LANES), 1) // KB
    total[...] = jnp.zeros_like(total)
    weights[...] = jnp.zeros_like(weights)
    scalars.wait()

    def group(cell, index, slot):
        first = pl.multiple_of(index * 8, 8)
        rows = pl.ds(first, 8)
        columns = pl.ds(pl.multiple_of(cell * LANES, LANES), LANES)
        second = second_ref[rows, columns]
        for m in range(4):
            value = axis_ref[m, rows, columns] * second
            high = value.astype(jnp.bfloat16).astype(jnp.float32)
            weights[slot, pl.ds(m, 8, stride=16), :] = high
            weights[slot, pl.ds(4 + m, 8, stride=16), :] = value - high
        values = spline_basis(phase_ref[rows, columns])
        for order in range(4):
            basis[slot, order] = values[order]
        offsets[slot] = offset_ref[rows, columns]
        for j in range(8):
            relative = knots - pair_rows(offsets[slot, pl.ds(j, 1), :])
            piece = jnp.zeros((KB, LANES), jnp.float32)
            for order in range(4):
                value = pair_rows(basis[slot, order, pl.ds(j, 1), :])
                piece = jnp.where(relative == order, value, piece)
            high, low = split(piece)
            weight = weights[slot, pl.ds(j * 16, 16), :]
            right = jnp.where(knots < 4, weight, 0.0)
            result = product(
                jnp.concatenate([weight, right], axis=1).astype(jnp.bfloat16),
                jnp.concatenate([high] * 4, axis=0),
                jnp.concatenate([low] * 4, axis=0),
            )[0:8]
            result = jnp.concatenate([result, result], axis=1)
            place = facts[HOME_LANES, cell, first + j]
            chosen = jnp.where(lanes_block == (place & 7), result, 0.0)
            block = pl.ds(pl.multiple_of((place >> 3) * 8, 8), 8)
            total[block, :] = total[block, :] + chosen

    over_groups(cells, groups, group)

    levels = lax.axis_size(axes).bit_length() - 1
    places = [reversed_place(owner, levels) for owner in range(1 << levels)]
    rows = total.shape[0] // len(places)
    for lower, upper in zip(places[:-1], places[1:]):
        start, stop = upper * rows, (lower + 1) * rows
        ending, opening = total[stop - 8 : stop, :], total[start : start + 8, :]
        total[start : start + 8, :] = opening + jnp.where(lanes_block == 0, ending, 0.0)
        total[stop - 8 : stop, :] = ending + jnp.where(lanes_block == 1, opening, 0.0)
    mine = lax.axis_index(axes) & 1
    count = len(places) // 2
    chunk = kept_ref.shape[0] // count
    filler = jnp.zeros((chunk - rows // 2, LANES), jnp.float32)

    def pack(index, carry):
        target = pl.ds(pl.multiple_of(index * chunk, 8), chunk)
        for out_ref, part in ((kept_ref, mine), (sent_ref, 1 - mine)):
            source = pl.multiple_of((part * count + index) * rows, 8)
            tiles = [total[pl.ds(source + j, 8), :] for j in range(0, rows, 8)]
            pieces = [tile[0:4] + tile[4:8] for tile in tiles]
            if filler.shape[0]:
                pieces.append(filler)
            out_ref[target, :] = jnp.concatenate(pieces, axis=0)
        return carry

    lax.fori_loop(0, count, pack, 0)
    result_copy.wait()


def share_of(axes, group):
    me = lax.axis_index(axes)
    mine = 0
    for bit in group:
        mine = mine * 2 + ((me >> bit) & 1)
    return mine


def add_rows(out_ref, base, inputs, start, rows):
    step = 64 if rows % 64 == 0 else rows

    def add(index, carry):
        first = pl.multiple_of(start + index * step, 8)
        terms = [ref[pl.ds(first + offset, step), :] for ref, offset in inputs]
        added = terms[0]
        for term in terms[1:]:
            added = added + term
        out_ref[pl.ds(pl.multiple_of(base + index * step, 8), step), :] = added
        return carry

    if step == rows:
        add(0, 0)
    else:
        lax.fori_loop(0, rows // step, add, 0)


def whole_tiles(rows):
    return (rows + 7) // 8 * 8


def order_of(members):
    return {2: ((1,), (1,)), 4: ((3, 2, 1), (1, 3, 2))}[members]


def add_kernel(axes, group, families, *refs):
    mine = share_of(axes, group)
    members = 1 << len(group)
    odd = lax.axis_index(axes) & 1
    others = [0] + [jnp.where(odd == 1, second, first) for first, second in zip(*order_of(members))]
    outputs = refs[-members:]
    first = 0
    base = 0
    for offsets, rows in families:
        segments = []
        for begins in offsets:
            segments.append(list(zip(refs[first : first + len(begins)], begins)))
            first += len(begins)
        within = members // len(segments)
        for other, out_ref in zip(others, outputs):
            which = mine ^ other
            for number, inputs in enumerate(segments):
                if len(segments) == 1:
                    add_rows(out_ref, base, inputs, which * rows, rows)
                else:

                    @pl.when(which // within == number)
                    def _(out_ref=out_ref, inputs=inputs, which=which, base=base, rows=rows):
                        add_rows(out_ref, base, inputs, (which % within) * rows, rows)

        base += rows


def cut_kernel(axes, cuts, count, *refs):
    me = lax.axis_index(axes)
    odd = me & 1
    outputs = refs[count:]
    for place, (inputs, base, rows, bit) in enumerate(cuts):
        mine = (me >> jnp.where(odd == 1, 3 - bit, bit)) & 1
        arrays = [(refs[index], 0) for index in inputs]
        add_rows(outputs[2 * place], 0, arrays, base + mine * rows, rows)
        add_rows(outputs[2 * place + 1], 0, arrays, base + (1 - mine) * rows, rows)


def meet_kernel(axes, size, rows, *refs):
    low, high, gradients = refs[0:2], refs[2:4], refs[4:6]
    own_low, own_high, own_rows, first, second, third = refs[6:]
    me = lax.axis_index(axes)
    odd = me & 1
    mine = share_of(axes, [1, 2])
    zip_low, zip_high, zip_rows = [[(ref, 0) for ref in pair] for pair in (low, high, gradients)]
    keep_low = (me >> (2 - odd)) & 1
    keep_high = (me >> (1 + odd)) & 1
    add_rows(first, 0, zip_rows, (mine ^ (1 + odd)) * rows, rows)
    add_rows(first, rows, zip_low, (1 - keep_low) * size, size)
    add_rows(second, 0, zip_rows, (mine ^ (2 - odd)) * rows, rows)
    add_rows(second, rows, zip_high, (1 - keep_high) * size, size)
    add_rows(third, 0, zip_rows, (mine ^ 3) * rows, rows)
    add_rows(own_low, 0, zip_low, keep_low * size, size)
    add_rows(own_high, 0, zip_high, keep_high * size, size)
    add_rows(own_rows, 0, zip_rows, mine * rows, rows)


def sweep_kernel(spread, axes, *refs):
    *parts, out_ref, band_ref, band = refs
    added = parts[0][...]
    for part in parts[1:]:
        added = added + part[...]
    band_ref[...] = added
    width = band.shape[2]
    tiles = width // LANES
    lane_block = lax.broadcasted_iota(jnp.int32, (8, LANES), 1) // KB
    filler = jnp.zeros((8 - ROWS, LANES), jnp.float32)
    for half in range(2):
        for shift in range(4):
            start = half * 64 + shift * KB
            for tile in range(tiles):
                merged = jnp.zeros((8, LANES), jnp.float32)
                for place in range(min(8, spread - tile * 8)):
                    block = tile * 8 + place
                    piece = jnp.concatenate(
                        [band_ref[block * ROWS : (block + 1) * ROWS, :], filler], axis=0
                    )
                    moved = (place * KB - start) % LANES
                    if moved:
                        piece = pltpu.roll(piece, moved, axis=1)
                    merged = jnp.where(lane_block == place, piece, merged)
                band[shift, half * 8 : half * 8 + 8, tile * LANES : (tile + 1) * LANES] = merged
    index = {}
    for place, (m, n) in enumerate(PAIRS):
        row = place if place < ROWS else place + 3
        index[(m, n)] = row
        index[(n, m)] = row

    def row_of(shift, m, n):
        return band[shift, index[(m, n)] : index[(m, n)] + 1, :]

    def square(entry):
        return jnp.concatenate([entry(m, n) for m in range(4) for n in range(4)], axis=0)

    diagonal = [
        [
            row_of(0, row, column) + (2.0 * smoothing + damping if row == column else 0.0)
            for column in range(4)
        ]
        for row in range(4)
    ]
    lower, inverse = cholesky_factor(diagonal, 4)
    one = jnp.ones((1, width), jnp.float32)
    zero = jnp.zeros((1, width), jnp.float32)
    columns = [
        cholesky_solve(lower, inverse, [one if row == column else zero for row in range(4)], 4)
        for column in range(4)
    ]
    solve = square(lambda m, n: columns[n][m])
    sublane = lax.broadcasted_iota(jnp.int32, (16, width), 0)
    same = (sublane >> 2) == (sublane & 3)
    operator = {0: square(lambda m, n: diagonal[m][n])}
    for shift in range(1, 4):
        ahead = square(lambda m, n: row_of(shift, m, n))
        operator[shift] = ahead
        operator[-shift] = pltpu.roll(ahead, shift, axis=1)
    for shift in (1, -1):
        operator[shift] = operator[shift] - jnp.where(same, smoothing, 0.0)
    own = jnp.concatenate(
        [
            band_ref[whole_tiles(spread * ROWS) + tile * 4 :, :][0:4]
            for tile in range(tiles)
        ],
        axis=1,
    )
    gradient = square(lambda m, n: own[m : m + 1])
    lane = lax.broadcasted_iota(jnp.int32, (8, width), 1)
    me = lax.axis_index(axes)
    start = jnp.where(me == 0, KB, 0)
    stop = jnp.where(me == lax.axis_size(axes) - 1, (spread - 1) * KB, spread * KB)
    keep = jnp.where((lane >= start) & (lane < stop), relaxation, 0.0)
    place = lax.broadcasted_iota(jnp.int32, (8, width), 0)
    odd = (place & 1) == 1
    late = (place & 2) == 2

    def over_columns(value):
        value = value + jnp.where(odd, pltpu.roll(value, 1, axis=0), pltpu.roll(value, 7, axis=0))
        return value + jnp.where(late, pltpu.roll(value, 2, axis=0), pltpu.roll(value, 6, axis=0))

    answer = jnp.zeros((8, width), jnp.float32)
    for sweep in range(ITERS):
        misfit = [gradient[0:8], gradient[8:16]]
        if sweep:
            moved = {0: answer}
            for shift in range(1, 4):
                moved[shift] = pltpu.roll(answer, width - shift, axis=1)
                moved[-shift] = pltpu.roll(answer, shift, axis=1)
            for half in range(2):
                rows = slice(half * 8, half * 8 + 8)
                terms = [operator[shift][rows] * moved[shift] for shift in range(-3, 4)]
                applied = ((terms[0] + terms[1]) + (terms[2] + terms[3])) + (
                    (terms[4] + terms[5]) + terms[6]
                )
                misfit[half] = misfit[half] - over_columns(applied)
        correction = solve[0:8] * misfit[0] + solve[8:16] * misfit[1]
        correction = correction + pltpu.roll(correction, 4, axis=0)
        answer = answer + keep * correction
    out_ref[...] = answer[0:4, KB : KB + out_ref.shape[1]]


def in_vmem(count):
    return [pl.BlockSpec(memory_space=pltpu.VMEM) for operand in range(count)]


def in_smem(count):
    return [pl.BlockSpec(memory_space=pltpu.SMEM) for operand in range(count)]


def work(microseconds):
    return pl.CostEstimate(flops=0, bytes_accessed=microseconds * 3_600_000, transcendentals=0)


def params(rows=0):
    return pltpu.CompilerParams(vmem_limit_bytes=min(56 << 20, (8 << 20) + 2 * rows * LANES * 4))


def call_facts(counts, attitude, owners, slots, devices):
    shape = (COUNT + 1,) + owners.shape
    return pl.pallas_call(
        functools.partial(facts_kernel, attitude.shape[1] // KB),
        out_shape=[
            jax.ShapeDtypeStruct(shape, jnp.int32),
            jax.ShapeDtypeStruct((devices,) + attitude.shape, jnp.float32),
        ],
        in_specs=in_smem(1) + in_vmem(3),
        out_specs=in_vmem(2),
        compiler_params=pltpu.CompilerParams(vmem_limit_bytes=62 << 20),
        cost_estimate=work(1),
        name="facts",
    )(counts, attitude, owners, slots)


def call_clear():
    return pl.pallas_call(
        clear_kernel,
        out_shape=jax.ShapeDtypeStruct((UNROLL, 9 * 16, LANES), jnp.float32),
        out_specs=in_vmem(1)[0],
        compiler_params=params(),
        cost_estimate=work(200),
        name="clear",
    )()


def call_normals(axes, facts, factors, phase, knot_offset, partials, clear, devices, spread):
    f32 = jnp.float32
    half = jax.ShapeDtypeStruct((devices // 2 * whole_tiles(spread * ROWS), LANES), f32)
    blocks = devices * spread
    return pl.pallas_call(
        functools.partial(normal_kernel, axes),
        out_shape=[half, half]
        + [jax.ShapeDtypeStruct(x.shape, x.dtype) for x in (facts, phase, knot_offset, partials)],
        in_specs=in_vmem(6),
        out_specs=in_vmem(6),
        scratch_shapes=[
            pltpu.VMEM((blocks * 8, LANES), f32),
            pltpu.VMEM((UNROLL, 9 * 16, LANES), f32),
            pltpu.VMEM((UNROLL, 16, 8, LANES), f32),
            pltpu.VMEM((UNROLL, 8, LANES), jnp.int32),
            pltpu.SMEM(facts.shape, jnp.int32),
            pltpu.SemaphoreType.DMA,
        ],
        compiler_params=params(blocks * 13),
        cost_estimate=work(100),
        name="normals",
    )(facts, factors, phase, knot_offset, partials, clear)


def call_add(axes, group, families):
    members = 1 << len(group)
    rows = sum(count for segments, count in families)
    out = jax.ShapeDtypeStruct((rows, LANES), jnp.float32)
    arrays = [pair[0] for segments, count in families for segment in segments for pair in segment]
    shapes = [
        ([[begin for array, begin in segment] for segment in segments], count)
        for segments, count in families
    ]
    return pl.pallas_call(
        functools.partial(add_kernel, axes, group, shapes),
        out_shape=[out] * members,
        in_specs=in_vmem(len(arrays)),
        out_specs=in_vmem(members),
        compiler_params=params(rows * members * 3),
        cost_estimate=work(0),
        name="shares",
    )(*arrays)


def call_cut(axes, arrays, cuts):
    outs = [
        jax.ShapeDtypeStruct((rows, LANES), jnp.float32) for inputs, base, rows, bit in cuts for half in range(2)
    ]
    return pl.pallas_call(
        functools.partial(cut_kernel, axes, cuts, len(arrays)),
        out_shape=outs,
        in_specs=in_vmem(len(arrays)),
        out_specs=in_vmem(len(outs)),
        compiler_params=params(sum(out.shape[0] for out in outs) * 3),
        cost_estimate=work(0),
        name="halves",
    )(*arrays)


def call_meet(axes, arrays, size, rows):
    counts = (size, size, rows, rows + size, rows + size, rows)
    return pl.pallas_call(
        functools.partial(meet_kernel, axes, size, rows),
        out_shape=[jax.ShapeDtypeStruct((count, LANES), jnp.float32) for count in counts],
        in_specs=in_vmem(len(arrays)),
        out_specs=in_vmem(len(counts)),
        compiler_params=params(sum(counts) * 3),
        cost_estimate=work(0),
        name="meet",
    )(*arrays)


def call_factors(facts, star_partials):
    return pl.pallas_call(
        factor_kernel,
        out_shape=jax.ShapeDtypeStruct((len(ENTRIES), 8, LANES), jnp.float32),
        in_specs=in_vmem(2),
        out_specs=in_vmem(1)[0],
        scratch_shapes=[pltpu.VMEM((len(ENTRIES), 8, LANES), jnp.float32)],
        compiler_params=params(),
        cost_estimate=work(200),
        name="factors",
    )(facts, star_partials)


def call_stars(facts, attitude, factors, phase, knot_offset, partials, star_partials, observed):
    f32 = jnp.float32
    transits, stars = phase.shape
    return pl.pallas_call(
        star_kernel,
        out_shape=[
            jax.ShapeDtypeStruct((5, stars), f32),
            jax.ShapeDtypeStruct((transits, stars), f32),
        ],
        in_specs=in_smem(1) + in_vmem(7),
        out_specs=in_vmem(2),
        scratch_shapes=[
            pltpu.VMEM((transits // 8, 40, LANES), f32),
            pltpu.VMEM((5, 8, LANES), f32),
        ],
        compiler_params=params(),
        cost_estimate=work(5),
        name="stars",
    )(facts, attitude, factors, phase, knot_offset, partials, star_partials, observed)


def call_gradients(axes, facts, phase, knot_offset, partials, second, step, devices, spread):
    f32 = jnp.float32
    tiles = (spread + 7) // 8
    half = jax.ShapeDtypeStruct((devices // 2 * whole_tiles(tiles * 4), LANES), f32)
    return pl.pallas_call(
        functools.partial(gradient_kernel, axes),
        out_shape=[half, half, jax.ShapeDtypeStruct(step.shape, f32)],
        in_specs=in_vmem(6),
        out_specs=in_vmem(2) + [pl.BlockSpec(memory_space=pltpu.HBM)],
        scratch_shapes=[
            pltpu.VMEM((devices * tiles * 8, LANES), f32),
            pltpu.VMEM((UNROLL, 9 * 16, LANES), f32),
            pltpu.VMEM((UNROLL, 4, 8, LANES), f32),
            pltpu.VMEM((UNROLL, 8, LANES), jnp.int32),
            pltpu.SMEM(facts.shape, jnp.int32),
            pltpu.SemaphoreType.DMA((2,)),
        ],
        compiler_params=params((devices + 1) * tiles * 12),
        cost_estimate=work(5),
        name="gradients",
    )(facts, phase, knot_offset, partials, second, step)


def swap(arrays, group, axes, devices):
    def mask(other):
        return sum(1 << bit for place, bit in enumerate(reversed(group)) if (other >> place) & 1)

    even, odd = order_of(len(arrays) + 1)
    arrived = []
    for array, first, second in zip(arrays, even, odd):
        pairs = [(i, i ^ mask(second if i & 1 else first)) for i in range(devices)]
        arrived.append(lax.ppermute(array, axes, pairs))
    return arrived


def hop(array, bit, axes, devices):
    pairs = [(i, i ^ (1 << (3 - bit if bit and i & 1 else bit))) for i in range(devices)]
    return lax.ppermute(array, axes, pairs)


def per_device(
    attitude,
    star_partials,
    attitude_partials,
    observed,
    phase,
    knot_offset,
    cell_counts,
    interval_owner,
    block_slot,
):
    axes = ("cells", "tm")
    devices = lax.axis_size("cells") * lax.axis_size("tm")
    levels = devices.bit_length() - 1
    cells = cell_counts.shape[0]
    transits = observed.shape[0]
    blocks = attitude.shape[1] // KB
    spread = blocks + 2
    tiles = (spread + 7) // 8
    width = tiles * LANES

    owners = interval_owner.reshape(cells, transits)
    facts, wide = call_facts(cell_counts, attitude, owners, block_slot, devices)
    whole = lax.all_to_all(wide, axes, split_axis=0, concat_axis=0, tiled=True)
    bits = list(range(devices.bit_length() - 1))
    later = [bits[start : start + 2] for start in range(3, len(bits), 2)]
    groups = [bits[:1], bits[1:3]] + later
    final = later[-1]
    chunks = (whole_tiles(spread * ROWS), whole_tiles(tiles * 4))

    def rows(kind, group):
        return chunks[kind] * (devices >> (group[-1] + 1))

    def advance(segments, kind, group):
        kept, *sent = call_add(axes, group, [(segments, rows(kind, group))])
        return [[(array, 0) for array in [kept] + swap(sent, group, axes, devices)]]

    def turn(array, bit):
        return hop(array, bit, axes, devices)

    clear = call_clear()
    clear, facts = lax.optimization_barrier((clear, facts))
    factors = call_factors(facts, star_partials)
    kept, sent, facts, phase, knot_offset, attitude_partials = call_normals(
        axes, facts, factors, phase, knot_offset, attitude_partials, clear, devices, spread
    )
    kept, sent, whole = lax.optimization_barrier((kept, sent, whole))
    arrived = turn(sent, 0)
    step, second = call_stars(
        facts, whole, factors, phase, knot_offset, attitude_partials, star_partials, observed
    )
    kept, arrived, second = lax.optimization_barrier((kept, arrived, second))
    size = kept.shape[0] // 4
    halves = call_cut(
        axes, [kept, arrived], [([0, 1], 0, size, 1), ([0, 1], 2 * size, size, 2)]
    )
    second, *halves = lax.optimization_barrier((second, *halves))
    low = [halves[0], turn(halves[1], 1)]
    high = [halves[2], turn(halves[3], 2)]
    kept, sent, star_step = call_gradients(
        axes, facts, phase, knot_offset, attitude_partials, second, step, devices, spread
    )
    gradients = [kept, turn(sent, 0)]
    both = lax.optimization_barrier((*low, *high, *gradients))
    count = rows(1, groups[1])
    own_low, own_high, own_rows, *sent = call_meet(axes, both, size // 2, count)
    first = turn(sent[0], 2)
    second = turn(sent[1], 1)
    third = lax.ppermute(sent[2], axes, [(i, i ^ 6) for i in range(devices)])
    normals = [[(own_low, 0), (first, count)], [(own_high, 0), (second, count)]]
    gradients = [[(own_rows, 0), (first, 0), (second, 0), (third, 0)]]
    for group in later[:-1]:
        gradients = advance(gradients, 1, group)
    for group in later[:-1]:
        normals = advance(normals, 0, group)
    families = [(normals, rows(0, final)), (gradients, rows(1, final))]
    kept, *sent = call_add(axes, final, families)
    parts = [kept] + swap(sent, final, axes, devices)
    attitude_step = pl.pallas_call(
        functools.partial(sweep_kernel, spread, axes),
        out_shape=jax.ShapeDtypeStruct((4, blocks * KB), jnp.float32),
        in_specs=in_vmem(len(parts)),
        out_specs=in_vmem(1)[0],
        scratch_shapes=[
            pltpu.VMEM(kept.shape, jnp.float32),
            pltpu.VMEM((4, 16, width), jnp.float32),
        ],
        compiler_params=params(),
        cost_estimate=work(2),
        name="sweeps",
    )(*parts)
    return (star_step, attitude_step)


def solution(mesh):
    split_axes = ("cells", "tm")
    placed = (
        P(None, split_axes),
        P(None, None, split_axes),
        P(None, None, split_axes),
        P(None, split_axes),
        P(None, split_axes),
        P(None, split_axes),
        P(split_axes),
        P(split_axes, None, None),
        P(split_axes, None),
    )
    return jax.shard_map(
        per_device,
        mesh=mesh,
        in_specs=placed,
        out_specs=(P(None, split_axes), P(None, split_axes)),
        check_vma=False,
    )
```

```python
import functools

import jax
import jax.numpy as jnp
from jax import lax
from jax.experimental import pallas as pl
from jax.experimental.pallas import tpu as pltpu
from jax.sharding import PartitionSpec as P

CS = 128
KB = 16
ITERS = 6
LANES = 128
PAIRS = tuple((m, n) for m in range(4) for n in range(m, 4))
HOME, HOME_LANES, OWNER, SLOT, COUNT = range(5)
ROWS = 5
UNROLL = 8

smoothing = 16.0
damping = 2.0
relaxation = 0.5
star_prior = 1.0


def spline_basis(phase):
    square = phase * phase
    cube = square * phase
    rest = 1.0 - phase
    return (
        rest * rest * rest * (1.0 / 6.0),
        (3.0 * cube - 6.0 * square + 4.0) * (1.0 / 6.0),
        (-3.0 * cube + 3.0 * square + 3.0 * phase + 1.0) * (1.0 / 6.0),
        cube * (1.0 / 6.0),
    )


def cholesky_factor(matrix, size):
    lower = [[None for column in range(size)] for row in range(size)]
    inverse = [None for column in range(size)]
    for column in range(size):
        total = matrix[column][column]
        for inner in range(column):
            total = total - lower[column][inner] * lower[column][inner]
        inverse[column] = 1.0 / jnp.sqrt(total)
        for row in range(column + 1, size):
            accum = matrix[row][column]
            for inner in range(column):
                accum = accum - lower[row][inner] * lower[column][inner]
            lower[row][column] = accum * inverse[column]
    return lower, inverse


def cholesky_solve(lower, inverse, rhs, size):
    forward = []
    for row in range(size):
        accum = rhs[row]
        for inner in range(row):
            accum = accum - lower[row][inner] * forward[inner]
        forward.append(accum * inverse[row])
    answer = [None for row in range(size)]
    for row in reversed(range(size)):
        accum = forward[row]
        for inner in range(row + 1, size):
            accum = accum - lower[inner][row] * answer[inner]
        answer[row] = accum * inverse[row]
    return answer


def split(value):
    high = value.astype(jnp.bfloat16)
    low = (value - high.astype(jnp.float32)).astype(jnp.bfloat16)
    return high, low


def over_groups(cells, groups, body):
    def cell_body(cell, carry):
        def some(index, inner):
            for slot in range(UNROLL):
                body(cell, index * UNROLL + slot, slot)
            return inner

        return lax.fori_loop(0, groups // UNROLL, some, carry)

    lax.fori_loop(0, cells, cell_body, 0)


def pair_rows(value):
    return jnp.broadcast_to(value, (KB, LANES))


def product(weights, matrix_high, matrix_low):
    return lax.dot_general(
        weights,
        jnp.concatenate([matrix_high, matrix_low], axis=1),
        (((1,), (1,)), ((), ())),
        preferred_element_type=jnp.float32,
    )


def reversed_place(owner, levels):
    place = owner * 0
    for bit in range(levels):
        place = place * 2 + ((owner >> bit) & 1)
    return place


def band_place(owner, levels):
    bits = [(owner >> bit) & 1 for bit in range(levels)]
    differ = bits[0] ^ bits[3]
    third = bits[1] ^ (differ * (bits[1] ^ bits[2]))
    place = owner * 0
    for bit in [bits[0], bits[3], third, bits[1] ^ bits[2] ^ third] + bits[4:]:
        place = place * 2 + bit
    return place


def facts_kernel(blocks, counts, attitude_ref, owners_ref, slots_ref, facts_ref, wide_ref):
    devices = wide_ref.shape[0]
    levels = devices.bit_length() - 1
    spread = blocks + 2
    lanes = (spread + 7) // 8 * 8
    owners = owners_ref[...]
    slots = slots_ref[...]
    cells = owners.shape[0]

    facts_ref[HOME] = band_place(owners, levels) * spread + slots + 1
    facts_ref[HOME_LANES] = reversed_place(owners, levels) * lanes + slots + 1
    facts_ref[OWNER] = owners
    facts_ref[SLOT] = slots
    for cell in range(cells):
        facts_ref[COUNT, cell : cell + 1, :] = jnp.full((1, owners.shape[1]), counts[cell], jnp.int32)
    attitude = attitude_ref[...]

    def copy(index, carry):
        wide_ref[index] = attitude
        return carry

    lax.fori_loop(0, devices, copy, 0, unroll=8)


def clear_kernel(out_ref):
    out_ref[...] = jnp.zeros_like(out_ref)


def normal_kernel(
    axes,
    facts_ref,
    factors_ref,
    phase_ref,
    offset_ref,
    axis_ref,
    clear_ref,
    kept_ref,
    sent_ref,
    facts_out,
    phase_out,
    offset_out,
    axis_out,
    total,
    weights,
    basis,
    offsets,
    facts,
    semaphore,
):
    scalars = pltpu.make_async_copy(facts_ref, facts, semaphore)
    scalars.start()
    facts_out[...] = facts_ref[...]
    phase_out[...] = phase_ref[...]
    offset_out[...] = offset_ref[...]
    axis_out[...] = axis_ref[...]
    transits, stars = phase_ref.shape
    cells = stars // LANES
    knots = lax.broadcasted_iota(jnp.int32, (KB, LANES), 0)
    total[...] = jnp.zeros_like(total)
    weights[...] = clear_ref[...]
    scalars.wait()
    groups = transits // 8

    def group(cell, index, slot):
        first = pl.multiple_of(index * 8, 8)
        rows = pl.ds(first, 8)
        columns = pl.ds(pl.multiple_of(cell * LANES, LANES), LANES)
        number = first + lax.broadcasted_iota(jnp.int32, (8, LANES), 0)
        live = jnp.where(number < facts[COUNT, cell, 0], 1.0, 0.0)
        values = spline_basis(phase_ref[rows, columns])
        for shift in range(4):
            for order in range(4 - shift):
                basis[slot, shift * 4 + order] = values[order] * values[order + shift]
        offsets[slot] = offset_ref[rows, columns]
        parts = [axis_ref[m, rows, columns] for m in range(4)]
        lively = [part * live for part in parts]
        for place, (m, n) in enumerate(PAIRS):
            row = place if place < ROWS else place + 3
            weights[slot, pl.ds(row, 8, stride=16), :] = lively[m] * parts[n]
        for j in range(8):
            relative = knots - pair_rows(offsets[slot, pl.ds(j, 1), :])
            hits = [relative == order for order in range(4)]
            highs, lows = [], []
            for shift in range(4):
                piece = jnp.zeros((KB, LANES), jnp.float32)
                for order in range(4 - shift):
                    value = pair_rows(basis[slot, shift * 4 + order, pl.ds(j, 1), :])
                    piece = jnp.where(hits[order], value, piece)
                high, low = split(piece)
                highs.append(high)
                lows.append(low)
            weight_high, weight_low = split(weights[slot, pl.ds(j * 16, 16), :])
            left = jnp.concatenate([weight_high, weight_low], axis=0)
            right = jnp.concatenate([weight_high, jnp.zeros_like(weight_low)], axis=0)
            result = product(
                jnp.concatenate([left, right], axis=1),
                jnp.concatenate(highs, axis=0),
                jnp.concatenate(lows, axis=0),
            )
            band = jnp.concatenate(
                [result[0:8] + result[16:24], result[8:16] + result[24:32]], axis=1
            )
            block = pl.ds(pl.multiple_of(facts[HOME, cell, first + j] * 8, 8), 8)
            total[block, :] = total[block, :] + band

    over_groups(cells, groups, group)

    levels = lax.axis_size(axes).bit_length() - 1
    places = [band_place(owner, levels) for owner in range(1 << levels)]
    spread = total.shape[0] // 8 // len(places)
    for lower, upper in zip(places[:-1], places[1:]):
        start, stop = upper * spread * 8, (lower + 1) * spread * 8
        total[start : start + 8, :] = total[stop - 16 : stop - 8, :]
        total[stop - 8 : stop, :] = total[start + 8 : start + 16, :]
    mine = lax.axis_index(axes) & 1
    count = len(places) // 2
    chunk = kept_ref.shape[0] // count
    filler = jnp.zeros((chunk - spread * ROWS, LANES), jnp.float32)

    def pack(index, carry):
        target = pl.ds(pl.multiple_of(index * chunk, 8), chunk)
        for out_ref, part in ((kept_ref, mine), (sent_ref, 1 - mine)):
            source = pl.multiple_of((part * count + index) * spread * 8, 8)
            pieces = [total[pl.ds(source + j * 8, 8), :][0:ROWS] for j in range(spread)]
            out_ref[target, :] = jnp.concatenate(pieces + [filler], axis=0)
        return carry

    lax.fori_loop(0, count, pack, 0)


ENTRIES = tuple((row, column) for row in range(5) for column in range(row + 1))


def factor_kernel(facts_ref, star_ref, factors_ref, sums):
    transits, stars = star_ref.shape[1:]
    sums[...] = jnp.zeros_like(sums)

    for cell in range(stars // LANES):
        columns = pl.ds(cell * LANES, LANES)
        count = facts_ref[COUNT, cell : cell + 1, :]
        count = jnp.concatenate([count] * (LANES // transits), axis=1)
        count = jnp.broadcast_to(count, (8, LANES))

        def add(index, accumulated, columns=columns, count=count):
            first = pl.multiple_of(index * 8, 8)
            number = first + lax.broadcasted_iota(jnp.int32, (8, LANES), 0)
            live = jnp.where(number < count, 1.0, 0.0)
            parts = [star_ref[row, pl.ds(first, 8), columns] for row in range(5)]
            lively = [part * live for part in parts]
            return tuple(
                old + lively[row] * parts[column] for old, (row, column) in zip(accumulated, ENTRIES)
            )

        start = tuple(jnp.zeros((8, LANES), jnp.float32) for entry in ENTRIES)
        accumulated = lax.fori_loop(0, transits // 8, add, start, unroll=4)
        for entry in range(len(ENTRIES)):
            sums[entry, pl.ds(cell, 1), :] = jnp.sum(accumulated[entry], axis=0, keepdims=True)
    normal = [[None for column in range(5)] for row in range(5)]
    for entry, (row, column) in enumerate(ENTRIES):
        normal[row][column] = sums[entry] + (star_prior if row == column else 0.0)
    lower, inverse = cholesky_factor(normal, 5)
    for entry, (row, column) in enumerate(ENTRIES):
        factors_ref[entry] = inverse[row] if row == column else lower[row][column]


def star_kernel(
    facts,
    attitude_ref,
    factors_ref,
    phase_ref,
    offset_ref,
    axis_ref,
    star_ref,
    observed_ref,
    step_ref,
    second_ref,
    table,
    sums,
):
    transits, stars = phase_ref.shape
    cells = stars // LANES
    groups = transits // 8
    sums[...] = jnp.zeros_like(sums)
    sublane = lax.broadcasted_iota(jnp.int32, (8, LANES), 0)

    def predict_cell(cell, carry):
        columns = pl.ds(pl.multiple_of(cell * LANES, LANES), LANES)

        def predict(index, accumulated):
            first = pl.multiple_of(index * 8, 8)
            rows = pl.ds(first, 8)
            shift = jnp.zeros((8, LANES), jnp.int32)
            for j in range(8):
                owner = facts[OWNER, cell, first + j]
                slot = facts[SLOT, cell, first + j]
                column = pl.multiple_of((slot >> 3) * LANES, LANES)
                table[index, pl.ds(j, 4, stride=8), :] = attitude_ref[owner, :, pl.ds(column, LANES)]
                shift = jnp.where(sublane == j, (slot & 7) * KB, shift)
            number = first + lax.broadcasted_iota(jnp.int32, (8, LANES), 0)
            live = jnp.where(number < facts[COUNT, cell, 0], 1.0, 0.0)
            values = spline_basis(phase_ref[rows, columns])
            offset = offset_ref[rows, columns] + shift
            places = [offset + order for order in range(4)]
            predicted = jnp.zeros((8, LANES), jnp.float32)
            for m in range(4):
                spline = jnp.zeros((8, LANES), jnp.float32)
                looked = table[index, m * 8 : m * 8 + 8, :]
                for order in range(4):
                    found = jnp.take_along_axis(looked, places[order], axis=1)
                    spline = spline + found * values[order]
                predicted = predicted + spline * axis_ref[m, rows, columns]
            first_value = live * (observed_ref[rows, columns] - predicted)
            second_ref[rows, columns] = first_value
            parts = [star_ref[row, rows, columns] for row in range(5)]
            return tuple(old + part * first_value for old, part in zip(accumulated, parts))

        start = tuple(jnp.zeros((8, LANES), jnp.float32) for row in range(5))
        accumulated = lax.fori_loop(0, groups, predict, start, unroll=8)
        for entry in range(5):
            sums[entry, pl.ds(cell, 1), :] = jnp.sum(accumulated[entry], axis=0, keepdims=True)
        return carry

    lax.fori_loop(0, cells, predict_cell, 0)

    lower = [[None for column in range(5)] for row in range(5)]
    for entry, (row, column) in enumerate(ENTRIES):
        lower[row][column] = factors_ref[entry]
    inverse = [lower[row][row] for row in range(5)]
    answer = cholesky_solve(lower, inverse, [sums[row] for row in range(5)], 5)
    for row in range(5):
        sums[row] = answer[row]
        for cell in range(cells):
            step_ref[row : row + 1, cell * LANES : (cell + 1) * LANES] = answer[row][
                cell : cell + 1
            ]

    def correct(cell, carry):
        columns = pl.ds(pl.multiple_of(cell * LANES, LANES), LANES)
        own = [jnp.broadcast_to(sums[row, pl.ds(cell, 1), :], (8, LANES)) for row in range(5)]
        for index in range(groups):
            rows = pl.ds(index * 8, 8)
            number = index * 8 + sublane
            live = jnp.where(number < facts[COUNT, cell, 0], 1.0, 0.0)
            fitted = star_ref[0, rows, columns] * own[0]
            for row in range(1, 5):
                fitted = fitted + star_ref[row, rows, columns] * own[row]
            second_ref[rows, columns] = second_ref[rows, columns] - live * fitted
        return carry

    lax.fori_loop(0, cells, correct, 0)


def gradient_kernel(
    axes,
    facts_ref,
    phase_ref,
    offset_ref,
    axis_ref,
    second_ref,
    step_ref,
    kept_ref,
    sent_ref,
    step_hbm,
    total,
    weights,
    basis,
    offsets,
    facts,
    semaphores,
):
    scalars = pltpu.make_async_copy(facts_ref, facts, semaphores.at[0])
    scalars.start()
    result_copy = pltpu.make_async_copy(step_ref, step_hbm, semaphores.at[1])
    result_copy.start()
    transits, stars = phase_ref.shape
    cells = stars // LANES
    groups = transits // 8
    knots = lax.broadcasted_iota(jnp.int32, (KB, LANES), 0)
    lanes_block = lax.broadcasted_iota(jnp.int32, (8, LANES), 1) // KB
    total[...] = jnp.zeros_like(total)
    weights[...] = jnp.zeros_like(weights)
    scalars.wait()

    def group(cell, index, slot):
        first = pl.multiple_of(index * 8, 8)
        rows = pl.ds(first, 8)
        columns = pl.ds(pl.multiple_of(cell * LANES, LANES), LANES)
        second = second_ref[rows, columns]
        for m in range(4):
            value = axis_ref[m, rows, columns] * second
            high = value.astype(jnp.bfloat16).astype(jnp.float32)
            weights[slot, pl.ds(m, 8, stride=16), :] = high
            weights[slot, pl.ds(4 + m, 8, stride=16), :] = value - high
        values = spline_basis(phase_ref[rows, columns])
        for order in range(4):
            basis[slot, order] = values[order]
        offsets[slot] = offset_ref[rows, columns]
        for j in range(8):
            relative = knots - pair_rows(offsets[slot, pl.ds(j, 1), :])
            piece = jnp.zeros((KB, LANES), jnp.float32)
            for order in range(4):
                value = pair_rows(basis[slot, order, pl.ds(j, 1), :])
                piece = jnp.where(relative == order, value, piece)
            high, low = split(piece)
            weight = weights[slot, pl.ds(j * 16, 16), :]
            right = jnp.where(knots < 4, weight, 0.0)
            result = product(
                jnp.concatenate([weight, right], axis=1).astype(jnp.bfloat16),
                jnp.concatenate([high] * 4, axis=0),
                jnp.concatenate([low] * 4, axis=0),
            )[0:8]
            result = jnp.concatenate([result, result], axis=1)
            place = facts[HOME_LANES, cell, first + j]
            chosen = jnp.where(lanes_block == (place & 7), result, 0.0)
            block = pl.ds(pl.multiple_of((place >> 3) * 8, 8), 8)
            total[block, :] = total[block, :] + chosen

    over_groups(cells, groups, group)

    levels = lax.axis_size(axes).bit_length() - 1
    places = [reversed_place(owner, levels) for owner in range(1 << levels)]
    rows = total.shape[0] // len(places)
    for lower, upper in zip(places[:-1], places[1:]):
        start, stop = upper * rows, (lower + 1) * rows
        ending, opening = total[stop - 8 : stop, :], total[start : start + 8, :]
        total[start : start + 8, :] = opening + jnp.where(lanes_block == 0, ending, 0.0)
        total[stop - 8 : stop, :] = ending + jnp.where(lanes_block == 1, opening, 0.0)
    mine = lax.axis_index(axes) & 1
    count = len(places) // 2
    chunk = kept_ref.shape[0] // count
    filler = jnp.zeros((chunk - rows // 2, LANES), jnp.float32)

    def pack(index, carry):
        target = pl.ds(pl.multiple_of(index * chunk, 8), chunk)
        for out_ref, part in ((kept_ref, mine), (sent_ref, 1 - mine)):
            source = pl.multiple_of((part * count + index) * rows, 8)
            tiles = [total[pl.ds(source + j, 8), :] for j in range(0, rows, 8)]
            pieces = [tile[0:4] + tile[4:8] for tile in tiles]
            if filler.shape[0]:
                pieces.append(filler)
            out_ref[target, :] = jnp.concatenate(pieces, axis=0)
        return carry

    lax.fori_loop(0, count, pack, 0)
    result_copy.wait()


def share_of(axes, group):
    me = lax.axis_index(axes)
    mine = 0
    for bit in group:
        mine = mine * 2 + ((me >> bit) & 1)
    return mine


def add_rows(out_ref, base, inputs, start, rows):
    step = 64 if rows % 64 == 0 else rows

    def add(index, carry):
        first = pl.multiple_of(start + index * step, 8)
        terms = [ref[pl.ds(first + offset, step), :] for ref, offset in inputs]
        added = terms[0]
        for term in terms[1:]:
            added = added + term
        out_ref[pl.ds(pl.multiple_of(base + index * step, 8), step), :] = added
        return carry

    if step == rows:
        add(0, 0)
    else:
        lax.fori_loop(0, rows // step, add, 0)


def whole_tiles(rows):
    return (rows + 7) // 8 * 8


def order_of(members):
    return {2: ((1,), (1,)), 4: ((3, 2, 1), (1, 3, 2))}[members]


def add_kernel(axes, group, families, *refs):
    mine = share_of(axes, group)
    members = 1 << len(group)
    odd = lax.axis_index(axes) & 1
    others = [0] + [jnp.where(odd == 1, second, first) for first, second in zip(*order_of(members))]
    outputs = refs[-members:]
    first = 0
    base = 0
    for offsets, rows in families:
        segments = []
        for begins in offsets:
            segments.append(list(zip(refs[first : first + len(begins)], begins)))
            first += len(begins)
        within = members // len(segments)
        for other, out_ref in zip(others, outputs):
            which = mine ^ other
            for number, inputs in enumerate(segments):
                if len(segments) == 1:
                    add_rows(out_ref, base, inputs, which * rows, rows)
                else:

                    @pl.when(which // within == number)
                    def _(out_ref=out_ref, inputs=inputs, which=which, base=base, rows=rows):
                        add_rows(out_ref, base, inputs, (which % within) * rows, rows)

        base += rows


def final_kernel(axes, group, families, *refs):
    mine = share_of(axes, group)
    members = 1 << len(group)
    odd = lax.axis_index(axes) & 1
    others = [0] + [jnp.where(odd == 1, second, first) for first, second in zip(*order_of(members))]
    outputs = refs[-members:]
    for other, out_ref in zip(others, outputs):
        which = mine ^ other
        pieces = []
        first = 0
        for offsets, rows, valid in families:
            within = members // len(offsets)
            parts = []
            for begins in offsets:
                inputs = list(zip(refs[first : first + len(begins)], begins))
                first += len(begins)
                start = pl.multiple_of((which % within) * rows, 8)
                terms = [ref[pl.ds(start + offset, rows), :] for ref, offset in inputs]
                parts.append(functools.reduce(jnp.add, terms))
            value = parts[0]
            for number, part in enumerate(parts[1:], start=1):
                value = jnp.where(which // within == number, part, value)
            pieces.append(value[0:valid])
        filler = out_ref.shape[0] - sum(piece.shape[0] for piece in pieces)
        if filler:
            pieces.append(jnp.zeros((filler, LANES), jnp.float32))
        out_ref[...] = jnp.concatenate(pieces, axis=0)


def cut_kernel(axes, cuts, count, *refs):
    me = lax.axis_index(axes)
    odd = me & 1
    outputs = refs[count:]
    for place, (inputs, base, rows, bit) in enumerate(cuts):
        mine = (me >> jnp.where(odd == 1, 3 - bit, bit)) & 1
        arrays = [(refs[index], 0) for index in inputs]
        add_rows(outputs[2 * place], 0, arrays, base + mine * rows, rows)
        add_rows(outputs[2 * place + 1], 0, arrays, base + (1 - mine) * rows, rows)


def meet_kernel(axes, size, rows, *refs):
    low, high, gradients = refs[0:2], refs[2:4], refs[4:6]
    own_low, own_high, own_rows, first, second, third = refs[6:]
    me = lax.axis_index(axes)
    odd = me & 1
    mine = share_of(axes, [1, 2])
    zip_low, zip_high, zip_rows = [[(ref, 0) for ref in pair] for pair in (low, high, gradients)]
    keep_low = (me >> (2 - odd)) & 1
    keep_high = (me >> (1 + odd)) & 1
    add_rows(first, 0, zip_rows, (mine ^ (1 + odd)) * rows, rows)
    add_rows(first, rows, zip_low, (1 - keep_low) * size, size)
    add_rows(second, 0, zip_rows, (mine ^ (2 - odd)) * rows, rows)
    add_rows(second, rows, zip_high, (1 - keep_high) * size, size)
    add_rows(third, 0, zip_rows, (mine ^ 3) * rows, rows)
    add_rows(own_low, 0, zip_low, keep_low * size, size)
    add_rows(own_high, 0, zip_high, keep_high * size, size)
    add_rows(own_rows, 0, zip_rows, mine * rows, rows)


def sweep_kernel(spread, axes, *refs):
    *parts, out_ref, band_ref, band = refs
    added = parts[0][...]
    for part in parts[1:]:
        added = added + part[...]
    band_ref[...] = added
    width = band.shape[2]
    tiles = width // LANES
    lane_block = lax.broadcasted_iota(jnp.int32, (8, LANES), 1) // KB
    filler = jnp.zeros((8 - ROWS, LANES), jnp.float32)
    for half in range(2):
        for shift in range(4):
            start = half * 64 + shift * KB
            for tile in range(tiles):
                merged = jnp.zeros((8, LANES), jnp.float32)
                for place in range(min(8, spread - tile * 8)):
                    block = tile * 8 + place
                    piece = jnp.concatenate(
                        [band_ref[block * ROWS : (block + 1) * ROWS, :], filler], axis=0
                    )
                    moved = (place * KB - start) % LANES
                    if moved:
                        piece = pltpu.roll(piece, moved, axis=1)
                    merged = jnp.where(lane_block == place, piece, merged)
                band[shift, half * 8 : half * 8 + 8, tile * LANES : (tile + 1) * LANES] = merged
    index = {}
    for place, (m, n) in enumerate(PAIRS):
        row = place if place < ROWS else place + 3
        index[(m, n)] = row
        index[(n, m)] = row

    def row_of(shift, m, n):
        return band[shift, index[(m, n)] : index[(m, n)] + 1, :]

    def square(entry):
        return jnp.concatenate([entry(m, n) for m in range(4) for n in range(4)], axis=0)

    diagonal = [
        [
            row_of(0, row, column) + (2.0 * smoothing + damping if row == column else 0.0)
            for column in range(4)
        ]
        for row in range(4)
    ]
    lower, inverse = cholesky_factor(diagonal, 4)
    one = jnp.ones((1, width), jnp.float32)
    zero = jnp.zeros((1, width), jnp.float32)
    columns = [
        cholesky_solve(lower, inverse, [one if row == column else zero for row in range(4)], 4)
        for column in range(4)
    ]
    solve = square(lambda m, n: columns[n][m])
    sublane = lax.broadcasted_iota(jnp.int32, (16, width), 0)
    same = (sublane >> 2) == (sublane & 3)
    operator = {0: square(lambda m, n: diagonal[m][n])}
    for shift in range(1, 4):
        ahead = square(lambda m, n: row_of(shift, m, n))
        operator[shift] = ahead
        operator[-shift] = pltpu.roll(ahead, shift, axis=1)
    for shift in (1, -1):
        operator[shift] = operator[shift] - jnp.where(same, smoothing, 0.0)
    own = jnp.concatenate(
        [
            band_ref[...][spread * ROWS + tile * 4 : spread * ROWS + (tile + 1) * 4]
            for tile in range(tiles)
        ],
        axis=1,
    )
    gradient = square(lambda m, n: own[m : m + 1])
    lane = lax.broadcasted_iota(jnp.int32, (8, width), 1)
    me = lax.axis_index(axes)
    start = jnp.where(me == 0, KB, 0)
    stop = jnp.where(me == lax.axis_size(axes) - 1, (spread - 1) * KB, spread * KB)
    keep = jnp.where((lane >= start) & (lane < stop), relaxation, 0.0)
    place = lax.broadcasted_iota(jnp.int32, (8, width), 0)
    odd = (place & 1) == 1
    late = (place & 2) == 2

    def over_columns(value):
        value = value + jnp.where(odd, pltpu.roll(value, 1, axis=0), pltpu.roll(value, 7, axis=0))
        return value + jnp.where(late, pltpu.roll(value, 2, axis=0), pltpu.roll(value, 6, axis=0))

    answer = jnp.zeros((8, width), jnp.float32)
    for sweep in range(ITERS):
        misfit = [gradient[0:8], gradient[8:16]]
        if sweep:
            moved = {0: answer}
            for shift in range(1, 4):
                moved[shift] = pltpu.roll(answer, width - shift, axis=1)
                moved[-shift] = pltpu.roll(answer, shift, axis=1)
            for half in range(2):
                rows = slice(half * 8, half * 8 + 8)
                terms = [operator[shift][rows] * moved[shift] for shift in range(-3, 4)]
                applied = ((terms[0] + terms[1]) + (terms[2] + terms[3])) + (
                    (terms[4] + terms[5]) + terms[6]
                )
                misfit[half] = misfit[half] - over_columns(applied)
        correction = solve[0:8] * misfit[0] + solve[8:16] * misfit[1]
        correction = correction + pltpu.roll(correction, 4, axis=0)
        answer = answer + keep * correction
    out_ref[...] = answer[0:4, KB : KB + out_ref.shape[1]]


def in_vmem(count):
    return [pl.BlockSpec(memory_space=pltpu.VMEM) for operand in range(count)]


def in_smem(count):
    return [pl.BlockSpec(memory_space=pltpu.SMEM) for operand in range(count)]


def work(microseconds):
    return pl.CostEstimate(flops=0, bytes_accessed=microseconds * 3_600_000, transcendentals=0)


def params(rows=0):
    return pltpu.CompilerParams(vmem_limit_bytes=min(56 << 20, (8 << 20) + 2 * rows * LANES * 4))


def call_facts(counts, attitude, owners, slots, devices):
    shape = (COUNT + 1,) + owners.shape
    return pl.pallas_call(
        functools.partial(facts_kernel, attitude.shape[1] // KB),
        out_shape=[
            jax.ShapeDtypeStruct(shape, jnp.int32),
            jax.ShapeDtypeStruct((devices,) + attitude.shape, jnp.float32),
        ],
        in_specs=in_smem(1) + in_vmem(3),
        out_specs=in_vmem(2),
        compiler_params=pltpu.CompilerParams(vmem_limit_bytes=62 << 20),
        cost_estimate=work(1),
        name="facts",
    )(counts, attitude, owners, slots)


def call_clear():
    return pl.pallas_call(
        clear_kernel,
        out_shape=jax.ShapeDtypeStruct((UNROLL, 9 * 16, LANES), jnp.float32),
        out_specs=in_vmem(1)[0],
        compiler_params=params(),
        cost_estimate=work(200),
        name="clear",
    )()


def call_normals(axes, facts, factors, phase, knot_offset, partials, clear, devices, spread):
    f32 = jnp.float32
    half = jax.ShapeDtypeStruct((devices // 2 * whole_tiles(spread * ROWS), LANES), f32)
    blocks = devices * spread
    return pl.pallas_call(
        functools.partial(normal_kernel, axes),
        out_shape=[half, half]
        + [jax.ShapeDtypeStruct(x.shape, x.dtype) for x in (facts, phase, knot_offset, partials)],
        in_specs=in_vmem(6),
        out_specs=in_vmem(6),
        scratch_shapes=[
            pltpu.VMEM((blocks * 8, LANES), f32),
            pltpu.VMEM((UNROLL, 9 * 16, LANES), f32),
            pltpu.VMEM((UNROLL, 16, 8, LANES), f32),
            pltpu.VMEM((UNROLL, 8, LANES), jnp.int32),
            pltpu.SMEM(facts.shape, jnp.int32),
            pltpu.SemaphoreType.DMA,
        ],
        compiler_params=params(blocks * 13),
        cost_estimate=work(100),
        name="normals",
    )(facts, factors, phase, knot_offset, partials, clear)


def call_add(axes, group, families, valid=None):
    members = 1 << len(group)
    rows = sum(count for segments, count in families)
    if valid:
        rows = whole_tiles(sum(valid))
    out = jax.ShapeDtypeStruct((rows, LANES), jnp.float32)
    arrays = [pair[0] for segments, count in families for segment in segments for pair in segment]
    shapes = [
        ([[begin for array, begin in segment] for segment in segments], count)
        for segments, count in families
    ]
    kernel = add_kernel
    if valid:
        kernel = final_kernel
        shapes = [(offsets, count, kept) for (offsets, count), kept in zip(shapes, valid)]
    return pl.pallas_call(
        functools.partial(kernel, axes, group, shapes),
        out_shape=[out] * members,
        in_specs=in_vmem(len(arrays)),
        out_specs=in_vmem(members),
        compiler_params=params(rows * members * 3),
        cost_estimate=work(0),
        name="shares",
    )(*arrays)


def call_cut(axes, arrays, cuts):
    outs = [
        jax.ShapeDtypeStruct((rows, LANES), jnp.float32) for inputs, base, rows, bit in cuts for half in range(2)
    ]
    return pl.pallas_call(
        functools.partial(cut_kernel, axes, cuts, len(arrays)),
        out_shape=outs,
        in_specs=in_vmem(len(arrays)),
        out_specs=in_vmem(len(outs)),
        compiler_params=params(sum(out.shape[0] for out in outs) * 3),
        cost_estimate=work(0),
        name="halves",
    )(*arrays)


def call_meet(axes, arrays, size, rows):
    counts = (size, size, rows, rows + size, rows + size, rows)
    return pl.pallas_call(
        functools.partial(meet_kernel, axes, size, rows),
        out_shape=[jax.ShapeDtypeStruct((count, LANES), jnp.float32) for count in counts],
        in_specs=in_vmem(len(arrays)),
        out_specs=in_vmem(len(counts)),
        compiler_params=params(sum(counts) * 3),
        cost_estimate=work(0),
        name="meet",
    )(*arrays)


def call_factors(facts, star_partials):
    return pl.pallas_call(
        factor_kernel,
        out_shape=jax.ShapeDtypeStruct((len(ENTRIES), 8, LANES), jnp.float32),
        in_specs=in_vmem(2),
        out_specs=in_vmem(1)[0],
        scratch_shapes=[pltpu.VMEM((len(ENTRIES), 8, LANES), jnp.float32)],
        compiler_params=params(),
        cost_estimate=work(200),
        name="factors",
    )(facts, star_partials)


def call_stars(facts, attitude, factors, phase, knot_offset, partials, star_partials, observed):
    f32 = jnp.float32
    transits, stars = phase.shape
    return pl.pallas_call(
        star_kernel,
        out_shape=[
            jax.ShapeDtypeStruct((5, stars), f32),
            jax.ShapeDtypeStruct((transits, stars), f32),
        ],
        in_specs=in_smem(1) + in_vmem(7),
        out_specs=in_vmem(2),
        scratch_shapes=[
            pltpu.VMEM((transits // 8, 40, LANES), f32),
            pltpu.VMEM((5, 8, LANES), f32),
        ],
        compiler_params=params(),
        cost_estimate=work(5),
        name="stars",
    )(facts, attitude, factors, phase, knot_offset, partials, star_partials, observed)


def call_gradients(axes, facts, phase, knot_offset, partials, second, step, devices, spread):
    f32 = jnp.float32
    tiles = (spread + 7) // 8
    half = jax.ShapeDtypeStruct((devices // 2 * whole_tiles(tiles * 4), LANES), f32)
    return pl.pallas_call(
        functools.partial(gradient_kernel, axes),
        out_shape=[half, half, jax.ShapeDtypeStruct(step.shape, f32)],
        in_specs=in_vmem(6),
        out_specs=in_vmem(2) + [pl.BlockSpec(memory_space=pltpu.HBM)],
        scratch_shapes=[
            pltpu.VMEM((devices * tiles * 8, LANES), f32),
            pltpu.VMEM((UNROLL, 9 * 16, LANES), f32),
            pltpu.VMEM((UNROLL, 4, 8, LANES), f32),
            pltpu.VMEM((UNROLL, 8, LANES), jnp.int32),
            pltpu.SMEM(facts.shape, jnp.int32),
            pltpu.SemaphoreType.DMA((2,)),
        ],
        compiler_params=params((devices + 1) * tiles * 12),
        cost_estimate=work(5),
        name="gradients",
    )(facts, phase, knot_offset, partials, second, step)


def swap(arrays, group, axes, devices):
    def mask(other):
        return sum(1 << bit for place, bit in enumerate(reversed(group)) if (other >> place) & 1)

    even, odd = order_of(len(arrays) + 1)
    arrived = []
    for array, first, second in zip(arrays, even, odd):
        pairs = [(i, i ^ mask(second if i & 1 else first)) for i in range(devices)]
        arrived.append(lax.ppermute(array, axes, pairs))
    return arrived


def hop(array, bit, axes, devices):
    pairs = [(i, i ^ (1 << (3 - bit if bit and i & 1 else bit))) for i in range(devices)]
    return lax.ppermute(array, axes, pairs)


def per_device(
    attitude,
    star_partials,
    attitude_partials,
    observed,
    phase,
    knot_offset,
    cell_counts,
    interval_owner,
    block_slot,
):
    axes = ("cells", "tm")
    devices = lax.axis_size("cells") * lax.axis_size("tm")
    levels = devices.bit_length() - 1
    cells = cell_counts.shape[0]
    transits = observed.shape[0]
    blocks = attitude.shape[1] // KB
    spread = blocks + 2
    tiles = (spread + 7) // 8
    width = tiles * LANES

    owners = interval_owner.reshape(cells, transits)
    facts, wide = call_facts(cell_counts, attitude, owners, block_slot, devices)
    whole = lax.all_to_all(wide, axes, split_axis=0, concat_axis=0, tiled=True)
    bits = list(range(devices.bit_length() - 1))
    later = [bits[start : start + 2] for start in range(3, len(bits), 2)]
    groups = [bits[:1], bits[1:3]] + later
    final = later[-1]
    chunks = (whole_tiles(spread * ROWS), whole_tiles(tiles * 4))

    def rows(kind, group):
        return chunks[kind] * (devices >> (group[-1] + 1))

    def advance(segments, kind, group):
        kept, *sent = call_add(axes, group, [(segments, rows(kind, group))])
        return [[(array, 0) for array in [kept] + swap(sent, group, axes, devices)]]

    def turn(array, bit):
        return hop(array, bit, axes, devices)

    clear = call_clear()
    clear, facts = lax.optimization_barrier((clear, facts))
    factors = call_factors(facts, star_partials)
    kept, sent, facts, phase, knot_offset, attitude_partials = call_normals(
        axes, facts, factors, phase, knot_offset, attitude_partials, clear, devices, spread
    )
    kept, sent, whole = lax.optimization_barrier((kept, sent, whole))
    arrived = turn(sent, 0)
    step, second = call_stars(
        facts, whole, factors, phase, knot_offset, attitude_partials, star_partials, observed
    )
    kept, arrived, second = lax.optimization_barrier((kept, arrived, second))
    size = kept.shape[0] // 4
    halves = call_cut(
        axes, [kept, arrived], [([0, 1], 0, size, 1), ([0, 1], 2 * size, size, 2)]
    )
    second, *halves = lax.optimization_barrier((second, *halves))
    low = [halves[0], turn(halves[1], 1)]
    high = [halves[2], turn(halves[3], 2)]
    kept, sent, star_step = call_gradients(
        axes, facts, phase, knot_offset, attitude_partials, second, step, devices, spread
    )
    gradients = [kept, turn(sent, 0)]
    both = lax.optimization_barrier((*low, *high, *gradients))
    count = rows(1, groups[1])
    own_low, own_high, own_rows, *sent = call_meet(axes, both, size // 2, count)
    first = turn(sent[0], 2)
    second = turn(sent[1], 1)
    third = lax.ppermute(sent[2], axes, [(i, i ^ 6) for i in range(devices)])
    normals = [[(own_low, 0), (first, count)], [(own_high, 0), (second, count)]]
    gradients = [[(own_rows, 0), (first, 0), (second, 0), (third, 0)]]
    for group in later[:-1]:
        gradients = advance(gradients, 1, group)
    for group in later[:-1]:
        normals = advance(normals, 0, group)
    families = [(normals, rows(0, final)), (gradients, rows(1, final))]
    kept, *sent = call_add(axes, final, families, (spread * ROWS, tiles * 4))
    parts = [kept] + swap(sent, final, axes, devices)
    attitude_step = pl.pallas_call(
        functools.partial(sweep_kernel, spread, axes),
        out_shape=jax.ShapeDtypeStruct((4, blocks * KB), jnp.float32),
        in_specs=in_vmem(len(parts)),
        out_specs=in_vmem(1)[0],
        scratch_shapes=[
            pltpu.VMEM(kept.shape, jnp.float32),
            pltpu.VMEM((4, 16, width), jnp.float32),
        ],
        compiler_params=params(),
        cost_estimate=work(2),
        name="sweeps",
    )(*parts)
    return (star_step, attitude_step)


def solution(mesh):
    split_axes = ("cells", "tm")
    placed = (
        P(None, split_axes),
        P(None, None, split_axes),
        P(None, None, split_axes),
        P(None, split_axes),
        P(None, split_axes),
        P(None, split_axes),
        P(split_axes),
        P(split_axes, None, None),
        P(split_axes, None),
    )
    return jax.shard_map(
        per_device,
        mesh=mesh,
        in_specs=placed,
        out_specs=(P(None, split_axes), P(None, split_axes)),
        check_vma=False,
    )
```
